256 devices in a mesh: cell: 64 (over z, y, core), cuts: 4 (over x).
Axes of the slice: x: 4, y: 4, z: 8, core: 2. Of those that a mesh axis runs over, the one named last changes fastest.
Arguments:
- node_positions: float32 [3, 262144], P(None, 'cell'), may hold values from -7 to 13
- connectivity: int32 [2, 262144], P(None, 'cell'), may hold values from 0 to 4095, as said below
- burgers_index: int32 [2048], P('cell'), may hold values from 0 to 5
- applied_stress: float32 [3, 3], replicated, may hold values from -4 to 4
- ghost_request: int32 [64, 64, 4], P('cell'), may hold values from -1 to 31, as said below
- pair_list: int32 [2, 65536], P(None, ('cell', 'cuts')), may hold values from -1 to 287, as said below
Outputs:
- velocity: float32 [3, 262144], P(None, 'cell')
The draws below stay inside these ranges and needn't reach their ends.
Inputs may be any that keep to these rules, and one draw needn't show every extreme that they name: `connectivity`: column s holds the two end nodes of segment s, numbered among the 4096 nodes of the same index of cell; each block of 128 segments is one closed loop, and every node is an end of exactly two segments. `ghost_request`: entry [c, o, t] names a block of index o of cell, numbered among its 32 blocks, that index c of cell uses, or -1 for an unused slot; in each row the used slots come first, and at least one slot of each row is used. `pair_list`: each device's 256 columns are its pair rows. A used row holds a block number below 32 of the device's cell index, then either such a block number or 32 + o * 4 + t for a used slot t of owner o in ghost_request. Empty rows hold -1 twice and come after all used rows; on each index of cell one device along cuts uses all its rows.
All inputs are finite; a program needn't handle non-finite values.
Results may differ from the reference program's by a relative error of at most 0.00027.
Values sent between devices are 32-bit elements; how exact they have to be, the bound alone decides.
A program may use at most 64 MiB of HBM per device.

```python
import math
import jax
import jax.numpy as jnp
from jax import lax

SEG = 128
CAP = 4
BLK_DEV = 32
PAIR_DEV = 256
NODE_DEV = 4096
NODES = 262144
BLOCKS = 2048
PAIRS = 65536
N_CELL = 64
N_CUTS = 4


def loop_order(key):
    order_key = jax.random.fold_in(key, 11)
    cell_keys = jax.random.split(order_key, N_CELL)
    return jax.vmap(lambda one_key: jax.random.permutation(one_key, NODE_DEV))(cell_keys).astype(jnp.int32)


def ghost_layout(key):
    layout_key = jax.random.fold_in(key, 21)
    layout_keys = jax.random.split(layout_key, 3)
    owner_grid = jnp.arange(N_CELL, dtype=jnp.int32)[None, :]
    asker_grid = jnp.arange(N_CELL, dtype=jnp.int32)[:, None]
    used_slots = jax.random.randint(layout_keys[0], (N_CELL, N_CELL), 1, CAP + 1)
    filled = (owner_grid == (asker_grid + 1) % N_CELL) | (owner_grid == N_CELL - 1)
    sparse_one = (asker_grid == 0) & (owner_grid == 0)
    used_slots = jnp.where(sparse_one, 1, used_slots)
    used_slots = jnp.where(filled, CAP, used_slots)
    base_block = jax.random.randint(layout_keys[1], (N_CELL, N_CELL), 0, BLK_DEV)
    top_one = (asker_grid == 0) & (owner_grid == 1)
    base_block = jnp.where(top_one, BLK_DEV - 1, base_block)
    stride = 2 * jax.random.randint(layout_keys[2], (N_CELL, N_CELL), 0, BLK_DEV // 2) + 1
    slot_ids = jnp.arange(CAP, dtype=jnp.int32)
    request = jnp.where(slot_ids[None, None, :] < used_slots[:, :, None], (base_block[:, :, None] + slot_ids[None, None, :] * stride[:, :, None]) % BLK_DEV, -1)
    return (used_slots.astype(jnp.int32), request.astype(jnp.int32))


def draw_connectivity(key, part):
    order = loop_order(key)
    ahead = jnp.roll(order.reshape(N_CELL, BLK_DEV, SEG), -1, axis=2).reshape(N_CELL, NODE_DEV)
    return jnp.stack([order.reshape(NODES), ahead.reshape(NODES)], axis=0).astype(jnp.int32)


def draw_node_positions(key, part):
    order = loop_order(key)
    key = jax.random.fold_in(key, 2)
    draw_keys = jax.random.split(key, 5)
    loops = N_CELL * BLK_DEV
    centers = jax.random.uniform(draw_keys[0], (3, loops), jnp.float32, 0.0, 8.0)
    radius = jax.random.uniform(draw_keys[1], (loops,), jnp.float32, 2.5, 4.5)
    azimuth = jax.random.uniform(draw_keys[2], (loops,), jnp.float32, -math.pi, math.pi)
    tilt = jax.random.uniform(draw_keys[3], (loops,), jnp.float32, -0.5 * math.pi, 0.5 * math.pi)
    theta = 2.0 * math.pi * jnp.arange(SEG, dtype=jnp.float32) / SEG
    first_axis = jnp.stack([jnp.cos(azimuth), jnp.sin(azimuth), jnp.zeros_like(azimuth)], axis=0)
    second_axis = jnp.stack([-jnp.sin(azimuth) * jnp.cos(tilt), jnp.cos(azimuth) * jnp.cos(tilt), jnp.sin(tilt)], axis=0)
    rough = jax.random.uniform(draw_keys[4], (3, loops, SEG), jnp.float32, -0.08, 0.08)
    points = centers[:, :, None] + radius[None, :, None] * (first_axis[:, :, None] * jnp.cos(theta)[None, None, :] + second_axis[:, :, None] * jnp.sin(theta)[None, None, :]) + rough
    points = points.reshape(3, N_CELL, NODE_DEV)
    cell_rows = jnp.arange(N_CELL, dtype=jnp.int32)[:, None]
    placed = jnp.zeros((3, N_CELL, NODE_DEV), jnp.float32).at[:, cell_rows, order].set(points)
    return placed.reshape(3, NODES)


def draw_ghost_request(key, part):
    used_slots, request = ghost_layout(key)
    return request


def draw_pair_list(key, part):
    used_slots, request = ghost_layout(key)
    key = jax.random.fold_in(key, 4)
    draw_keys = jax.random.split(key, 6)
    devices = N_CELL * N_CUTS
    cell_of = jnp.arange(devices, dtype=jnp.int32) // N_CUTS
    cut_of = jnp.arange(devices, dtype=jnp.int32) % N_CUTS
    filled = jax.random.randint(draw_keys[0], (devices,), PAIR_DEV // 8, PAIR_DEV // 2 + 1)
    filled = jnp.where(cut_of == cell_of % N_CUTS, PAIR_DEV, filled)
    first_idx = jax.random.randint(draw_keys[1], (devices, PAIR_DEV), 0, BLK_DEV)
    local_second = jax.random.randint(draw_keys[2], (devices, PAIR_DEV), 0, BLK_DEV)
    owner = jax.random.randint(draw_keys[3], (devices, PAIR_DEV), 0, N_CELL)
    room = used_slots[cell_of[:, None], owner]
    slot_pick = jax.random.randint(draw_keys[4], (devices, PAIR_DEV), 0, room)
    ghost_second = BLK_DEV + owner * CAP + slot_pick
    is_local = jax.random.randint(draw_keys[5], (devices, PAIR_DEV), 0, 4) == 0
    second_idx = jnp.where(is_local, local_second, ghost_second)
    row_ids = jnp.arange(PAIR_DEV, dtype=jnp.int32)[None, :]
    second_idx = jnp.where(row_ids == 0, BLK_DEV + N_CELL * CAP - 1, second_idx)
    alive = row_ids < filled[:, None]
    first_idx = jnp.where(alive, first_idx, -1)
    second_idx = jnp.where(alive, second_idx, -1)
    return jnp.stack([first_idx.reshape(-1), second_idx.reshape(-1)], axis=0).astype(jnp.int32)


def plant(drawn, rng, smallest, high):
    shape = drawn.shape
    place = [jax.random.randint(jax.random.fold_in(rng, axis), (), 0, shape[axis]) for axis in range(len(shape))]
    drawn = drawn.at[tuple(place)].set(smallest)
    longest = shape.index(max(shape))
    place[longest] = (place[longest] + 1) % shape[longest]
    return drawn.at[tuple(place)].set(high)


def normal_values(stream_key, dims, scale, bound, kind=jnp.bfloat16):
    return jnp.clip(scale * jax.random.normal(stream_key, dims, jnp.float32), -bound, bound).astype(kind)


def setup_inputs(seed: int = 0) -> dict:
    splits = jax.random.split(jax.random.key(seed), 7)
    return {
        "node_positions": draw_node_positions(jax.random.fold_in(splits[6], 71), 0),
        "connectivity": draw_connectivity(jax.random.fold_in(splits[6], 71), 0),
        "burgers_index": plant(jax.random.randint(splits[2], (BLOCKS,), 0, 6), jax.random.fold_in(splits[2], 1), 0, 5).astype(jnp.int32),
        "applied_stress": normal_values(splits[3], (3, 3), 1.0, 4.0, jnp.float32),
        "ghost_request": draw_ghost_request(jax.random.fold_in(splits[6], 71), 0),
        "pair_list": draw_pair_list(jax.random.fold_in(splits[6], 71), 0),
    }


MU_FACTOR = 10.0
CORE_SQUARED = 0.25
DRAG_FACTOR = 1.0
ref_group = 64

def burgers_table():
    scale_half = 0.5 ** 0.5
    return jnp.array([[1.0, 1.0, 1.0, 1.0, 0.0, 0.0], [1.0, -1.0, 0.0, 0.0, 1.0, 1.0], [0.0, 0.0, 1.0, -1.0, 1.0, -1.0]], jnp.float32) * scale_half

def block_data(positions, end_links, burgers, seg_count):
    block_count = burgers.shape[0]
    start = jnp.take(positions, end_links[0], axis=1)
    finish = jnp.take(positions, end_links[1], axis=1)
    middle = 0.5 * (start + finish)
    line_vectors = finish - start
    choose = (burgers[None, :] == jnp.arange(6, dtype=jnp.int32)[:, None]).astype(jnp.float32)
    vectors = jnp.dot(burgers_table(), choose, precision=lax.Precision.HIGHEST)
    line_blocks = line_vectors.reshape(3, block_count, seg_count)
    coupling = vectors[:, None, :, None] * line_blocks[None, :, :, :]
    coupling = coupling.reshape(9, block_count, seg_count)
    packed = jnp.concatenate([middle.reshape(3, block_count, seg_count), coupling], axis=0)
    return (jnp.transpose(packed, (1, 0, 2)), vectors, line_vectors)

def pair_forces(near_data, far_data, pair_scale):
    separation = near_data[:, :3, :, None] - far_data[:, :3, None, :]
    dist_sq = lax.optimization_barrier(jnp.sum(separation * separation, axis=1)) + CORE_SQUARED
    coupling = jnp.einsum('gci,gcj->gij', near_data[:, 3:], far_data[:, 3:], precision=lax.Precision.HIGHEST)
    weight = MU_FACTOR * pair_scale[:, None, None] * coupling / (dist_sq * jnp.sqrt(dist_sq))
    on_first = lax.optimization_barrier(jnp.sum(weight[:, None] * separation, axis=3))
    on_second = -lax.optimization_barrier(jnp.sum(weight[:, None] * separation, axis=2))
    return (on_first, on_second)

def nodal_velocity(seg_force, line_vectors, end_links):
    node_total = end_links.shape[1]
    zero_field = jnp.zeros((3, node_total), jnp.float32)
    node_force = 0.5 * (zero_field.at[:, end_links[0]].add(seg_force) + zero_field.at[:, end_links[1]].add(seg_force))
    length = jnp.sqrt(lax.optimization_barrier(jnp.sum(line_vectors * line_vectors, axis=0)) + CORE_SQUARED)
    flat_zero = jnp.zeros((node_total,), jnp.float32)
    drag_sum = DRAG_FACTOR * 0.5 * (flat_zero.at[end_links[0]].add(length) + flat_zero.at[end_links[1]].add(length))
    return node_force / drag_sum[None, :]

def reference(node_positions, connectivity, burgers_index, applied_stress, ghost_request, pair_list):
    offset = jnp.arange(NODES, dtype=jnp.int32) // NODE_DEV * NODE_DEV
    end_links = connectivity + offset[None, :]
    blocks, vectors, line_vectors = block_data(node_positions, end_links, burgers_index, SEG)
    column = jnp.arange(PAIRS, dtype=jnp.int32)
    home = column // (PAIR_DEV * N_CUTS)
    first_idx = pair_list[0]
    second_idx = pair_list[1]
    alive = first_idx >= 0
    first_block = home * BLK_DEV + jnp.clip(first_idx, 0, BLK_DEV - 1)
    ghost_slot = jnp.clip(second_idx - BLK_DEV, 0, N_CELL * CAP - 1)
    owner = ghost_slot // CAP
    wanted = ghost_request.reshape(N_CELL, N_CELL * CAP)[home, ghost_slot]
    second_block = jnp.where(second_idx < BLK_DEV, home * BLK_DEV + jnp.clip(second_idx, 0, BLK_DEV - 1), owner * BLK_DEV + jnp.clip(wanted, 0, BLK_DEV - 1))
    pair_scale = jnp.where(alive, jnp.where(first_block == second_block, 0.5, 1.0), 0.0).astype(jnp.float32)

    def one_group(forces, group_rows):
        near_rows, far_rows, scales = group_rows
        on_first, on_second = pair_forces(blocks[near_rows], blocks[far_rows], scales)
        forces = forces.at[near_rows].add(on_first).at[far_rows].add(on_second)
        return (forces, None)
    group_count = PAIRS // ref_group
    start_forces = jnp.zeros((BLOCKS, 3, SEG), jnp.float32)
    forces, unused = lax.scan(one_group, start_forces, (first_block.reshape(group_count, ref_group), second_block.reshape(group_count, ref_group), pair_scale.reshape(group_count, ref_group)))
    seg_force = jnp.transpose(forces, (1, 0, 2)).reshape(3, NODES)
    symmetric = 0.5 * (applied_stress + applied_stress.T)
    traction = jnp.dot(symmetric, vectors, precision=lax.Precision.HIGHEST)
    traction = jnp.repeat(traction, SEG, axis=1)
    seg_force = seg_force + jnp.cross(traction, line_vectors, axis=0)
    return nodal_velocity(seg_force, line_vectors, end_links)
```

```python
import functools

import jax
import jax.numpy as jnp
from jax import lax
from jax.experimental import pallas as pl
from jax.experimental.pallas import tpu as pltpu
from jax.sharding import PartitionSpec as P

SEG = 128
COMPS = 9
ROWS = 16
UNROLL = 4
MU_FACTOR = 10.0
CORE_SQUARED = 0.25
HALF_ROOT = 0.5**0.5
MESH = pl.DeviceIdType.MESH
F32 = jnp.float32
BF16 = jnp.bfloat16
I32 = jnp.int32
VMEM = pl.BlockSpec(memory_space=pltpu.VMEM)
SMEM = pl.BlockSpec(memory_space=pltpu.SMEM)
NN = (((1,), (0,)), ((), ()))
NT = (((1,), (1,)), ((), ()))


def iota(shape, axis):
    return lax.broadcasted_iota(I32, shape, axis)


def dot(a, b, dims):
    return lax.dot_general(a, b, dims, preferred_element_type=F32)


def split(value, parts):
    pieces = []
    rest = value
    for part in range(parts):
        piece = rest.astype(BF16)
        pieces.append(piece)
        if part < parts - 1:
            rest = rest - piece.astype(F32)
    return pieces


def prep_kernel(pos, conn, burg, req, data, table, reqb, links):
    blocks = data.shape[0]
    for end in range(2):
        for b in range(blocks):
            links[end, b : b + 1, :] = conn[end : end + 1, b * SEG : (b + 1) * SEG]
    low = [links[end] & (SEG - 1) for end in range(2)]
    high = [links[end] >> 7 for end in range(2)]

    def step(h, carry):
        lanes = pl.ds(pl.multiple_of(h * SEG, SEG), SEG)
        out = []
        for end in range(2):
            hit = high[end] == h
            for c in range(3):
                row = jnp.broadcast_to(pos[c : c + 1, lanes], (blocks, SEG))
                got = jnp.take_along_axis(row, low[end], axis=1)
                out.append(jnp.where(hit, got, carry[end * 3 + c]))
        return tuple(out)

    zero = jnp.zeros((blocks, SEG), F32)
    ends = lax.fori_loop(0, pos.shape[1] // SEG, step, (zero,) * 6)
    comps = [0.5 * (ends[c] + ends[3 + c]) for c in range(3)]
    comps += [ends[3 + c] - ends[c] for c in range(3)]
    diagonal = iota((blocks, blocks), 0) == iota((blocks, blocks), 1)
    spread = jnp.where(diagonal, jnp.broadcast_to(burg[...], (blocks, blocks)), 0)
    kind = jnp.broadcast_to(jnp.sum(spread, axis=1, keepdims=True), (blocks, SEG))
    odd = jnp.where((kind & 1) == 1, -HALF_ROOT, HALF_ROOT)
    comps.append(jnp.where(kind < 4, HALF_ROOT, 0.0))
    comps.append(jnp.where(kind < 2, odd, jnp.where(kind < 4, 0.0, HALF_ROOT)))
    comps.append(jnp.where(kind < 2, 0.0, odd))
    table[...] = jnp.zeros(table.shape, table.dtype)
    for c in range(COMPS):
        lanes = slice(c * SEG, (c + 1) * SEG)
        data[:, lanes] = comps[c]
        for part, piece in enumerate(split(comps[c], 3)):
            table[part * blocks : (part + 1) * blocks, lanes] = piece
    reqb[...] = jnp.full(reqb.shape, -1, I32)
    owners, cap = req.shape
    for t in range(cap):
        reqb[pl.ds(t, owners, stride=8), :] = jnp.broadcast_to(req[:, t : t + 1], (owners, SEG))


def greet(me, cut, rho, groups, cuts):
    barrier = pltpu.get_barrier_semaphore()

    def step(m, carry):
        other = m * cuts + rho

        @pl.when(other != me)
        def _():
            pl.semaphore_signal(barrier, inc=1, device_id=(other, cut), device_id_type=MESH)

        return carry

    lax.fori_loop(0, groups, step, 0)
    for d in range(1, cuts):
        peer = lax.rem(cut + d, cuts)
        pl.semaphore_signal(barrier, inc=1, device_id=(me, peer), device_id_type=MESH)
    own = jnp.where(rho == lax.rem(me, cuts), 1, 0)
    pl.semaphore_wait(barrier, groups + cuts - 1 - own)


def for_partners(me, rho, groups, cuts, run):
    def step(m, carry):
        other = m * cuts + rho

        @pl.when(other != me)
        def _():
            run(m, other)

        return carry

    lax.fori_loop(0, groups, step, 0)


def prefix(flags):
    rows, lanes = flags.shape
    value = jnp.where(flags, 1.0, 0.0).astype(F32)
    coded = value.astype(BF16)
    upper = jnp.where(iota((lanes, lanes), 0) <= iota((lanes, lanes), 1), 1.0, 0.0).astype(BF16)
    along = dot(coded, upper, NN)
    ones = jnp.ones((lanes, lanes), BF16)
    totals = dot(coded, ones, NN)
    row = iota((rows, lanes), 0)
    offset = jnp.zeros((rows, lanes), F32)
    for r in range(rows - 1):
        offset = offset + jnp.where(row > r, jnp.broadcast_to(totals[r : r + 1, :], (rows, lanes)), 0.0)
    return (along - value + offset).astype(I32)


def count(flags):
    value = jnp.where(flags, 1.0, 0.0).astype(F32)
    return jnp.sum(jnp.sum(value, axis=1, keepdims=True), axis=0, keepdims=True).astype(I32)


def share_pairs(first, second, own_rows, me, cut, cuts, cap, blocks):
    alive = first >= 0
    ghost = second >= blocks
    slot = jnp.maximum(second - blocks, 0)
    owner = slot >> 2
    part = slot & 3
    own = ghost & (owner == me)
    far = ghost & (owner != me)
    wanted = jnp.zeros_like(second)
    for t in range(cap):
        row = jnp.broadcast_to(own_rows[t : t + 1, :], second.shape)
        wanted = jnp.where(part == t, row, wanted)
    near_block = jnp.where(own, wanted, second)
    block = jnp.where(far, blocks + (owner >> 2) * cap + part, near_block)
    half = jnp.logical_and(jnp.logical_not(far), block == first)
    place = (owner + me) & 3
    far_alive = alive & far
    near_alive = alive & jnp.logical_not(far)
    target = (count(alive) + cuts - 1) >> 2
    begin = jnp.zeros((1, 1), I32)
    low = begin
    top = begin
    for j in range(cuts):
        room = jnp.maximum(target - count(far_alive & (place == j)), 0)
        low = jnp.where(cut == j, begin, low)
        top = jnp.where(cut == j, begin + room, top)
        begin = begin + room
    rank = prefix(near_alive)
    mine = (far_alive & (place == cut)) | (near_alive & (rank >= low) & (rank < top))
    spot = prefix(mine)
    first_code = jnp.where(mine, first + jnp.where(half, 64, 32), 0).astype(F32)
    second_code = jnp.where(mine, block, 0).astype(F32)
    rows, lanes = first.shape
    codes = jnp.zeros((2 * rows, lanes), F32)
    for r in range(rows):
        at = spot[r : r + 1, :]
        hit = iota((rows, lanes), 0) == jnp.broadcast_to(at >> 7, (rows, lanes))
        left = jnp.concatenate(
            [
                jnp.where(hit, jnp.broadcast_to(first_code[r : r + 1, :], (rows, lanes)), 0.0),
                jnp.where(hit, jnp.broadcast_to(second_code[r : r + 1, :], (rows, lanes)), 0.0),
            ],
            axis=0,
        ).astype(BF16)
        chosen = iota((lanes, lanes), 0) == jnp.broadcast_to(at & (lanes - 1), (lanes, lanes))
        codes = codes + dot(left, jnp.where(chosen, 1.0, 0.0).astype(BF16), NT)
    return codes.astype(I32), count(mine)


def exchange_kernel(
    cuts, groups, cap, blocks,
    reqb, table, pairs,
    ghost, asked, codes,
    plist, stage, ordered, rsend, rrecv, psend, precv, bsend, brecv,
):
    me = lax.axis_index("cell")
    cut = lax.axis_index("cuts")
    rho = lax.rem(cut - lax.rem(me, cuts) + cuts, cuts)
    slot = lax.div(me, cuts)
    asked[...] = jnp.full(asked.shape, -1, I32)
    ghost[...] = jnp.zeros(ghost.shape, F32)
    plist[cut] = jnp.zeros(plist.shape[1:], I32)
    for e in range(2):
        for r in range(2):
            plist[cut, 2 * e + r : 2 * e + r + 1, :] = pairs[e : e + 1, r * SEG : (r + 1) * SEG]
    greet(me, cut, rho, groups, cuts)

    def request_copy(m, other):
        return pltpu.make_async_remote_copy(
            src_ref=reqb.at[pl.ds(pl.multiple_of(other * 8, 8), 8)],
            dst_ref=asked.at[pl.ds(pl.multiple_of(slot * 8, 8), 8)],
            send_sem=rsend.at[m],
            recv_sem=rrecv.at[slot],
            device_id=(other, cut),
            device_id_type=MESH,
        )

    def request_arrival(m, other):
        return pltpu.make_async_remote_copy(
            src_ref=reqb.at[pl.ds(pl.multiple_of(other * 8, 8), 8)],
            dst_ref=asked.at[pl.ds(pl.multiple_of(m * 8, 8), 8)],
            send_sem=rsend.at[m],
            recv_sem=rrecv.at[m],
            device_id=(other, cut),
            device_id_type=MESH,
        )

    def pair_copy(d, at):
        return pltpu.make_async_remote_copy(
            src_ref=plist.at[cut],
            dst_ref=plist.at[at],
            send_sem=psend.at[d - 1],
            recv_sem=precv.at[at],
            device_id=(me, lax.rem(cut + d, cuts)),
            device_id_type=MESH,
        )

    for_partners(me, rho, groups, cuts, lambda m, other: request_copy(m, other).start())
    for d in range(1, cuts):
        pair_copy(d, cut).start()
    for_partners(me, rho, groups, cuts, lambda m, other: request_arrival(m, other).wait_recv())

    wide = asked.shape[0]
    lane = iota((wide, SEG), 1)
    hit = ((lane & (blocks - 1)) == asked[...]) & (lane < 3 * blocks)
    onehot = jnp.where(hit, 1.0, 0.0).astype(BF16)
    for c in range(COMPS):
        lanes = slice(c * SEG, (c + 1) * SEG)
        got = dot(onehot, table[:, lanes], NN)
        for m in range(groups):
            stage[m, :, lanes] = got[m * 8 : m * 8 + cap, :]

    def block_copy(m, other, at):
        return pltpu.make_async_remote_copy(
            src_ref=stage.at[m],
            dst_ref=ghost.at[at],
            send_sem=bsend.at[m],
            recv_sem=brecv.at[at],
            device_id=(other, cut),
            device_id_type=MESH,
        )

    for_partners(me, rho, groups, cuts, lambda m, other: block_copy(m, other, slot).start())
    for d in range(1, cuts):
        pair_copy(d, lax.rem(cut - d + cuts, cuts)).wait_recv()
    for j in range(cuts):
        ordered[0, 2 * j : 2 * j + 2, :] = plist[j, 0:2, :]
        ordered[1, 2 * j : 2 * j + 2, :] = plist[j, 2:4, :]
    own_rows = reqb[pl.ds(pl.multiple_of(me * 8, 8), 8), :]
    listed, total = share_pairs(ordered[0], ordered[1], own_rows, me, cut, cuts, cap, blocks)
    codes[0:16, :] = listed
    codes[16:24, :] = jnp.broadcast_to(total, (8, SEG))
    for_partners(me, rho, groups, cuts, lambda m, other: block_copy(m, other, m).wait_recv())
    for_partners(me, rho, groups, cuts, lambda m, other: block_copy(m, other, m).wait_send())
    for_partners(me, rho, groups, cuts, lambda m, other: request_copy(m, other).wait_send())
    for d in range(1, cuts):
        pair_copy(d, cut).wait_send()


def pair_kernel(codes, data, ghost, near_force, far_force, everything, total, moments, columns):
    blocks = data.shape[0]
    groups, cap, _ = ghost.shape
    count_all = blocks + groups * cap

    def fill(target, row, value, start, rows):
        target[pl.ds(start * ROWS + row, rows, stride=ROWS), :] = value

    def fill_moments(values, start, rows):
        for c in range(3):
            for part, piece in enumerate(split(values[c], 3)):
                fill(moments, part * 3 + c, piece.astype(F32), start, rows)

    moments[...] = jnp.where((iota(moments.shape, 0) & (ROWS - 1)) == 9, 1.0, 0.0)
    total[...] = jnp.zeros(total.shape, F32)
    everything[...] = jnp.zeros(everything.shape, F32)
    values = [data[:, c * SEG : (c + 1) * SEG] for c in range(COMPS)]
    for c in range(COMPS):
        fill(everything, c, values[c], 0, blocks)
    fill_moments(values, 0, blocks)
    for m in range(groups):
        values = [ghost[m, :, c * SEG : (c + 1) * SEG] for c in range(COMPS)]
        for c in range(COMPS):
            fill(everything, c, values[c], blocks + m * cap, cap)
        fill_moments(values, blocks + m * cap, cap)

    def tile(ref, block, rows):
        return ref[pl.ds(pl.multiple_of(block * ROWS, ROWS), rows), :]

    def spread(block, carry):
        turned = jnp.transpose(tile(everything, block, 8))
        for c in range(6):
            columns[block, c] = jnp.broadcast_to(turned[:, c : c + 1], (SEG, SEG))
        return carry

    lax.fori_loop(0, blocks, spread, 0)

    def one_pair(index):
        code = codes[index >> 7, index & (SEG - 1)]
        second = codes[8 + (index >> 7), index & (SEG - 1)]
        first = code & 31
        kind = code >> 5
        scale = jnp.where(kind == 1, MU_FACTOR, jnp.where(kind == 2, 0.5 * MU_FACTOR, 0.0))
        near = tile(everything, first, ROWS)
        far = tile(everything, second, ROWS)
        match = near[6:7] * far[6:7] + near[7:8] * far[7:8] + near[8:9] * far[8:9]
        factor = match * scale
        middle = [far[c : c + 1] for c in range(3)]
        line = [far[3 + c : 4 + c] * factor for c in range(3)]
        high, low = [], []
        step = 32
        for start in range(0, SEG, step):
            rows = slice(start, start + step)
            r = [columns[first, c, rows, :] - middle[c] for c in range(3)]
            dist = r[0] * r[0] + CORE_SQUARED + r[1] * r[1] + r[2] * r[2]
            g = (
                columns[first, 3, rows, :] * line[0]
                + columns[first, 4, rows, :] * line[1]
                + columns[first, 5, rows, :] * line[2]
            )
            inverse = lax.rsqrt(dist)
            weight = g * inverse * (inverse * inverse)
            big, small = split(weight, 2)
            high.append(big)
            low.append(small)
        high = jnp.concatenate(high, axis=0)
        low = jnp.concatenate(low, axis=0)
        near_moments = tile(moments, first, ROWS).astype(BF16)
        far_moments = tile(moments, second, ROWS).astype(BF16)
        on_first = dot(
            jnp.concatenate([far_moments, far_moments], axis=1),
            jnp.concatenate([high, low], axis=1),
            NT,
        )
        on_second = dot(
            jnp.concatenate([near_moments, near_moments], axis=1),
            jnp.concatenate([high, low], axis=0),
            NN,
        )
        return first, second, on_first, on_second

    def body(step, carry):
        results = [one_pair(step * UNROLL + u) for u in range(UNROLL)]
        for first, second, on_first, on_second in results:
            at = pl.ds(pl.multiple_of(first * ROWS, ROWS), ROWS)
            total[at, :] = total[at, :] + on_first
            at = pl.ds(pl.multiple_of(second * ROWS, ROWS), ROWS)
            total[at, :] = total[at, :] + on_second
        return carry

    lax.fori_loop(0, (codes[16, 0] + UNROLL - 1) // UNROLL, body, 0)

    def take(ref, row, start, rows):
        return ref[pl.ds(start * ROWS + row, rows, stride=ROWS), :]

    def force(start, rows, c):
        weight = take(total, 9, start, rows)
        others = take(total, c, start, rows) + take(total, 3 + c, start, rows) + take(total, 6 + c, start, rows)
        return take(everything, c, start, rows) * weight - others

    for c in range(3):
        lanes = slice(c * SEG, (c + 1) * SEG)
        near_force[:, lanes] = force(0, blocks, c)
        for m in range(groups):
            far_force[m, :, lanes] = force(blocks + m * cap, cap, c)


def return_kernel(
    cuts, groups, cap, blocks,
    near_force, far_force, asked,
    result,
    back, table, shares, bsend, brecv, ssend, srecv,
):
    me = lax.axis_index("cell")
    cut = lax.axis_index("cuts")
    rho = lax.rem(cut - lax.rem(me, cuts) + cuts, cuts)
    slot = lax.div(me, cuts)
    back[...] = jnp.zeros(back.shape, F32)
    table[...] = jnp.zeros(table.shape, F32)
    greet(me, cut, rho, groups, cuts)

    def reaction_copy(m, other, at):
        return pltpu.make_async_remote_copy(
            src_ref=far_force.at[m],
            dst_ref=back.at[at],
            send_sem=bsend.at[m],
            recv_sem=brecv.at[at],
            device_id=(other, cut),
            device_id_type=MESH,
        )

    for_partners(me, rho, groups, cuts, lambda m, other: reaction_copy(m, other, slot).start())
    wide = asked.shape[0]
    hit = iota((wide, SEG), 1) == asked[...]
    onehot = jnp.transpose(jnp.where(hit, 1.0, 0.0))[:blocks, :].astype(BF16)
    for_partners(me, rho, groups, cuts, lambda m, other: reaction_copy(m, other, m).wait_recv())
    for m in range(groups):
        table[m * 8 : m * 8 + cap, :] = back[m]
    mine = near_force[...]
    for piece in split(table[...], 3):
        mine = mine + dot(onehot, piece, NN)
    shares[cut] = mine

    def share_copy(d, at):
        return pltpu.make_async_remote_copy(
            src_ref=shares.at[cut],
            dst_ref=shares.at[at],
            send_sem=ssend.at[d - 1],
            recv_sem=srecv.at[at],
            device_id=(me, lax.rem(cut + d, cuts)),
            device_id_type=MESH,
        )

    for d in range(1, cuts):
        share_copy(d, cut).start()
    for d in range(1, cuts):
        share_copy(d, lax.rem(cut - d + cuts, cuts)).wait_recv()
    added = shares[0]
    for j in range(1, cuts):
        added = added + shares[j]
    result[...] = added
    for d in range(1, cuts):
        share_copy(d, cut).wait_send()
    for_partners(me, rho, groups, cuts, lambda m, other: reaction_copy(m, other, m).wait_send())


def node_kernel(pair_force, data, conn, stress, velocity):
    blocks = data.shape[0]
    value = [data[:, c * SEG : (c + 1) * SEG] for c in range(COMPS)]
    line = value[3:6]
    burgers = value[6:9]
    sigma = [[0.5 * (stress[a, b] + stress[b, a]) for b in range(3)] for a in range(3)]
    pull = [sigma[a][0] * burgers[0] + sigma[a][1] * burgers[1] + sigma[a][2] * burgers[2] for a in range(3)]
    fields = []
    for c in range(3):
        u, v = (c + 1) % 3, (c + 2) % 3
        turned = pull[u] * line[v] - pull[v] * line[u]
        fields.append(pair_force[:, c * SEG : (c + 1) * SEG] + turned)
    fields.append(jnp.sqrt(line[0] * line[0] + line[1] * line[1] + line[2] * line[2] + CORE_SQUARED))
    pieces = [piece for field in fields for piece in split(field, 2)]
    sums = jnp.zeros((len(pieces) * blocks, SEG), F32)
    for b in range(blocks):
        left, right = [], []
        for end in range(2):
            node = conn[end : end + 1, b * SEG : (b + 1) * SEG]
            hit = iota((blocks, SEG), 0) == jnp.broadcast_to(node >> 7, (blocks, SEG))
            column = [
                jnp.where(hit, jnp.broadcast_to(piece[b : b + 1, :].astype(F32), (blocks, SEG)), 0.0)
                for piece in pieces
            ]
            left.append(jnp.concatenate(column, axis=0).astype(BF16))
            chosen = iota((SEG, SEG), 0) == jnp.broadcast_to(node & (SEG - 1), (SEG, SEG))
            right.append(jnp.where(chosen, 1.0, 0.0).astype(BF16))
        sums = sums + dot(jnp.concatenate(left, axis=1), jnp.concatenate(right, axis=1), NT)
    merged = [sums[2 * f * blocks : (2 * f + 1) * blocks] + sums[(2 * f + 1) * blocks : (2 * f + 2) * blocks] for f in range(4)]
    for c in range(3):
        speed = merged[c] / merged[3]
        for b in range(blocks):
            velocity[c : c + 1, b * SEG : (b + 1) * SEG] = speed[b : b + 1, :]


def body(cuts, node_positions, connectivity, burgers_index, applied_stress, ghost_request, pair_list):
    blocks = burgers_index.shape[0]
    owners, cap = ghost_request.shape[1:]
    groups = owners // cuts
    nodes = node_positions.shape[1]
    width = COMPS * SEG
    shape = jax.ShapeDtypeStruct
    data, table, reqb = pl.pallas_call(
        prep_kernel,
        name="segments",
        out_shape=(
            shape((blocks, width), F32),
            shape((SEG, width), BF16),
            shape((owners * 8, SEG), I32),
        ),
        in_specs=[VMEM] * 4,
        out_specs=(VMEM,) * 3,
        scratch_shapes=[pltpu.VMEM((2, blocks, SEG), I32)],
    )(node_positions, connectivity, burgers_index.reshape(1, blocks), ghost_request[0])
    dma = pltpu.SemaphoreType.DMA
    ghost, asked, codes = pl.pallas_call(
        functools.partial(exchange_kernel, cuts, groups, cap, blocks),
        name="exchange",
        out_shape=(
            shape((groups, cap, width), F32),
            shape((groups * 8, SEG), I32),
            shape((24, SEG), I32),
        ),
        in_specs=[VMEM] * 3,
        out_specs=(VMEM,) * 3,
        scratch_shapes=[
            pltpu.VMEM((cuts, 8, SEG), I32),
            pltpu.VMEM((groups, cap, width), F32),
            pltpu.VMEM((2, 8, SEG), I32),
            dma((groups,)), dma((groups,)), dma((cuts,)), dma((cuts,)), dma((groups,)), dma((groups,)),
        ],
        compiler_params=pltpu.CompilerParams(collective_id=0, has_side_effects=True),
    )(reqb, table, pair_list)
    total_blocks = blocks + groups * cap
    near_force, far_force = pl.pallas_call(
        pair_kernel,
        name="pairs",
        out_shape=(
            shape((blocks, 3 * SEG), F32),
            shape((groups, cap, 3 * SEG), F32),
        ),
        in_specs=[SMEM, VMEM, VMEM],
        out_specs=(VMEM,) * 2,
        scratch_shapes=[
            pltpu.VMEM((total_blocks * ROWS, SEG), F32),
            pltpu.VMEM((total_blocks * ROWS, SEG), F32),
            pltpu.VMEM((total_blocks * ROWS, SEG), F32),
            pltpu.VMEM((blocks, 6, SEG, SEG), F32),
        ],
        compiler_params=pltpu.CompilerParams(vmem_limit_bytes=32 * 1024 * 1024),
    )(codes, data, ghost)
    pair_force = pl.pallas_call(
        functools.partial(return_kernel, cuts, groups, cap, blocks),
        name="reactions",
        out_shape=shape((blocks, 3 * SEG), F32),
        in_specs=[VMEM] * 3,
        out_specs=VMEM,
        scratch_shapes=[
            pltpu.VMEM((groups, cap, 3 * SEG), F32),
            pltpu.VMEM((groups * 8, 3 * SEG), F32),
            pltpu.VMEM((cuts, blocks, 3 * SEG), F32),
            dma((groups,)), dma((groups,)), dma((cuts,)), dma((cuts,)),
        ],
        compiler_params=pltpu.CompilerParams(collective_id=1, has_side_effects=True),
    )(near_force, far_force, asked)
    return pl.pallas_call(
        node_kernel,
        name="nodes",
        out_shape=shape((3, nodes), F32),
        in_specs=[VMEM, VMEM, VMEM, SMEM],
        out_specs=VMEM,
    )(pair_force, data, connectivity, applied_stress)


def solution(mesh):
    in_specs = (
        P(None, "cell"),
        P(None, "cell"),
        P("cell"),
        P(),
        P("cell", None, None),
        P(None, ("cell", "cuts")),
    )
    return jax.shard_map(
        functools.partial(body, mesh.shape["cuts"]),
        mesh=mesh,
        in_specs=in_specs,
        out_specs=P(None, "cell"),
        check_vma=False,
    )
```

```python
import functools

import jax
import jax.numpy as jnp
from jax import lax
from jax.experimental import pallas as pl
from jax.experimental.pallas import tpu as pltpu
from jax.sharding import PartitionSpec as P

SEG = 128
COMPS = 7
ROWS = 16
UNROLL = 8
MIB = 1024 * 1024
EXCHANGE_VMEM = 24 * MIB
PAIRS_VMEM = 24 * MIB
FINISH_VMEM = 16 * MIB
MU_FACTOR = 10.0
CORE_SQUARED = 0.25
HALF_ROOT = 0.5**0.5
MESH = pl.DeviceIdType.MESH
F32 = jnp.float32
BF16 = jnp.bfloat16
I32 = jnp.int32
VMEM = pl.BlockSpec(memory_space=pltpu.VMEM)
SMEM = pl.BlockSpec(memory_space=pltpu.SMEM)
NN = (((1,), (0,)), ((), ()))
NT = (((1,), (1,)), ((), ()))


def iota(shape, axis):
    return lax.broadcasted_iota(I32, shape, axis)


def dot(a, b, dims):
    return lax.dot_general(a, b, dims, preferred_element_type=F32)


def split(value, parts):
    pieces = []
    rest = value
    for part in range(parts):
        piece = rest.astype(BF16)
        pieces.append(piece)
        if part < parts - 1:
            rest = rest - piece.astype(F32)
    return pieces


def segment_values(pos, conn, burg, links):
    blocks = links.shape[1]
    for end in range(2):
        for b in range(blocks):
            links[end, b : b + 1, :] = conn[end : end + 1, b * SEG : (b + 1) * SEG]
    low = [links[end] & (SEG - 1) for end in range(2)]
    high = [links[end] >> 7 for end in range(2)]

    def step(h, carry):
        lanes = pl.ds(pl.multiple_of(h * SEG, SEG), SEG)
        out = []
        for end in range(2):
            hit = high[end] == h
            for c in range(3):
                row = jnp.broadcast_to(pos[c : c + 1, lanes], (blocks, SEG))
                got = jnp.take_along_axis(row, low[end], axis=1)
                out.append(jnp.where(hit, got, carry[end * 3 + c]))
        return tuple(out)

    zero = jnp.zeros((blocks, SEG), F32)
    ends = lax.fori_loop(0, pos.shape[1] // SEG, step, (zero,) * 6, unroll=2)
    values = [0.5 * (ends[c] + ends[3 + c]) for c in range(3)]
    values += [ends[3 + c] - ends[c] for c in range(3)]
    diagonal = iota((blocks, blocks), 0) == iota((blocks, blocks), 1)
    kinds = jnp.broadcast_to(burg[...], (blocks, blocks)).astype(F32)
    kind = jnp.sum(jnp.where(diagonal, kinds, 0.0), axis=1, keepdims=True)
    values.append(jnp.broadcast_to(kind, (blocks, SEG)))
    return values


def burgers_of(kind):
    odd = jnp.where((kind == 1.0) | (kind == 3.0) | (kind == 5.0), -HALF_ROOT, HALF_ROOT)
    return [
        jnp.where(kind < 4.0, HALF_ROOT, 0.0),
        jnp.where(kind < 2.0, odd, jnp.where(kind < 4.0, 0.0, HALF_ROOT)),
        jnp.where(kind < 2.0, 0.0, odd),
    ]


def fill_requests(req, reqb):
    cap, owners = req.shape
    reqb[...] = jnp.full(reqb.shape, -1, I32)
    diagonal = iota((owners, owners), 0) == iota((owners, owners), 1)
    for t in range(cap):
        row = jnp.broadcast_to(req[t : t + 1, :], (owners, owners)).astype(F32)
        column = jnp.sum(jnp.where(diagonal, row, 0.0), axis=1, keepdims=True)
        reqb[pl.ds(t, owners, stride=8), :] = jnp.broadcast_to(column, (owners, SEG)).astype(I32)


def spread_columns(flat, columns):
    blocks = columns.shape[0]

    def step(block, carry):
        tall = jnp.transpose(flat[pl.ds(pl.multiple_of(block * 8, 8), 8), :])
        for c in range(6):
            columns[block, c] = jnp.broadcast_to(tall[:, c : c + 1], (SEG, SEG))
        return carry

    lax.fori_loop(0, blocks, step, 0, unroll=2)


def for_partners(me, rho, groups, cuts, run):
    def step(i, carry):
        hop = jnp.where(lax.rem(i, 2) == 0, groups // 2 + lax.div(i, 2), groups // 2 - lax.div(i + 1, 2))
        m = lax.rem(lax.div(me, cuts) + hop, groups)
        other = m * cuts + rho

        @pl.when(other != me)
        def _():
            run(m, other)

        return carry

    lax.fori_loop(0, groups, step, 0)


def greet(me, cut, rho, groups, cuts):
    barrier = pltpu.get_barrier_semaphore()

    def signal(m, other):
        pl.semaphore_signal(barrier, inc=1, device_id=(other, cut), device_id_type=MESH)

    for_partners(me, rho, groups, cuts, signal)
    for d in range(1, cuts):
        peer = lax.rem(cut + d, cuts)
        pl.semaphore_signal(barrier, inc=1, device_id=(me, peer), device_id_type=MESH)


def await_greetings(me, rho, groups, cuts):
    own = jnp.where(rho == lax.rem(me, cuts), 1, 0)
    pl.semaphore_wait(pltpu.get_barrier_semaphore(), groups + cuts - 1 - own)


def prefix(flags):
    rows, lanes = flags.shape
    value = jnp.where(flags, 1.0, 0.0).astype(F32)
    coded = value.astype(BF16)
    upper = jnp.where(iota((lanes, lanes), 0) <= iota((lanes, lanes), 1), 1.0, 0.0).astype(BF16)
    along = dot(coded, upper, NN)
    ones = jnp.ones((lanes, lanes), BF16)
    totals = dot(coded, ones, NN)
    row = iota((rows, lanes), 0)
    offset = jnp.zeros((rows, lanes), F32)
    for r in range(rows - 1):
        offset = offset + jnp.where(row > r, jnp.broadcast_to(totals[r : r + 1, :], (rows, lanes)), 0.0)
    return (along - value + offset).astype(I32)


def count(flags):
    value = jnp.where(flags, 1.0, 0.0).astype(F32)
    return jnp.sum(jnp.sum(value, axis=1, keepdims=True), axis=0, keepdims=True).astype(I32)


def share_pairs(first, second, own_rows, me, cut, cuts, cap, blocks):
    alive = first >= 0
    ghost = second >= blocks
    slot = jnp.maximum(second - blocks, 0)
    owner = slot >> 2
    part = slot & 3
    own = ghost & (owner == me)
    far = ghost & (owner != me)
    wanted = jnp.zeros_like(second)
    for t in range(cap):
        row = jnp.broadcast_to(own_rows[t : t + 1, :], second.shape)
        wanted = jnp.where(part == t, row, wanted)
    near_block = jnp.where(own, wanted, second)
    block = jnp.where(far, blocks + (owner >> 2) * cap + part, near_block)
    half = jnp.logical_and(jnp.logical_not(far), block == first)
    place = (owner + me) & 3
    far_alive = alive & far
    near_alive = alive & jnp.logical_not(far)
    target = (count(alive) + cuts - 1) >> 2
    begin = jnp.zeros((1, 1), I32)
    low = begin
    top = begin
    for j in range(cuts):
        room = jnp.maximum(target - count(far_alive & (place == j)), 0)
        low = jnp.where(cut == j, begin, low)
        top = jnp.where(cut == j, begin + room, top)
        begin = begin + room
    rank = prefix(near_alive)
    mine = (far_alive & (place == cut)) | (near_alive & (rank >= low) & (rank < top))
    spot = prefix(mine)
    first_code = jnp.where(mine, first + jnp.where(half, 64, 32), 0).astype(F32)
    second_code = jnp.where(mine, block, 0).astype(F32)
    rows, lanes = first.shape
    codes = jnp.zeros((2 * rows, lanes), F32)
    for r in range(rows):
        at = spot[r : r + 1, :]
        hit = iota((rows, lanes), 0) == jnp.broadcast_to(at >> 7, (rows, lanes))
        left = jnp.concatenate(
            [
                jnp.where(hit, jnp.broadcast_to(first_code[r : r + 1, :], (rows, lanes)), 0.0),
                jnp.where(hit, jnp.broadcast_to(second_code[r : r + 1, :], (rows, lanes)), 0.0),
            ],
            axis=0,
        ).astype(BF16)
        chosen = iota((lanes, lanes), 0) == jnp.broadcast_to(at & (lanes - 1), (lanes, lanes))
        codes = codes + dot(left, jnp.where(chosen, 1.0, 0.0).astype(BF16), NT)
    return codes.astype(I32), count(mine)


def exchange_kernel(
    cuts, groups, cap, blocks,
    pos, conn, burg, req, pairs,
    data, ghost, asked, codes, columns,
    links, flat, reqb, table, plist, stage, ordered, rsend, rrecv, psend, precv, bsend, brecv,
):
    me = lax.axis_index("cell")
    cut = lax.axis_index("cuts")
    rho = lax.rem(cut - lax.rem(me, cuts) + cuts, cuts)
    slot = lax.div(me, cuts)
    asked[...] = jnp.full(asked.shape, -1, I32)
    ghost[...] = jnp.zeros(ghost.shape, F32)
    greet(me, cut, rho, groups, cuts)
    fill_requests(req, reqb)
    plist[cut] = jnp.zeros(plist.shape[1:], I32)
    for e in range(2):
        for r in range(2):
            plist[cut, 2 * e + r : 2 * e + r + 1, :] = pairs[e : e + 1, r * SEG : (r + 1) * SEG]
    await_greetings(me, rho, groups, cuts)

    def request_copy(m, other):
        return pltpu.make_async_remote_copy(
            src_ref=reqb.at[pl.ds(pl.multiple_of(other * 8, 8), 8)],
            dst_ref=asked.at[pl.ds(pl.multiple_of(slot * 8, 8), 8)],
            send_sem=rsend.at[m],
            recv_sem=rrecv.at[slot],
            device_id=(other, cut),
            device_id_type=MESH,
        )

    def request_arrival(m, other):
        return pltpu.make_async_remote_copy(
            src_ref=reqb.at[pl.ds(pl.multiple_of(other * 8, 8), 8)],
            dst_ref=asked.at[pl.ds(pl.multiple_of(m * 8, 8), 8)],
            send_sem=rsend.at[m],
            recv_sem=rrecv.at[m],
            device_id=(other, cut),
            device_id_type=MESH,
        )

    def pair_copy(d, at):
        return pltpu.make_async_remote_copy(
            src_ref=plist.at[cut],
            dst_ref=plist.at[at],
            send_sem=psend.at[d - 1],
            recv_sem=precv.at[at],
            device_id=(me, lax.rem(cut + d, cuts)),
            device_id_type=MESH,
        )

    for_partners(me, rho, groups, cuts, lambda m, other: request_copy(m, other).start())
    for d in range(1, cuts):
        pair_copy(d, cut).start()
    values = segment_values(pos, conn, burg, links)
    table[...] = jnp.zeros(table.shape, table.dtype)
    for c in range(COMPS):
        lanes = slice(c * SEG, (c + 1) * SEG)
        data[:, lanes] = values[c]
        flat[pl.ds(c, blocks, stride=8), :] = values[c]
        for part, piece in enumerate(split(values[c], 3)):
            table[part * blocks : (part + 1) * blocks, lanes] = piece
    for_partners(me, rho, groups, cuts, lambda m, other: request_arrival(m, other).wait_recv())

    wide = asked.shape[0]
    lane = iota((wide, SEG), 1)
    hit = ((lane & (blocks - 1)) == asked[...]) & (lane < 3 * blocks)
    onehot = jnp.where(hit, 1.0, 0.0).astype(BF16)
    for c in range(COMPS):
        lanes = slice(c * SEG, (c + 1) * SEG)
        got = dot(onehot, table[:, lanes], NN)
        for m in range(groups):
            stage[m, :, lanes] = got[m * 8 : m * 8 + cap, :]

    def block_copy(m, other, at):
        return pltpu.make_async_remote_copy(
            src_ref=stage.at[m],
            dst_ref=ghost.at[at],
            send_sem=bsend.at[m],
            recv_sem=brecv.at[at],
            device_id=(other, cut),
            device_id_type=MESH,
        )

    for_partners(me, rho, groups, cuts, lambda m, other: block_copy(m, other, slot).start())
    spread_columns(flat, columns)
    for d in range(1, cuts):
        pair_copy(d, lax.rem(cut - d + cuts, cuts)).wait_recv()
    for j in range(cuts):
        ordered[0, 2 * j : 2 * j + 2, :] = plist[j, 0:2, :]
        ordered[1, 2 * j : 2 * j + 2, :] = plist[j, 2:4, :]
    own_rows = reqb[pl.ds(pl.multiple_of(me * 8, 8), 8), :]
    listed, total = share_pairs(ordered[0], ordered[1], own_rows, me, cut, cuts, cap, blocks)
    codes[0:16, :] = listed
    codes[16:24, :] = jnp.broadcast_to(total, (8, SEG))
    for_partners(me, rho, groups, cuts, lambda m, other: block_copy(m, other, m).wait_recv())
    for_partners(me, rho, groups, cuts, lambda m, other: block_copy(m, other, m).wait_send())
    for_partners(me, rho, groups, cuts, lambda m, other: request_copy(m, other).wait_send())
    for d in range(1, cuts):
        pair_copy(d, cut).wait_send()


def pair_kernel(codes, data, ghost, columns, near_force, far_force, everything, total, moments):
    blocks = data.shape[0]
    groups, cap, _ = ghost.shape

    def fill(target, row, value, start, rows):
        target[pl.ds(start * ROWS + row, rows, stride=ROWS), :] = value

    def fill_moments(values, start, rows):
        for c in range(3):
            for part, piece in enumerate(split(values[c], 3)):
                fill(moments, part * 3 + c, piece.astype(F32), start, rows)

    def tile(ref, block, rows):
        return ref[pl.ds(pl.multiple_of(block * ROWS, ROWS), rows), :]

    def fill_block(values, start):
        rows = values[0].shape[0]
        for c, value in enumerate(values[:6] + burgers_of(values[6])):
            fill(everything, c, value, start, rows)
        fill_moments(values, start, rows)

    moments[...] = jnp.where((iota(moments.shape, 0) & (ROWS - 1)) == 9, 1.0, 0.0)
    total[...] = jnp.zeros(total.shape, F32)
    fill_block([data[:, c * SEG : (c + 1) * SEG] for c in range(COMPS)], 0)
    for m in range(groups):
        fill_block([ghost[m, :, c * SEG : (c + 1) * SEG] for c in range(COMPS)], blocks + m * cap)

    def one_pair(index):
        code = codes[index >> 7, index & (SEG - 1)]
        second = codes[8 + (index >> 7), index & (SEG - 1)]
        first = code & 31
        kind = code >> 5
        scale = jnp.where(kind == 1, MU_FACTOR, jnp.where(kind == 2, 0.5 * MU_FACTOR, 0.0))
        near = tile(everything, first, ROWS)
        far = tile(everything, second, ROWS)
        match = near[6:7] * far[6:7] + near[7:8] * far[7:8] + near[8:9] * far[8:9]
        factor = match * scale
        middle = [far[c : c + 1] for c in range(3)]
        line = [far[3 + c : 4 + c] * factor for c in range(3)]
        high, low = [], []
        step = 32
        for start in range(0, SEG, step):
            rows = slice(start, start + step)
            r = [columns[first, c, rows, :] - middle[c] for c in range(3)]
            dist = r[0] * r[0] + CORE_SQUARED + r[1] * r[1] + r[2] * r[2]
            g = (
                columns[first, 3, rows, :] * line[0]
                + columns[first, 4, rows, :] * line[1]
                + columns[first, 5, rows, :] * line[2]
            )
            inverse = lax.rsqrt(dist)
            weight = g * inverse * (inverse * inverse)
            big, small = split(weight, 2)
            high.append(big)
            low.append(small)
        high = jnp.concatenate(high, axis=0)
        low = jnp.concatenate(low, axis=0)
        near_moments = tile(moments, first, ROWS).astype(BF16)
        far_moments = tile(moments, second, ROWS).astype(BF16)
        on_first = dot(
            jnp.concatenate([far_moments, far_moments], axis=1),
            jnp.concatenate([high, low], axis=1),
            NT,
        )
        on_second = dot(
            jnp.concatenate([near_moments, near_moments], axis=1),
            jnp.concatenate([high, low], axis=0),
            NN,
        )
        return first, second, on_first, on_second

    def body(step, carry):
        results = [one_pair(step * UNROLL + u) for u in range(UNROLL)]
        for first, second, on_first, on_second in results:
            at = pl.ds(pl.multiple_of(first * ROWS, ROWS), ROWS)
            total[at, :] = total[at, :] + on_first
            at = pl.ds(pl.multiple_of(second * ROWS, ROWS), ROWS)
            total[at, :] = total[at, :] + on_second
        return carry

    lax.fori_loop(0, (codes[16, 0] + UNROLL - 1) // UNROLL, body, 0)

    def take(ref, row, start, rows):
        return ref[pl.ds(start * ROWS + row, rows, stride=ROWS), :]

    def force(start, rows, c):
        weight = take(total, 9, start, rows)
        others = take(total, c, start, rows) + take(total, 3 + c, start, rows) + take(total, 6 + c, start, rows)
        return take(everything, c, start, rows) * weight - others

    for c in range(3):
        lanes = slice(c * SEG, (c + 1) * SEG)
        near_force[:, lanes] = force(0, blocks, c)
        for m in range(groups):
            far_force[m, :, lanes] = force(blocks + m * cap, cap, c)


def finish_kernel(
    cuts, groups, cap, blocks,
    near_force, far_force, asked, data, conn, stress,
    velocity,
    back, table, shares, chosen, pieces, base, bsend, brecv, ssend, srecv,
):
    me = lax.axis_index("cell")
    cut = lax.axis_index("cuts")
    rho = lax.rem(cut - lax.rem(me, cuts) + cuts, cuts)
    slot = lax.div(me, cuts)
    back[...] = jnp.zeros(back.shape, F32)
    greet(me, cut, rho, groups, cuts)
    table[...] = jnp.zeros(table.shape, F32)

    def node_of(b, end):
        return conn[end : end + 1, pl.ds(pl.multiple_of(b * SEG, SEG), SEG)]

    def choose(b, carry):
        for end in range(2):
            low = jnp.broadcast_to(node_of(b, end) & (SEG - 1), (SEG, SEG))
            hit = iota((SEG, SEG), 0) == low
            chosen[b, :, end * SEG : (end + 1) * SEG] = jnp.where(hit, 1.0, 0.0).astype(BF16)
        return carry

    lax.fori_loop(0, blocks, choose, 0, unroll=2)
    await_greetings(me, rho, groups, cuts)

    def reaction_copy(m, other, at):
        return pltpu.make_async_remote_copy(
            src_ref=far_force.at[m],
            dst_ref=back.at[at],
            send_sem=bsend.at[m],
            recv_sem=brecv.at[at],
            device_id=(other, cut),
            device_id_type=MESH,
        )

    for_partners(me, rho, groups, cuts, lambda m, other: reaction_copy(m, other, slot).start())

    def node_sums(first, last):
        def step(g, carry):
            at = pl.ds(pl.multiple_of(g * 8, 8), 8)
            eight = [pieces[p, at, :] for p in range(first, last)]
            for i in range(8):
                b = g * 8 + i
                left = []
                for end in range(2):
                    high = jnp.broadcast_to(node_of(b, end) >> 7, (blocks, SEG))
                    hit = iota((blocks, SEG), 0) == high
                    column = [
                        jnp.where(hit, jnp.broadcast_to(piece[i : i + 1, :], (blocks, SEG)), 0.0)
                        for piece in eight
                    ]
                    left.append(jnp.concatenate(column, axis=0).astype(BF16))
                carry = carry + dot(jnp.concatenate(left, axis=1), chosen[b], NT)
            return carry

        start = jnp.zeros(((last - first) * blocks, SEG), F32)
        sums = lax.fori_loop(0, blocks // 8, step, start)
        rows = [sums[p * blocks : (p + 1) * blocks] for p in range(last - first)]
        return [rows[p] + rows[p + 1] for p in range(0, last - first, 2)]

    def set_piece(at, value):
        for part, piece in enumerate(split(value, 2)):
            pieces[at + part] = piece.astype(F32)

    value = [data[:, c * SEG : (c + 1) * SEG] for c in range(COMPS)]
    line = value[3:6]
    burgers = burgers_of(value[6])
    sigma = [[0.5 * (stress[a, b] + stress[b, a]) for b in range(3)] for a in range(3)]
    pull = [sigma[a][0] * burgers[0] + sigma[a][1] * burgers[1] + sigma[a][2] * burgers[2] for a in range(3)]
    for c in range(3):
        u, v = (c + 1) % 3, (c + 2) % 3
        base[:, c * SEG : (c + 1) * SEG] = pull[u] * line[v] - pull[v] * line[u]
    set_piece(6, jnp.sqrt(line[0] * line[0] + line[1] * line[1] + line[2] * line[2] + CORE_SQUARED))
    drag = node_sums(6, 8)[0]
    wide = asked.shape[0]
    hit = iota((wide, SEG), 1) == asked[...]
    onehot = jnp.transpose(jnp.where(hit, 1.0, 0.0))[:blocks, :].astype(BF16)
    for_partners(me, rho, groups, cuts, lambda m, other: reaction_copy(m, other, m).wait_recv())
    for m in range(groups):
        table[m * 8 : m * 8 + cap, :] = back[m]
    mine = near_force[...]
    for piece in split(table[...], 3):
        mine = mine + dot(onehot, piece, NN)
    shares[cut] = mine

    def share_copy(d, at):
        return pltpu.make_async_remote_copy(
            src_ref=shares.at[cut],
            dst_ref=shares.at[at],
            send_sem=ssend.at[d - 1],
            recv_sem=srecv.at[at],
            device_id=(me, lax.rem(cut + d, cuts)),
            device_id_type=MESH,
        )

    for d in range(1, cuts):
        share_copy(d, cut).start()
    for d in range(1, cuts):
        share_copy(d, lax.rem(cut - d + cuts, cuts)).wait_recv()
    added = base[...]
    for j in range(cuts):
        added = added + shares[j]
    for c in range(3):
        set_piece(2 * c, added[:, c * SEG : (c + 1) * SEG])
    sums = node_sums(0, 6)
    for c in range(3):
        speed = sums[c] / drag
        for b in range(blocks):
            velocity[c : c + 1, b * SEG : (b + 1) * SEG] = speed[b : b + 1, :]
    for d in range(1, cuts):
        share_copy(d, cut).wait_send()
    for_partners(me, rho, groups, cuts, lambda m, other: reaction_copy(m, other, m).wait_send())


def body(cuts, node_positions, connectivity, burgers_index, applied_stress, ghost_request, pair_list):
    blocks = burgers_index.shape[0]
    owners, cap = ghost_request.shape[1:]
    groups = owners // cuts
    nodes = node_positions.shape[1]
    width = COMPS * SEG
    shape = jax.ShapeDtypeStruct
    dma = pltpu.SemaphoreType.DMA
    data, ghost, asked, codes, columns = pl.pallas_call(
        functools.partial(exchange_kernel, cuts, groups, cap, blocks),
        name="exchange",
        out_shape=(
            shape((blocks, width), F32),
            shape((groups, cap, width), F32),
            shape((groups * 8, SEG), I32),
            shape((24, SEG), I32),
            shape((blocks, 6, SEG, SEG), F32),
        ),
        in_specs=[VMEM] * 5,
        out_specs=(VMEM,) * 5,
        scratch_shapes=[
            pltpu.VMEM((2, blocks, SEG), I32),
            pltpu.VMEM((blocks * 8, SEG), F32),
            pltpu.VMEM((owners * 8, SEG), I32),
            pltpu.VMEM((SEG, width), BF16),
            pltpu.VMEM((cuts, 8, SEG), I32),
            pltpu.VMEM((groups, cap, width), F32),
            pltpu.VMEM((2, 8, SEG), I32),
            dma((groups,)), dma((groups,)), dma((cuts,)), dma((cuts,)), dma((groups,)), dma((groups,)),
        ],
        compiler_params=pltpu.CompilerParams(
            collective_id=0, has_side_effects=True, vmem_limit_bytes=EXCHANGE_VMEM
        ),
    )(
        node_positions,
        connectivity,
        burgers_index.reshape(1, blocks),
        jnp.transpose(ghost_request[0]),
        pair_list,
    )
    near_force, far_force = run_pairs(codes, data, ghost, columns)
    return pl.pallas_call(
        functools.partial(finish_kernel, cuts, groups, cap, blocks),
        name="finish",
        out_shape=shape((3, nodes), F32),
        in_specs=[VMEM] * 5 + [SMEM],
        out_specs=VMEM,
        scratch_shapes=[
            pltpu.VMEM((groups, cap, 3 * SEG), F32),
            pltpu.VMEM((groups * 8, 3 * SEG), F32),
            pltpu.VMEM((cuts, blocks, 3 * SEG), F32),
            pltpu.VMEM((blocks, SEG, 2 * SEG), BF16),
            pltpu.VMEM((8, blocks, SEG), F32),
            pltpu.VMEM((blocks, 3 * SEG), F32),
            dma((groups,)), dma((groups,)), dma((cuts,)), dma((cuts,)),
        ],
        compiler_params=pltpu.CompilerParams(
            collective_id=1, has_side_effects=True, vmem_limit_bytes=FINISH_VMEM
        ),
    )(near_force, far_force, asked, data, connectivity, applied_stress)


def run_pairs(codes, data, ghost, columns):
    groups, cap, _ = ghost.shape
    blocks = data.shape[0]
    shape = jax.ShapeDtypeStruct
    total_blocks = blocks + groups * cap
    return pl.pallas_call(
        pair_kernel,
        name="pairs",
        out_shape=(shape((blocks, 3 * SEG), F32), shape((groups, cap, 3 * SEG), F32)),
        in_specs=[SMEM, VMEM, VMEM, VMEM],
        out_specs=(VMEM,) * 2,
        scratch_shapes=[pltpu.VMEM((total_blocks * ROWS, SEG), F32)] * 3,
        compiler_params=pltpu.CompilerParams(vmem_limit_bytes=PAIRS_VMEM),
    )(codes, data, ghost, columns)


def solution(mesh):
    in_specs = (
        P(None, "cell"),
        P(None, "cell"),
        P("cell"),
        P(),
        P("cell", None, None),
        P(None, ("cell", "cuts")),
    )
    return jax.shard_map(
        functools.partial(body, mesh.shape["cuts"]),
        mesh=mesh,
        in_specs=in_specs,
        out_specs=P(None, "cell"),
        check_vma=False,
    )
```

```python
import functools

import jax
import jax.numpy as jnp
from jax import lax
from jax.experimental import pallas as pl
from jax.experimental.pallas import tpu as pltpu
from jax.sharding import PartitionSpec as P

SEG = 128
COMPS = 7
SENT = 6
FIRST_ASK = 64
ROWS = 16
UNROLL = 8
MIB = 1024 * 1024
EXCHANGE_VMEM = 24 * MIB
PAIRS_VMEM = 24 * MIB
FINISH_VMEM = 16 * MIB
MU_FACTOR = 10.0
CORE_SQUARED = 0.25
HALF_ROOT = 0.5**0.5
MESH = pl.DeviceIdType.MESH
F32 = jnp.float32
BF16 = jnp.bfloat16
I32 = jnp.int32
VMEM = pl.BlockSpec(memory_space=pltpu.VMEM)
SMEM = pl.BlockSpec(memory_space=pltpu.SMEM)
ANY = pl.BlockSpec(memory_space=pltpu.HBM)
NN = (((1,), (0,)), ((), ()))
NT = (((1,), (1,)), ((), ()))


def stay(value):
    return pltpu.with_memory_space_constraint(value, pltpu.HBM)


def iota(shape, axis):
    return lax.broadcasted_iota(I32, shape, axis)


def dot(a, b, dims):
    return lax.dot_general(a, b, dims, preferred_element_type=F32)


def split(value, parts):
    pieces = []
    rest = value
    for part in range(parts):
        piece = rest.astype(BF16)
        pieces.append(piece)
        if part < parts - 1:
            rest = rest - piece.astype(F32)
    return pieces


def segment_values(pos, conn, burg, links):
    blocks = links.shape[1]
    for end in range(2):
        for b in range(blocks):
            links[end, b : b + 1, :] = conn[end : end + 1, b * SEG : (b + 1) * SEG]
    low = [links[end] & (SEG - 1) for end in range(2)]
    high = [links[end] >> 7 for end in range(2)]

    def step(h, carry):
        lanes = pl.ds(pl.multiple_of(h * SEG, SEG), SEG)
        out = []
        for end in range(2):
            hit = high[end] == h
            for c in range(3):
                row = jnp.broadcast_to(pos[c : c + 1, lanes], (blocks, SEG))
                got = jnp.take_along_axis(row, low[end], axis=1)
                out.append(jnp.where(hit, got, carry[end * 3 + c]))
        return tuple(out)

    zero = jnp.zeros((blocks, SEG), F32)
    ends = lax.fori_loop(0, pos.shape[1] // SEG, step, (zero,) * 6, unroll=2)
    values = [0.5 * (ends[c] + ends[3 + c]) for c in range(3)]
    values += [ends[3 + c] - ends[c] for c in range(3)]
    diagonal = iota((blocks, blocks), 0) == iota((blocks, blocks), 1)
    kinds = jnp.broadcast_to(burg[...], (blocks, blocks)).astype(F32)
    kind = jnp.sum(jnp.where(diagonal, kinds, 0.0), axis=1, keepdims=True)
    values.append(jnp.broadcast_to(kind, (blocks, SEG)))
    return values


def burgers_of(kind):
    return [HALF_ROOT * value for value in whole_burgers(kind)]


def fill_requests(req, burg, wide, rows):
    cap, owners = req.shape
    blocks = burg.shape[1]
    wide[...] = jnp.zeros(wide.shape, I32)
    wide[:, 0:blocks] = burg[...]
    message = jnp.broadcast_to(wide[...], (owners, SEG))
    lane = iota((owners, SEG), 1)
    diagonal = iota((owners, owners), 0) == iota((owners, owners), 1)
    for t in range(cap):
        row = jnp.broadcast_to(req[t : t + 1, :], (owners, owners)).astype(F32)
        column = jnp.sum(jnp.where(diagonal, row, 0.0), axis=1, keepdims=True)
        column = jnp.broadcast_to(column, (owners, SEG)).astype(I32)
        message = jnp.where(lane == FIRST_ASK + t, column, message)
    for o in range(owners):
        rows[o] = message[o : o + 1, :]


def kind_table(own, heard, said, cap):
    groups = heard.shape[0]
    lane = iota((groups, SEG), 1)
    blocks = FIRST_ASK // 2
    wanted = jnp.zeros((groups, SEG), I32)
    for t in range(cap):
        column = jnp.broadcast_to(said[:, FIRST_ASK + t : FIRST_ASK + t + 1], (groups, SEG))
        wanted = jnp.where((lane & 3) == t, column, wanted)
    found = jnp.take_along_axis(heard, jnp.maximum(wanted, 0), axis=1)
    here = (lane >= blocks) & (((lane - blocks) >> 2) == iota((groups, SEG), 0))
    ghosts = jnp.sum(jnp.where(here, found, 0).astype(F32), axis=0, keepdims=True)
    return jnp.where(iota((1, SEG), 1) < blocks, own.astype(F32), ghosts)


def whole_burgers(kind):
    odd = jnp.where((kind == 1.0) | (kind == 3.0) | (kind == 5.0), -1.0, 1.0)
    return [
        jnp.where(kind < 4.0, 1.0, 0.0),
        jnp.where(kind < 2.0, odd, jnp.where(kind < 4.0, 0.0, 1.0)),
        jnp.where(kind < 2.0, 0.0, odd),
    ]


def spread_columns(flat, columns):
    blocks = columns.shape[0]

    def step(block, carry):
        tall = jnp.transpose(flat[pl.ds(pl.multiple_of(block * 8, 8), 8), :])
        for c in range(6):
            columns[block, c] = jnp.broadcast_to(tall[:, c : c + 1], (SEG, SEG))
        return carry

    lax.fori_loop(0, blocks, step, 0, unroll=2)


def for_partners(me, rho, groups, cuts, run):
    def step(i, carry):
        hop = jnp.where(lax.rem(i, 2) == 0, groups // 2 + lax.div(i, 2), groups // 2 - lax.div(i + 1, 2))
        m = lax.rem(lax.div(me, cuts) + hop, groups)
        other = m * cuts + rho

        @pl.when(other != me)
        def _():
            run(m, other)

        return carry

    lax.fori_loop(0, groups, step, 0)


def greet(me, cut, rho, groups, cuts):
    barrier = pltpu.get_barrier_semaphore()

    def signal(m, other):
        pl.semaphore_signal(barrier, inc=1, device_id=(other, cut), device_id_type=MESH)

    for_partners(me, rho, groups, cuts, signal)
    for d in range(1, cuts):
        peer = lax.rem(cut + d, cuts)
        pl.semaphore_signal(barrier, inc=1, device_id=(me, peer), device_id_type=MESH)


def await_greetings(me, rho, groups, cuts):
    own = jnp.where(rho == lax.rem(me, cuts), 1, 0)
    pl.semaphore_wait(pltpu.get_barrier_semaphore(), groups + cuts - 1 - own)


def prefix(flags):
    rows, lanes = flags.shape
    value = jnp.where(flags, 1.0, 0.0).astype(F32)
    coded = value.astype(BF16)
    upper = jnp.where(iota((lanes, lanes), 0) <= iota((lanes, lanes), 1), 1.0, 0.0).astype(BF16)
    along = dot(coded, upper, NN)
    ones = jnp.ones((lanes, lanes), BF16)
    totals = dot(coded, ones, NN)
    row = iota((rows, lanes), 0)
    offset = jnp.zeros((rows, lanes), F32)
    for r in range(rows - 1):
        offset = offset + jnp.where(row > r, jnp.broadcast_to(totals[r : r + 1, :], (rows, lanes)), 0.0)
    return (along - value + offset).astype(I32)


def count(flags):
    value = jnp.where(flags, 1.0, 0.0).astype(F32)
    return jnp.sum(jnp.sum(value, axis=1, keepdims=True), axis=0, keepdims=True).astype(I32)


def share_pairs(first, second, own_row, kinds, me, cut, cuts, cap, blocks):
    used = first >= 0
    ghost = second >= blocks
    slot = jnp.maximum(second - blocks, 0)
    owner = slot >> 2
    part = slot & 3
    own = ghost & (owner == me)
    far = ghost & (owner != me)
    wanted = jnp.zeros_like(second)
    for t in range(cap):
        row = jnp.broadcast_to(own_row[:, FIRST_ASK + t : FIRST_ASK + t + 1], second.shape)
        wanted = jnp.where(part == t, row, wanted)
    near_block = jnp.where(own, wanted, second)
    block = jnp.where(far, blocks + (owner >> 2) * cap + part, near_block)
    half = jnp.logical_and(jnp.logical_not(far), block == first)
    table = jnp.broadcast_to(kinds, first.shape)
    one = whole_burgers(jnp.take_along_axis(table, jnp.maximum(first, 0), axis=1))
    two = whole_burgers(jnp.take_along_axis(table, jnp.maximum(block, 0), axis=1))
    match = one[0] * two[0] + one[1] * two[1] + one[2] * two[2]
    match = jnp.where(half, 0.5 * match, match).astype(I32)
    alive = used & (match != 0)
    place = (owner + me) & 3
    far_alive = alive & far
    near_alive = alive & jnp.logical_not(far)
    shares = [(count(used & far & (place == j)) * 53) >> 6 for j in range(cuts)]
    target = (count(near_alive) + sum(shares) + cuts - 1) >> 2
    begin = jnp.zeros((1, 1), I32)
    low = begin
    top = begin
    for j in range(cuts):
        room = jnp.maximum(target - shares[j], 0)
        low = jnp.where(cut == j, begin, low)
        top = jnp.where(cut == j, begin + room, top)
        begin = begin + room
    rank = prefix(near_alive)
    mine = (far_alive & (place == cut)) | (near_alive & (rank >= low) & (rank < top))
    spot = prefix(mine)
    first_code = jnp.where(mine, first + 32 * (match + 2), 0).astype(F32)
    second_code = jnp.where(mine, block, 0).astype(F32)
    rows, lanes = first.shape
    codes = jnp.zeros((2 * rows, lanes), F32)
    for r in range(rows):
        at = spot[r : r + 1, :]
        hit = iota((rows, lanes), 0) == jnp.broadcast_to(at >> 7, (rows, lanes))
        left = jnp.concatenate(
            [
                jnp.where(hit, jnp.broadcast_to(first_code[r : r + 1, :], (rows, lanes)), 0.0),
                jnp.where(hit, jnp.broadcast_to(second_code[r : r + 1, :], (rows, lanes)), 0.0),
            ],
            axis=0,
        ).astype(BF16)
        chosen = iota((lanes, lanes), 0) == jnp.broadcast_to(at & (lanes - 1), (lanes, lanes))
        codes = codes + dot(left, jnp.where(chosen, 1.0, 0.0).astype(BF16), NT)
    return codes.astype(I32), count(mine)


def exchange_kernel(
    cuts, groups, cap, blocks,
    pos_in, conn_in, burg_in, req_in, pairs_in,
    data, ghost, asked, codes, columns,
    pos, conn, burg, req, pairs, links, flat, wide, rows, heard, table, plist, stage, ordered,
    isem, rsend, rrecv, psend, precv, bsend, brecv,
):
    me = lax.axis_index("cell")
    cut = lax.axis_index("cuts")
    rho = lax.rem(cut - lax.rem(me, cuts) + cuts, cuts)
    slot = lax.div(me, cuts)
    inputs = [(req_in, req), (burg_in, burg), (pairs_in, pairs), (conn_in, conn), (pos_in, pos)]
    loads = [pltpu.make_async_copy(src, dst, isem.at[i]) for i, (src, dst) in enumerate(inputs)]
    for load in loads:
        load.start()
    heard[...] = jnp.full(heard.shape, -1, I32)
    ghost[...] = jnp.zeros(ghost.shape, F32)
    greet(me, cut, rho, groups, cuts)
    for load in loads[:3]:
        load.wait()
    fill_requests(req, burg, wide, rows)
    plist[cut] = jnp.zeros(plist.shape[1:], I32)
    for e in range(2):
        for r in range(2):
            plist[cut, 2 * e + r : 2 * e + r + 1, :] = pairs[e : e + 1, r * SEG : (r + 1) * SEG]
    await_greetings(me, rho, groups, cuts)

    def request_copy(m, other, at):
        return pltpu.make_async_remote_copy(
            src_ref=rows.at[other],
            dst_ref=heard.at[at],
            send_sem=rsend.at[m],
            recv_sem=rrecv.at[at],
            device_id=(other, cut),
            device_id_type=MESH,
        )

    def pair_copy(d, at):
        return pltpu.make_async_remote_copy(
            src_ref=plist.at[cut],
            dst_ref=plist.at[at],
            send_sem=psend.at[d - 1],
            recv_sem=precv.at[at],
            device_id=(me, lax.rem(cut + d, cuts)),
            device_id_type=MESH,
        )

    for_partners(me, rho, groups, cuts, lambda m, other: request_copy(m, other, slot).start())
    for d in range(1, cuts):
        pair_copy(d, cut).start()
    for load in loads[3:]:
        load.wait()
    values = segment_values(pos, conn, burg, links)
    table[...] = jnp.zeros(table.shape, table.dtype)
    for c in range(COMPS):
        lanes = slice(c * SEG, (c + 1) * SEG)
        data[:, lanes] = values[c]
        if c == SENT:
            continue
        flat[pl.ds(c, blocks, stride=8), :] = values[c]
        for part, piece in enumerate(split(values[c], 3)):
            table[part * blocks : (part + 1) * blocks, lanes] = piece
    for_partners(me, rho, groups, cuts, lambda m, other: request_copy(m, other, m).wait_recv())
    hear = jnp.concatenate([heard[m] for m in range(groups)], axis=0)
    asked[...] = jnp.full(asked.shape, -1, I32)
    for t in range(cap):
        column = hear[:, FIRST_ASK + t : FIRST_ASK + t + 1]
        asked[pl.ds(t, groups, stride=8), :] = jnp.broadcast_to(column, (groups, SEG))

    lane = iota(asked.shape, 1)
    hit = ((lane & (blocks - 1)) == asked[...]) & (lane < 3 * blocks)
    onehot = jnp.where(hit, 1.0, 0.0).astype(BF16)
    for c in range(SENT):
        lanes = slice(c * SEG, (c + 1) * SEG)
        got = dot(onehot, table[:, lanes], NN)
        for m in range(groups):
            stage[m, :, lanes] = got[m * 8 : m * 8 + cap, :]

    def block_copy(m, other, at):
        return pltpu.make_async_remote_copy(
            src_ref=stage.at[m],
            dst_ref=ghost.at[at],
            send_sem=bsend.at[m],
            recv_sem=brecv.at[at],
            device_id=(other, cut),
            device_id_type=MESH,
        )

    for_partners(me, rho, groups, cuts, lambda m, other: block_copy(m, other, slot).start())
    spread_columns(flat, columns)
    for d in range(1, cuts):
        pair_copy(d, lax.rem(cut - d + cuts, cuts)).wait_recv()
    for j in range(cuts):
        ordered[0, 2 * j : 2 * j + 2, :] = plist[j, 0:2, :]
        ordered[1, 2 * j : 2 * j + 2, :] = plist[j, 2:4, :]
    said = jnp.concatenate([rows[m * cuts + rho] for m in range(groups)], axis=0)
    own_row = rows[me]
    kinds = kind_table(own_row, hear, said, cap)
    listed, total = share_pairs(ordered[0], ordered[1], own_row, kinds, me, cut, cuts, cap, blocks)
    codes[0:16, :] = listed
    codes[16:24, :] = jnp.broadcast_to(total, (8, SEG))
    for_partners(me, rho, groups, cuts, lambda m, other: block_copy(m, other, m).wait_recv())
    for_partners(me, rho, groups, cuts, lambda m, other: block_copy(m, other, m).wait_send())
    for_partners(me, rho, groups, cuts, lambda m, other: request_copy(m, other, m).wait_send())
    for d in range(1, cuts):
        pair_copy(d, cut).wait_send()


def pair_kernel(codes, data, ghost, columns, near_force, far_force, everything, total, moments):
    blocks = data.shape[0]
    groups, cap, _ = ghost.shape

    def fill(target, row, value, start, rows):
        target[pl.ds(start * ROWS + row, rows, stride=ROWS), :] = value

    def fill_moments(values, start, rows):
        for c in range(3):
            for part, piece in enumerate(split(values[c], 3)):
                fill(moments, part * 3 + c, piece.astype(F32), start, rows)

    def tile(ref, block, rows):
        return ref[pl.ds(pl.multiple_of(block * ROWS, ROWS), rows), :]

    def fill_block(values, start):
        rows = values[0].shape[0]
        for c, value in enumerate(values):
            fill(everything, c, value, start, rows)
        fill_moments(values, start, rows)

    moments[...] = jnp.where((iota(moments.shape, 0) & (ROWS - 1)) == 9, 1.0, 0.0)
    total[...] = jnp.zeros(total.shape, F32)
    fill_block([data[:, c * SEG : (c + 1) * SEG] for c in range(SENT)], 0)
    for m in range(groups):
        fill_block([ghost[m, :, c * SEG : (c + 1) * SEG] for c in range(SENT)], blocks + m * cap)

    def one_pair(index):
        code = codes[index >> 7, index & (SEG - 1)]
        second = codes[8 + (index >> 7), index & (SEG - 1)]
        first = code & 31
        kind = code >> 5
        factor = jnp.where(kind == 0, 0.0, (0.5 * MU_FACTOR) * (kind - 2).astype(F32))
        far = tile(everything, second, ROWS)
        middle = [far[c : c + 1] for c in range(3)]
        line = [far[3 + c : 4 + c] * factor for c in range(3)]
        high, low = [], []
        step = 32
        for start in range(0, SEG, step):
            rows = slice(start, start + step)
            r = [columns[first, c, rows, :] - middle[c] for c in range(3)]
            dist = r[0] * r[0] + CORE_SQUARED + r[1] * r[1] + r[2] * r[2]
            g = (
                columns[first, 3, rows, :] * line[0]
                + columns[first, 4, rows, :] * line[1]
                + columns[first, 5, rows, :] * line[2]
            )
            inverse = lax.rsqrt(dist)
            weight = g * inverse * (inverse * inverse)
            big, small = split(weight, 2)
            high.append(big)
            low.append(small)
        high = jnp.concatenate(high, axis=0)
        low = jnp.concatenate(low, axis=0)
        near_moments = tile(moments, first, ROWS).astype(BF16)
        far_moments = tile(moments, second, ROWS).astype(BF16)
        on_first = dot(
            jnp.concatenate([far_moments, far_moments], axis=1),
            jnp.concatenate([high, low], axis=1),
            NT,
        )
        on_second = dot(
            jnp.concatenate([near_moments, near_moments], axis=1),
            jnp.concatenate([high, low], axis=0),
            NN,
        )
        return first, second, on_first, on_second

    def body(step, carry):
        results = [one_pair(step * UNROLL + u) for u in range(UNROLL)]
        for first, second, on_first, on_second in results:
            at = pl.ds(pl.multiple_of(first * ROWS, ROWS), ROWS)
            total[at, :] = total[at, :] + on_first
            at = pl.ds(pl.multiple_of(second * ROWS, ROWS), ROWS)
            total[at, :] = total[at, :] + on_second
        return carry

    lax.fori_loop(0, (codes[16, 0] + UNROLL - 1) // UNROLL, body, 0)

    def take(ref, row, start, rows):
        return ref[pl.ds(start * ROWS + row, rows, stride=ROWS), :]

    def force(start, rows, c):
        weight = take(total, 9, start, rows)
        others = take(total, c, start, rows) + take(total, 3 + c, start, rows) + take(total, 6 + c, start, rows)
        return take(everything, c, start, rows) * weight - others

    for c in range(3):
        lanes = slice(c * SEG, (c + 1) * SEG)
        near_force[:, lanes] = force(0, blocks, c)
        for m in range(groups):
            far_force[m, :, lanes] = force(blocks + m * cap, cap, c)


def finish_kernel(
    cuts, groups, cap, blocks,
    near_force, far_force, asked, data, conn_in, stress,
    velocity,
    conn, isem, back, table, shares, chosen, pieces, base, bsend, brecv, ssend, srecv,
):
    me = lax.axis_index("cell")
    cut = lax.axis_index("cuts")
    rho = lax.rem(cut - lax.rem(me, cuts) + cuts, cuts)
    slot = lax.div(me, cuts)
    load = pltpu.make_async_copy(conn_in, conn, isem)
    load.start()
    back[...] = jnp.zeros(back.shape, F32)
    greet(me, cut, rho, groups, cuts)
    table[...] = jnp.zeros(table.shape, F32)

    def node_of(b, end):
        return conn[end : end + 1, pl.ds(pl.multiple_of(b * SEG, SEG), SEG)]

    def choose(b, carry):
        for end in range(2):
            low = jnp.broadcast_to(node_of(b, end) & (SEG - 1), (SEG, SEG))
            hit = iota((SEG, SEG), 0) == low
            chosen[b, :, end * SEG : (end + 1) * SEG] = jnp.where(hit, 1.0, 0.0).astype(BF16)
        return carry

    load.wait()
    lax.fori_loop(0, blocks, choose, 0, unroll=2)
    await_greetings(me, rho, groups, cuts)

    def reaction_copy(m, other, at):
        return pltpu.make_async_remote_copy(
            src_ref=far_force.at[m],
            dst_ref=back.at[at],
            send_sem=bsend.at[m],
            recv_sem=brecv.at[at],
            device_id=(other, cut),
            device_id_type=MESH,
        )

    for_partners(me, rho, groups, cuts, lambda m, other: reaction_copy(m, other, slot).start())

    def node_sums(first, last):
        def step(g, carry):
            at = pl.ds(pl.multiple_of(g * 8, 8), 8)
            eight = [pieces[p, at, :] for p in range(first, last)]
            for i in range(8):
                b = g * 8 + i
                left = []
                for end in range(2):
                    high = jnp.broadcast_to(node_of(b, end) >> 7, (blocks, SEG))
                    hit = iota((blocks, SEG), 0) == high
                    column = [
                        jnp.where(hit, jnp.broadcast_to(piece[i : i + 1, :], (blocks, SEG)), 0.0)
                        for piece in eight
                    ]
                    left.append(jnp.concatenate(column, axis=0).astype(BF16))
                carry = carry + dot(jnp.concatenate(left, axis=1), chosen[b], NT)
            return carry

        start = jnp.zeros(((last - first) * blocks, SEG), F32)
        sums = lax.fori_loop(0, blocks // 8, step, start)
        rows = [sums[p * blocks : (p + 1) * blocks] for p in range(last - first)]
        return [rows[p] + rows[p + 1] for p in range(0, last - first, 2)]

    def set_piece(at, value):
        for part, piece in enumerate(split(value, 2)):
            pieces[at + part] = piece.astype(F32)

    value = [data[:, c * SEG : (c + 1) * SEG] for c in range(COMPS)]
    line = value[3:6]
    burgers = burgers_of(value[6])
    sigma = [[0.5 * (stress[a, b] + stress[b, a]) for b in range(3)] for a in range(3)]
    pull = [sigma[a][0] * burgers[0] + sigma[a][1] * burgers[1] + sigma[a][2] * burgers[2] for a in range(3)]
    for c in range(3):
        u, v = (c + 1) % 3, (c + 2) % 3
        base[:, c * SEG : (c + 1) * SEG] = pull[u] * line[v] - pull[v] * line[u]
    set_piece(6, jnp.sqrt(line[0] * line[0] + line[1] * line[1] + line[2] * line[2] + CORE_SQUARED))
    drag = node_sums(6, 8)[0]
    hit = iota(asked.shape, 1) == asked[...]
    onehot = jnp.transpose(jnp.where(hit, 1.0, 0.0))[:blocks, :].astype(BF16)
    for_partners(me, rho, groups, cuts, lambda m, other: reaction_copy(m, other, m).wait_recv())
    for m in range(groups):
        table[m * 8 : m * 8 + cap, :] = back[m]
    mine = near_force[...]
    for piece in split(table[...], 3):
        mine = mine + dot(onehot, piece, NN)
    shares[cut] = mine

    def share_copy(d, at):
        return pltpu.make_async_remote_copy(
            src_ref=shares.at[cut],
            dst_ref=shares.at[at],
            send_sem=ssend.at[d - 1],
            recv_sem=srecv.at[at],
            device_id=(me, lax.rem(cut + d, cuts)),
            device_id_type=MESH,
        )

    for d in range(1, cuts):
        share_copy(d, cut).start()
    for d in range(1, cuts):
        share_copy(d, lax.rem(cut - d + cuts, cuts)).wait_recv()
    added = base[...]
    for j in range(cuts):
        added = added + shares[j]
    for c in range(3):
        set_piece(2 * c, added[:, c * SEG : (c + 1) * SEG])
    sums = node_sums(0, 6)
    for c in range(3):
        speed = sums[c] / drag
        for b in range(blocks):
            velocity[c : c + 1, b * SEG : (b + 1) * SEG] = speed[b : b + 1, :]
    for d in range(1, cuts):
        share_copy(d, cut).wait_send()
    for_partners(me, rho, groups, cuts, lambda m, other: reaction_copy(m, other, m).wait_send())


def body(cuts, node_positions, connectivity, burgers_index, applied_stress, ghost_request, pair_list):
    blocks = burgers_index.shape[0]
    owners, cap = ghost_request.shape[1:]
    groups = owners // cuts
    nodes = node_positions.shape[1]
    width = COMPS * SEG
    shape = jax.ShapeDtypeStruct
    dma = pltpu.SemaphoreType.DMA
    data, ghost, asked, codes, columns = pl.pallas_call(
        functools.partial(exchange_kernel, cuts, groups, cap, blocks),
        name="exchange",
        out_shape=(
            shape((blocks, width), F32),
            shape((groups, cap, SENT * SEG), F32),
            shape((groups * 8, SEG), I32),
            shape((24, SEG), I32),
            shape((blocks, 6, SEG, SEG), F32),
        ),
        in_specs=[ANY] * 5,
        out_specs=(VMEM,) * 5,
        scratch_shapes=[
            pltpu.VMEM((3, nodes), F32),
            pltpu.VMEM((2, nodes), I32),
            pltpu.VMEM((1, blocks), I32),
            pltpu.VMEM((cap, owners), I32),
            pltpu.VMEM(pair_list.shape, I32),
            pltpu.VMEM((2, blocks, SEG), I32),
            pltpu.VMEM((blocks * 8, SEG), F32),
            pltpu.VMEM((1, SEG), I32),
            pltpu.VMEM((owners, 1, SEG), I32),
            pltpu.VMEM((groups, 1, SEG), I32),
            pltpu.VMEM((SEG, SENT * SEG), BF16),
            pltpu.VMEM((cuts, 8, SEG), I32),
            pltpu.VMEM((groups, cap, SENT * SEG), F32),
            pltpu.VMEM((2, 8, SEG), I32),
            dma((5,)),
            dma((groups,)), dma((groups,)), dma((cuts,)), dma((cuts,)), dma((groups,)), dma((groups,)),
        ],
        compiler_params=pltpu.CompilerParams(
            collective_id=0, has_side_effects=True, vmem_limit_bytes=EXCHANGE_VMEM
        ),
    )(
        stay(node_positions),
        stay(connectivity),
        stay(burgers_index.reshape(1, blocks)),
        stay(jnp.transpose(ghost_request[0])),
        stay(pair_list),
    )
    near_force, far_force = run_pairs(codes, data, ghost, columns)
    return pl.pallas_call(
        functools.partial(finish_kernel, cuts, groups, cap, blocks),
        name="finish",
        out_shape=shape((3, nodes), F32),
        in_specs=[VMEM] * 4 + [ANY, SMEM],
        out_specs=VMEM,
        scratch_shapes=[
            pltpu.VMEM((2, nodes), I32),
            dma,
            pltpu.VMEM((groups, cap, 3 * SEG), F32),
            pltpu.VMEM((groups * 8, 3 * SEG), F32),
            pltpu.VMEM((cuts, blocks, 3 * SEG), F32),
            pltpu.VMEM((blocks, SEG, 2 * SEG), BF16),
            pltpu.VMEM((8, blocks, SEG), F32),
            pltpu.VMEM((blocks, 3 * SEG), F32),
            dma((groups,)), dma((groups,)), dma((cuts,)), dma((cuts,)),
        ],
        compiler_params=pltpu.CompilerParams(
            collective_id=1, has_side_effects=True, vmem_limit_bytes=FINISH_VMEM
        ),
    )(near_force, far_force, asked, data, stay(connectivity), applied_stress)


def run_pairs(codes, data, ghost, columns):
    groups, cap, _ = ghost.shape
    blocks = data.shape[0]
    shape = jax.ShapeDtypeStruct
    total_blocks = blocks + groups * cap
    return pl.pallas_call(
        pair_kernel,
        name="pairs",
        out_shape=(shape((blocks, 3 * SEG), F32), shape((groups, cap, 3 * SEG), F32)),
        in_specs=[SMEM, VMEM, VMEM, VMEM],
        out_specs=(VMEM,) * 2,
        scratch_shapes=[pltpu.VMEM((total_blocks * ROWS, SEG), F32)] * 3,
        compiler_params=pltpu.CompilerParams(vmem_limit_bytes=PAIRS_VMEM),
    )(codes, data, ghost, columns)


def solution(mesh):
    in_specs = (
        P(None, "cell"),
        P(None, "cell"),
        P("cell"),
        P(),
        P("cell", None, None),
        P(None, ("cell", "cuts")),
    )
    return jax.shard_map(
        functools.partial(body, mesh.shape["cuts"]),
        mesh=mesh,
        in_specs=in_specs,
        out_specs=P(None, "cell"),
        check_vma=False,
    )
```

```python
import functools

import jax
import jax.numpy as jnp
from jax import lax
from jax.experimental import pallas as pl
from jax.experimental.pallas import tpu as pltpu
from jax.sharding import PartitionSpec as P

SEG = 128
COMPS = 7
SENT = 6
FIRST_ASK = 64
ROWS = 16
UNROLL = 8
FAR_SLOTS = 120
NEAR_SLOTS = 40
FAR_ROW = 8
NEAR_ROW = 9
LIST_ROWS = 16
MIB = 1024 * 1024
EXCHANGE_VMEM = 24 * MIB
PAIRS_VMEM = 24 * MIB
FINISH_VMEM = 24 * MIB
MU_FACTOR = 10.0
CORE_SQUARED = 0.25
HALF_ROOT = 0.5**0.5
MESH = pl.DeviceIdType.MESH
F32 = jnp.float32
BF16 = jnp.bfloat16
I32 = jnp.int32
VMEM = pl.BlockSpec(memory_space=pltpu.VMEM)
SMEM = pl.BlockSpec(memory_space=pltpu.SMEM)
ANY = pl.BlockSpec(memory_space=pltpu.HBM)
NN = (((1,), (0,)), ((), ()))
NT = (((1,), (1,)), ((), ()))


def stay(value):
    return pltpu.with_memory_space_constraint(value, pltpu.HBM)


def iota(shape, axis):
    return lax.broadcasted_iota(I32, shape, axis)


def dot(a, b, dims):
    return lax.dot_general(a, b, dims, preferred_element_type=F32)


def split(value, parts):
    pieces = []
    rest = value
    for part in range(parts):
        piece = rest.astype(BF16)
        pieces.append(piece)
        if part < parts - 1:
            rest = rest - piece.astype(F32)
    return pieces


def segment_values(pos, conn, burg, links):
    blocks = links.shape[1]
    for end in range(2):
        for b in range(blocks):
            links[end, b : b + 1, :] = conn[end : end + 1, b * SEG : (b + 1) * SEG]
    low = [links[end] & (SEG - 1) for end in range(2)]
    high = [links[end] >> 7 for end in range(2)]

    def step(h, carry):
        lanes = pl.ds(pl.multiple_of(h * SEG, SEG), SEG)
        out = []
        for end in range(2):
            hit = high[end] == h
            for c in range(3):
                row = jnp.broadcast_to(pos[c : c + 1, lanes], (blocks, SEG))
                got = jnp.take_along_axis(row, low[end], axis=1)
                out.append(jnp.where(hit, got, carry[end * 3 + c]))
        return tuple(out)

    zero = jnp.zeros((blocks, SEG), F32)
    ends = lax.fori_loop(0, pos.shape[1] // SEG, step, (zero,) * 6, unroll=2)
    values = [0.5 * (ends[c] + ends[3 + c]) for c in range(3)]
    values += [ends[3 + c] - ends[c] for c in range(3)]
    diagonal = iota((blocks, blocks), 0) == iota((blocks, blocks), 1)
    kinds = jnp.broadcast_to(burg[...], (blocks, blocks)).astype(F32)
    kind = jnp.sum(jnp.where(diagonal, kinds, 0.0), axis=1, keepdims=True)
    values.append(jnp.broadcast_to(kind, (blocks, SEG)))
    return values


def burgers_of(kind):
    return [HALF_ROOT * value for value in whole_burgers(kind)]


def fill_requests(req, burg, wide, rows):
    cap, owners = req.shape
    blocks = burg.shape[1]
    wide[...] = jnp.zeros(wide.shape, I32)
    wide[:, 0:blocks] = burg[...]
    message = jnp.broadcast_to(wide[...], (owners, SEG))
    lane = iota((owners, SEG), 1)
    diagonal = iota((owners, owners), 0) == iota((owners, owners), 1)
    for t in range(cap):
        row = jnp.broadcast_to(req[t : t + 1, :], (owners, owners)).astype(F32)
        column = jnp.sum(jnp.where(diagonal, row, 0.0), axis=1, keepdims=True)
        column = jnp.broadcast_to(column, (owners, SEG)).astype(I32)
        message = jnp.where(lane == FIRST_ASK + t, column, message)
    for o in range(owners):
        rows[o] = message[o : o + 1, :]


def kind_table(own, heard, said, cap):
    groups = heard.shape[0]
    lane = iota((groups, SEG), 1)
    blocks = FIRST_ASK // 2
    wanted = jnp.zeros((groups, SEG), I32)
    for t in range(cap):
        column = jnp.broadcast_to(said[:, FIRST_ASK + t : FIRST_ASK + t + 1], (groups, SEG))
        wanted = jnp.where((lane & 3) == t, column, wanted)
    found = jnp.take_along_axis(heard, jnp.maximum(wanted, 0), axis=1)
    here = (lane >= blocks) & (((lane - blocks) >> 2) == iota((groups, SEG), 0))
    ghosts = jnp.sum(jnp.where(here, found, 0).astype(F32), axis=0, keepdims=True)
    return jnp.where(iota((1, SEG), 1) < blocks, own.astype(F32), ghosts)


def whole_burgers(kind):
    odd = jnp.where((kind == 1.0) | (kind == 3.0) | (kind == 5.0), -1.0, 1.0)
    return [
        jnp.where(kind < 4.0, 1.0, 0.0),
        jnp.where(kind < 2.0, odd, jnp.where(kind < 4.0, 0.0, 1.0)),
        jnp.where(kind < 2.0, 0.0, odd),
    ]


def spread_columns(flat, columns):
    blocks = columns.shape[0]

    def step(block, carry):
        tall = jnp.transpose(flat[pl.ds(pl.multiple_of(block * 8, 8), 8), :])
        for c in range(6):
            columns[block, c] = jnp.broadcast_to(tall[:, c : c + 1], (SEG, SEG))
        return carry

    lax.fori_loop(0, blocks, step, 0, unroll=2)


def for_partners(me, rho, groups, cuts, run):
    def step(i, carry):
        hop = jnp.where(lax.rem(i, 2) == 0, groups // 2 + lax.div(i, 2), groups // 2 - lax.div(i + 1, 2))
        m = lax.rem(lax.div(me, cuts) + hop, groups)
        other = m * cuts + rho

        @pl.when(other != me)
        def _():
            run(m, other)

        return carry

    lax.fori_loop(0, groups, step, 0)


def greet(me, cut, rho, groups, cuts):
    barrier = pltpu.get_barrier_semaphore()

    def signal(m, other):
        pl.semaphore_signal(barrier, inc=1, device_id=(other, cut), device_id_type=MESH)

    for_partners(me, rho, groups, cuts, signal)
    for d in range(1, cuts):
        peer = lax.rem(cut + d, cuts)
        pl.semaphore_signal(barrier, inc=1, device_id=(me, peer), device_id_type=MESH)


def await_greetings(me, rho, groups, cuts):
    own = jnp.where(rho == lax.rem(me, cuts), 1, 0)
    pl.semaphore_wait(pltpu.get_barrier_semaphore(), groups + cuts - 1 - own)


def prefix(flags):
    rows, lanes = flags.shape
    value = jnp.where(flags, 1.0, 0.0).astype(F32)
    coded = value.astype(BF16)
    upper = jnp.where(iota((lanes, lanes), 0) <= iota((lanes, lanes), 1), 1.0, 0.0).astype(BF16)
    along = dot(coded, upper, NN)
    ones = jnp.ones((lanes, lanes), BF16)
    totals = dot(coded, ones, NN)
    row = iota((rows, lanes), 0)
    offset = jnp.zeros((rows, lanes), F32)
    for r in range(rows - 1):
        offset = offset + jnp.where(row > r, jnp.broadcast_to(totals[r : r + 1, :], (rows, lanes)), 0.0)
    return (along - value + offset).astype(I32)


def count(flags):
    value = jnp.where(flags, 1.0, 0.0).astype(F32)
    return jnp.sum(jnp.sum(value, axis=1, keepdims=True), axis=0, keepdims=True).astype(I32)


def share_pairs(first, second, own_row, kinds, me, cut, cuts, cap, blocks):
    used = first >= 0
    ghost = second >= blocks
    slot = jnp.maximum(second - blocks, 0)
    owner = slot >> 2
    part = slot & 3
    own = ghost & (owner == me)
    far = ghost & (owner != me)
    wanted = jnp.zeros_like(second)
    for t in range(cap):
        row = jnp.broadcast_to(own_row[:, FIRST_ASK + t : FIRST_ASK + t + 1], second.shape)
        wanted = jnp.where(part == t, row, wanted)
    near_block = jnp.where(own, wanted, second)
    block = jnp.where(far, blocks + (owner >> 2) * cap + part, near_block)
    half = jnp.logical_and(jnp.logical_not(far), block == first)
    table = jnp.broadcast_to(kinds, first.shape)
    one = whole_burgers(jnp.take_along_axis(table, jnp.maximum(first, 0), axis=1))
    two = whole_burgers(jnp.take_along_axis(table, jnp.maximum(block, 0), axis=1))
    match = one[0] * two[0] + one[1] * two[1] + one[2] * two[2]
    match = jnp.where(half, 0.5 * match, match).astype(I32)
    alive = used & (match != 0)
    place = (owner + me) & 3
    mine_far = alive & far & (place == cut)
    near = alive & jnp.logical_not(far)
    part_size = (count(near) + cuts - 1) >> 2
    rank = prefix(near) - cut * part_size
    mine_near = near & (rank >= 0) & (rank < part_size)
    far_spot = prefix(mine_far)
    fits = (mine_far & (far_spot < FAR_SLOTS)) | (mine_near & (rank < NEAR_SLOTS))
    mine = mine_far | mine_near
    rest = mine & jnp.logical_not(fits)
    lanes = first.shape[1]
    spot = jnp.where(far, FAR_ROW * lanes + far_spot, NEAR_ROW * lanes + rank)
    spot = jnp.where(fits, spot, prefix(rest))
    first_code = jnp.where(mine, first + 32 * (match + 2), 0).astype(F32)
    second_code = jnp.where(mine, block, 0).astype(F32)
    rows = first.shape[0]
    codes = jnp.zeros((2 * LIST_ROWS, lanes), F32)
    for r in range(rows):
        at = spot[r : r + 1, :]
        hit = iota((LIST_ROWS, lanes), 0) == jnp.broadcast_to(at >> 7, (LIST_ROWS, lanes))
        left = jnp.concatenate(
            [
                jnp.where(hit, jnp.broadcast_to(first_code[r : r + 1, :], (LIST_ROWS, lanes)), 0.0),
                jnp.where(hit, jnp.broadcast_to(second_code[r : r + 1, :], (LIST_ROWS, lanes)), 0.0),
            ],
            axis=0,
        ).astype(BF16)
        chosen = iota((lanes, lanes), 0) == jnp.broadcast_to(at & (lanes - 1), (lanes, lanes))
        codes = codes + dot(left, jnp.where(chosen, 1.0, 0.0).astype(BF16), NT)
    return codes.astype(I32), count(rest)


def exchange_kernel(
    cuts, groups, cap, blocks,
    pos_in, conn_in, burg_in, req_in, pairs_in,
    data, ghost, asked, codes, extra, columns,
    pos, conn, burg, req, pairs, links, flat, wide, rows, heard, table, plist, stage, ordered,
    isem, rsend, rrecv, psend, precv, bsend, brecv,
):
    me = lax.axis_index("cell")
    cut = lax.axis_index("cuts")
    rho = lax.rem(cut - lax.rem(me, cuts) + cuts, cuts)
    slot = lax.div(me, cuts)
    inputs = [(req_in, req), (burg_in, burg), (pairs_in, pairs), (conn_in, conn), (pos_in, pos)]
    loads = [pltpu.make_async_copy(src, dst, isem.at[i]) for i, (src, dst) in enumerate(inputs)]
    for load in loads:
        load.start()
    heard[...] = jnp.full(heard.shape, -1, I32)
    ghost[...] = jnp.zeros(ghost.shape, F32)
    greet(me, cut, rho, groups, cuts)
    for load in loads[:3]:
        load.wait()
    fill_requests(req, burg, wide, rows)
    plist[cut] = jnp.zeros(plist.shape[1:], I32)
    for e in range(2):
        for r in range(2):
            plist[cut, 2 * e + r : 2 * e + r + 1, :] = pairs[e : e + 1, r * SEG : (r + 1) * SEG]
    await_greetings(me, rho, groups, cuts)

    def request_copy(m, other, at):
        return pltpu.make_async_remote_copy(
            src_ref=rows.at[other],
            dst_ref=heard.at[at],
            send_sem=rsend.at[m],
            recv_sem=rrecv.at[at],
            device_id=(other, cut),
            device_id_type=MESH,
        )

    def pair_copy(d, at):
        return pltpu.make_async_remote_copy(
            src_ref=plist.at[cut],
            dst_ref=plist.at[at],
            send_sem=psend.at[d - 1],
            recv_sem=precv.at[at],
            device_id=(me, lax.rem(cut + d, cuts)),
            device_id_type=MESH,
        )

    for_partners(me, rho, groups, cuts, lambda m, other: request_copy(m, other, slot).start())
    for d in range(1, cuts):
        pair_copy(d, cut).start()
    for load in loads[3:]:
        load.wait()
    values = segment_values(pos, conn, burg, links)
    table[...] = jnp.zeros(table.shape, table.dtype)
    for c in range(COMPS):
        lanes = slice(c * SEG, (c + 1) * SEG)
        data[:, lanes] = values[c]
        if c == SENT:
            continue
        flat[pl.ds(c, blocks, stride=8), :] = values[c]
        for part, piece in enumerate(split(values[c], 3)):
            table[part * blocks : (part + 1) * blocks, lanes] = piece
    for_partners(me, rho, groups, cuts, lambda m, other: request_copy(m, other, m).wait_recv())
    hear = jnp.concatenate([heard[m] for m in range(groups)], axis=0)
    asked[...] = jnp.full(asked.shape, -1, I32)
    for t in range(cap):
        column = hear[:, FIRST_ASK + t : FIRST_ASK + t + 1]
        asked[pl.ds(t, groups, stride=8), :] = jnp.broadcast_to(column, (groups, SEG))

    lane = iota(asked.shape, 1)
    hit = ((lane & (blocks - 1)) == asked[...]) & (lane < 3 * blocks)
    onehot = jnp.where(hit, 1.0, 0.0).astype(BF16)
    for c in range(SENT):
        lanes = slice(c * SEG, (c + 1) * SEG)
        got = dot(onehot, table[:, lanes], NN)
        for m in range(groups):
            stage[m, :, lanes] = got[m * 8 : m * 8 + cap, :]

    def block_copy(m, other, at):
        return pltpu.make_async_remote_copy(
            src_ref=stage.at[m],
            dst_ref=ghost.at[at],
            send_sem=bsend.at[m],
            recv_sem=brecv.at[at],
            device_id=(other, cut),
            device_id_type=MESH,
        )

    for_partners(me, rho, groups, cuts, lambda m, other: block_copy(m, other, slot).start())
    spread_columns(flat, columns)
    for d in range(1, cuts):
        pair_copy(d, lax.rem(cut - d + cuts, cuts)).wait_recv()
    for j in range(cuts):
        ordered[0, 2 * j : 2 * j + 2, :] = plist[j, 0:2, :]
        ordered[1, 2 * j : 2 * j + 2, :] = plist[j, 2:4, :]
    said = jnp.concatenate([rows[m * cuts + rho] for m in range(groups)], axis=0)
    own_row = rows[me]
    kinds = kind_table(own_row, hear, said, cap)
    listed, total = share_pairs(ordered[0], ordered[1], own_row, kinds, me, cut, cuts, cap, blocks)
    codes[...] = listed
    extra[...] = jnp.broadcast_to(total, extra.shape)
    for_partners(me, rho, groups, cuts, lambda m, other: block_copy(m, other, m).wait_recv())
    for_partners(me, rho, groups, cuts, lambda m, other: block_copy(m, other, m).wait_send())
    for_partners(me, rho, groups, cuts, lambda m, other: request_copy(m, other, m).wait_send())
    for d in range(1, cuts):
        pair_copy(d, cut).wait_send()


def fill_tables(data, ghost, everything, moments):
    blocks = data.shape[0]
    groups, cap, _ = ghost.shape

    def fill(target, row, value, start):
        target[start : start + value.shape[0], row, :] = value

    def fill_block(values, start):
        for c, value in enumerate(values):
            fill(everything, c, value, start)
        for c in range(3):
            for part, piece in enumerate(split(values[c], 3)):
                fill(moments, part * 3 + c, piece.astype(F32), start)

    moments[...] = jnp.where(iota(moments.shape, 1) == 9, 1.0, 0.0)
    fill_block([data[:, c * SEG : (c + 1) * SEG] for c in range(SENT)], 0)
    for m in range(groups):
        fill_block([ghost[m, :, c * SEG : (c + 1) * SEG] for c in range(SENT)], blocks + m * cap)


def one_pair(code, second, everything, moments, columns):
    first = code & 31
    kind = code >> 5
    factor = jnp.where(kind == 0, 0.0, (0.5 * MU_FACTOR) * (kind - 2).astype(F32))
    far = everything[second]
    middle = [far[c : c + 1] for c in range(3)]
    line = [far[3 + c : 4 + c] * factor for c in range(3)]
    high, low = [], []
    step = 32
    for start in range(0, SEG, step):
        rows = slice(start, start + step)
        r = [columns[first, c, rows, :] - middle[c] for c in range(3)]
        dist = r[0] * r[0] + CORE_SQUARED + r[1] * r[1] + r[2] * r[2]
        g = (
            columns[first, 3, rows, :] * line[0]
            + columns[first, 4, rows, :] * line[1]
            + columns[first, 5, rows, :] * line[2]
        )
        inverse = lax.rsqrt(dist)
        big, small = split(g * inverse * (inverse * inverse), 2)
        high.append(big)
        low.append(small)
    high = jnp.concatenate(high, axis=0)
    low = jnp.concatenate(low, axis=0)
    near_moments = moments[first].astype(BF16)
    far_moments = moments[second].astype(BF16)
    on_first = dot(
        jnp.concatenate([far_moments, far_moments], axis=1),
        jnp.concatenate([high, low], axis=1),
        NT,
    )
    on_second = dot(
        jnp.concatenate([near_moments, near_moments], axis=1),
        jnp.concatenate([high, low], axis=0),
        NN,
    )
    return first, on_first, on_second


def extra_kernel(extra, codes_in, data, ghost, columns, near_force, far_force, codes, sem, everything, moments, total):
    blocks = data.shape[0]
    groups, cap, _ = ghost.shape
    near_force[...] = jnp.zeros(near_force.shape, F32)
    far_force[...] = jnp.zeros(far_force.shape, F32)

    @pl.when(extra[0, 0] > 0)
    def _():
        load = pltpu.make_async_copy(codes_in, codes, sem)
        load.start()
        total[...] = jnp.zeros(total.shape, F32)
        fill_tables(data, ghost, everything, moments)
        load.wait()

        def body(index, carry):
            code = codes[index >> 7, index & (SEG - 1)]
            second = codes[LIST_ROWS + (index >> 7), index & (SEG - 1)]
            first, on_first, on_second = one_pair(code, second, everything, moments, columns)
            total[first] = total[first] + on_first
            total[second] = total[second] + on_second
            return carry

        lax.fori_loop(0, extra[0, 0], body, 0)

        def take(ref, row, start, rows):
            return ref[start : start + rows, row, :]

        def force(start, rows, c):
            weight = take(total, 9, start, rows)
            others = sum(take(total, 3 * part + c, start, rows) for part in range(3))
            return take(everything, c, start, rows) * weight - others

        for c in range(3):
            lanes = slice(c * SEG, (c + 1) * SEG)
            near_force[:, lanes] = force(0, blocks, c)
            for m in range(groups):
                far_force[m, :, lanes] = force(blocks + m * cap, cap, c)


def finish_kernel(
    cuts, groups, cap, blocks,
    near_extra, far_extra, codes_in, asked, data, ghost, columns, conn_in, stress,
    velocity,
    conn, isem, codes, csem, everything, moments, results, sums_of, near_force, far_force, back, table, shares, chosen, length, base, bsend, brecv, ssend, srecv,
):
    me = lax.axis_index("cell")
    cut = lax.axis_index("cuts")
    rho = lax.rem(cut - lax.rem(me, cuts) + cuts, cuts)
    slot = lax.div(me, cuts)
    load = pltpu.make_async_copy(conn_in, conn, isem)
    load.start()
    load_codes = pltpu.make_async_copy(codes_in, codes, csem)
    load_codes.start()
    back[...] = jnp.zeros(back.shape, F32)
    greet(me, cut, rho, groups, cuts)
    table[...] = jnp.zeros(table.shape, F32)
    fill_tables(data, ghost, everything, moments)
    load_codes.wait()

    def run_list(row, slots):
        def step(i, carry):
            for u in range(UNROLL):
                at = i * UNROLL + u
                code = codes[row, at]
                second = codes[LIST_ROWS + row, at]
                _, on_first, on_second = one_pair(code, second, everything, moments, columns)
                results[0, at] = on_first
                results[1, at] = on_second
            return carry

        lax.fori_loop(0, slots // UNROLL, step, 0)

    def collect(side, slots):
        def row(r):
            return results[side, 0:slots, r, :]

        for c in range(3):
            sums_of[0:slots, c * SEG : (c + 1) * SEG] = row(c) + row(3 + c) + row(6 + c)
        sums_of[0:slots, 3 * SEG : 4 * SEG] = row(9)
        return split(sums_of[...], 3)

    def near_collect(side):
        sums_of[...] = jnp.zeros(sums_of.shape, F32)
        return collect(side, NEAR_SLOTS)

    def scatter(at, start, size, pieces):
        hit = iota((size, SEG), 0) + start == jnp.broadcast_to(at, (size, SEG))
        onehot = jnp.where(hit, 1.0, 0.0).astype(BF16)
        return sum(dot(onehot, piece, NN) for piece in pieces)

    def middle_of(c, start, size):
        return everything[start : start + size, c, :]

    sums_of[...] = jnp.zeros(sums_of.shape, F32)
    run_list(FAR_ROW, FAR_SLOTS)
    ghosts = groups * cap
    second_at = codes_in[LIST_ROWS + FAR_ROW : LIST_ROWS + FAR_ROW + 1, :]
    far_sums = scatter(second_at, blocks, ghosts, collect(1, FAR_SLOTS))
    for c in range(3):
        lanes = slice(c * SEG, (c + 1) * SEG)
        force = middle_of(c, blocks, ghosts) * far_sums[:, 3 * SEG :] - far_sums[:, lanes]
        for m in range(groups):
            far_force[m, :, lanes] = force[m * cap : (m + 1) * cap, :] + far_extra[m, :, lanes]

    def node_of(b, end):
        return conn[end : end + 1, pl.ds(pl.multiple_of(b * SEG, SEG), SEG)]

    def choose(b, carry):
        for end in range(2):
            low = jnp.broadcast_to(node_of(b, end) & (SEG - 1), (SEG, SEG))
            hit = iota((SEG, SEG), 0) == low
            chosen[b, :, end * SEG : (end + 1) * SEG] = jnp.where(hit, 1.0, 0.0).astype(BF16)
        return carry

    await_greetings(me, rho, groups, cuts)

    def reaction_copy(m, other, at):
        return pltpu.make_async_remote_copy(
            src_ref=far_force.at[m],
            dst_ref=back.at[at],
            send_sem=bsend.at[m],
            recv_sem=brecv.at[at],
            device_id=(other, cut),
            device_id_type=MESH,
        )

    for_partners(me, rho, groups, cuts, lambda m, other: reaction_copy(m, other, slot).start())
    first_at = codes_in[FAR_ROW : FAR_ROW + 1, :] & 31
    near_sums = scatter(first_at, 0, blocks, collect(0, FAR_SLOTS))
    run_list(NEAR_ROW, NEAR_SLOTS)
    first_at = codes_in[NEAR_ROW : NEAR_ROW + 1, :] & 31
    near_sums = near_sums + scatter(first_at, 0, blocks, near_collect(0))
    second_at = codes_in[LIST_ROWS + NEAR_ROW : LIST_ROWS + NEAR_ROW + 1, :]
    near_sums = near_sums + scatter(second_at, 0, blocks, near_collect(1))
    for c in range(3):
        lanes = slice(c * SEG, (c + 1) * SEG)
        force = middle_of(c, 0, blocks) * near_sums[:, 3 * SEG :] - near_sums[:, lanes]
        near_force[:, lanes] = force + near_extra[:, lanes]
    load.wait()
    lax.fori_loop(0, blocks, choose, 0, unroll=2)

    def node_step(g, eight, carry):
        for i in range(8):
            b = g * 8 + i
            left = []
            for end in range(2):
                high = jnp.broadcast_to(node_of(b, end) >> 7, (blocks, SEG))
                hit = iota((blocks, SEG), 0) == high
                column = [
                    jnp.where(hit, jnp.broadcast_to(piece[i : i + 1, :], (blocks, SEG)), 0.0)
                    for piece in eight
                ]
                left.append(jnp.concatenate(column, axis=0).astype(BF16))
            carry = carry + dot(jnp.concatenate(left, axis=1), chosen[b], NT)
        return carry

    def node_sums(fetch, parts):
        def step(g, carry):
            pieces = [piece.astype(F32) for value in fetch(g) for piece in split(value, 2)]
            return node_step(g, pieces, carry)

        sums = lax.fori_loop(0, blocks // 8, step, jnp.zeros((2 * parts * blocks, SEG), F32))
        rows = [sums[p * blocks : (p + 1) * blocks] for p in range(2 * parts)]
        return [rows[p] + rows[p + 1] for p in range(0, 2 * parts, 2)]

    def eight_rows(g):
        return pl.ds(pl.multiple_of(g * 8, 8), 8)

    value = [data[:, c * SEG : (c + 1) * SEG] for c in range(COMPS)]
    line = value[3:6]
    burgers = burgers_of(value[6])
    sigma = [[0.5 * (stress[a, b] + stress[b, a]) for b in range(3)] for a in range(3)]
    pull = [sigma[a][0] * burgers[0] + sigma[a][1] * burgers[1] + sigma[a][2] * burgers[2] for a in range(3)]
    for c in range(3):
        u, v = (c + 1) % 3, (c + 2) % 3
        base[:, c * SEG : (c + 1) * SEG] = pull[u] * line[v] - pull[v] * line[u]
    length[...] = jnp.sqrt(line[0] * line[0] + line[1] * line[1] + line[2] * line[2] + CORE_SQUARED)
    drag = node_sums(lambda g: [length[eight_rows(g), :]], 1)[0]
    hit = iota(asked.shape, 1) == asked[...]
    onehot = jnp.transpose(jnp.where(hit, 1.0, 0.0))[:blocks, :].astype(BF16)
    for_partners(me, rho, groups, cuts, lambda m, other: reaction_copy(m, other, m).wait_recv())
    for m in range(groups):
        table[m * 8 : m * 8 + cap, :] = back[m]
    mine = near_force[...]
    for piece in split(table[...], 3):
        mine = mine + dot(onehot, piece, NN)
    shares[cut] = mine

    def share_copy(d, at, g):
        return pltpu.make_async_remote_copy(
            src_ref=shares.at[cut, eight_rows(g)],
            dst_ref=shares.at[at, eight_rows(g)],
            send_sem=ssend.at[d - 1, g],
            recv_sem=srecv.at[at, g],
            device_id=(me, lax.rem(cut + d, cuts)),
            device_id_type=MESH,
        )

    for g in range(blocks // 8):
        for d in range(1, cuts):
            share_copy(d, cut, g).start()

    def added(g):
        for d in range(1, cuts):
            share_copy(d, lax.rem(cut - d + cuts, cuts), g).wait_recv()
        value = base[eight_rows(g), :]
        for j in range(cuts):
            value = value + shares[j, eight_rows(g), :]
        return [value[:, c * SEG : (c + 1) * SEG] for c in range(3)]

    sums = node_sums(added, 3)
    for c in range(3):
        speed = sums[c] / drag
        for b in range(blocks):
            velocity[c : c + 1, b * SEG : (b + 1) * SEG] = speed[b : b + 1, :]
    for g in range(blocks // 8):
        for d in range(1, cuts):
            share_copy(d, cut, g).wait_send()
    for_partners(me, rho, groups, cuts, lambda m, other: reaction_copy(m, other, m).wait_send())


def body(cuts, node_positions, connectivity, burgers_index, applied_stress, ghost_request, pair_list):
    blocks = burgers_index.shape[0]
    owners, cap = ghost_request.shape[1:]
    groups = owners // cuts
    nodes = node_positions.shape[1]
    width = COMPS * SEG
    shape = jax.ShapeDtypeStruct
    dma = pltpu.SemaphoreType.DMA
    data, ghost, asked, codes, extra, columns = pl.pallas_call(
        functools.partial(exchange_kernel, cuts, groups, cap, blocks),
        name="exchange",
        out_shape=(
            shape((blocks, width), F32),
            shape((groups, cap, SENT * SEG), F32),
            shape((groups * 8, SEG), I32),
            shape((2 * LIST_ROWS, SEG), I32),
            shape((1, SEG), I32),
            shape((blocks, 6, SEG, SEG), F32),
        ),
        in_specs=[ANY] * 5,
        out_specs=(VMEM,) * 6,
        scratch_shapes=[
            pltpu.VMEM((3, nodes), F32),
            pltpu.VMEM((2, nodes), I32),
            pltpu.VMEM((1, blocks), I32),
            pltpu.VMEM((cap, owners), I32),
            pltpu.VMEM(pair_list.shape, I32),
            pltpu.VMEM((2, blocks, SEG), I32),
            pltpu.VMEM((blocks * 8, SEG), F32),
            pltpu.VMEM((1, SEG), I32),
            pltpu.VMEM((owners, 1, SEG), I32),
            pltpu.VMEM((groups, 1, SEG), I32),
            pltpu.VMEM((SEG, SENT * SEG), BF16),
            pltpu.VMEM((cuts, 8, SEG), I32),
            pltpu.VMEM((groups, cap, SENT * SEG), F32),
            pltpu.VMEM((2, 8, SEG), I32),
            dma((5,)),
            dma((groups,)), dma((groups,)), dma((cuts,)), dma((cuts,)), dma((groups,)), dma((groups,)),
        ],
        compiler_params=pltpu.CompilerParams(
            collective_id=0, has_side_effects=True, vmem_limit_bytes=EXCHANGE_VMEM
        ),
    )(
        stay(node_positions),
        stay(connectivity),
        stay(burgers_index.reshape(1, blocks)),
        stay(jnp.transpose(ghost_request[0])),
        stay(pair_list),
    )
    total_blocks = blocks + groups * cap
    tables = [pltpu.VMEM((total_blocks, ROWS, SEG), F32)] * 2
    list_scratch = [pltpu.SMEM((2 * LIST_ROWS, SEG), I32), dma]
    near_extra, far_extra = pl.pallas_call(
        extra_kernel,
        name="extra",
        out_shape=(shape((blocks, 3 * SEG), F32), shape((groups, cap, 3 * SEG), F32)),
        in_specs=[SMEM, VMEM, VMEM, VMEM, VMEM],
        out_specs=(VMEM,) * 2,
        scratch_shapes=list_scratch + tables + [pltpu.VMEM((total_blocks, ROWS, SEG), F32)],
        compiler_params=pltpu.CompilerParams(vmem_limit_bytes=PAIRS_VMEM),
    )(extra, codes, data, ghost, columns)
    return pl.pallas_call(
        functools.partial(finish_kernel, cuts, groups, cap, blocks),
        name="finish",
        out_shape=shape((3, nodes), F32),
        in_specs=[VMEM] * 7 + [ANY, SMEM],
        out_specs=VMEM,
        scratch_shapes=[
            pltpu.VMEM((2, nodes), I32),
            dma,
            *list_scratch,
            *tables,
            pltpu.VMEM((2, SEG, ROWS, SEG), F32),
            pltpu.VMEM((SEG, 4 * SEG), F32),
            pltpu.VMEM((blocks, 3 * SEG), F32),
            pltpu.VMEM((groups, cap, 3 * SEG), F32),
            pltpu.VMEM((groups, cap, 3 * SEG), F32),
            pltpu.VMEM((groups * 8, 3 * SEG), F32),
            pltpu.VMEM((cuts, blocks, 3 * SEG), F32),
            pltpu.VMEM((blocks, SEG, 2 * SEG), BF16),
            pltpu.VMEM((blocks, SEG), F32),
            pltpu.VMEM((blocks, 3 * SEG), F32),
            dma((groups,)), dma((groups,)), dma((cuts, blocks // 8)), dma((cuts, blocks // 8)),
        ],
        compiler_params=pltpu.CompilerParams(
            collective_id=1, has_side_effects=True, vmem_limit_bytes=FINISH_VMEM
        ),
    )(near_extra, far_extra, codes, asked, data, ghost, columns, stay(connectivity), applied_stress)


def solution(mesh):
    in_specs = (
        P(None, "cell"),
        P(None, "cell"),
        P("cell"),
        P(),
        P("cell", None, None),
        P(None, ("cell", "cuts")),
    )
    return jax.shard_map(
        functools.partial(body, mesh.shape["cuts"]),
        mesh=mesh,
        in_specs=in_specs,
        out_specs=P(None, "cell"),
        check_vma=False,
    )
```

```python
import functools

import jax
import jax.numpy as jnp
from jax import lax
from jax.experimental import pallas as pl
from jax.experimental.pallas import tpu as pltpu
from jax.sharding import PartitionSpec as P

SEG = 128
COMPS = 7
SENT = 6
FIRST_ASK = 64
ROWS = 16
FAR_STEP = 40
NEAR_STEP = 40
FAR_SLOTS = 120
NEAR_SLOTS = 40
FAR_ROW = 8
NEAR_ROW = 9
LIST_ROWS = 16
MIB = 1024 * 1024
EXCHANGE_VMEM = 24 * MIB
PAIRS_VMEM = 24 * MIB
FINISH_VMEM = 24 * MIB
MU_FACTOR = 10.0
CORE_SQUARED = 0.25
HALF_ROOT = 0.5**0.5
MESH = pl.DeviceIdType.MESH
F32 = jnp.float32
BF16 = jnp.bfloat16
I32 = jnp.int32
VMEM = pl.BlockSpec(memory_space=pltpu.VMEM)
SMEM = pl.BlockSpec(memory_space=pltpu.SMEM)
ANY = pl.BlockSpec(memory_space=pltpu.HBM)
NN = (((1,), (0,)), ((), ()))
NT = (((1,), (1,)), ((), ()))


def stay(value):
    return pltpu.with_memory_space_constraint(value, pltpu.HBM)


def iota(shape, axis):
    return lax.broadcasted_iota(I32, shape, axis)


def dot(a, b, dims):
    return lax.dot_general(a, b, dims, preferred_element_type=F32)


def split(value, parts):
    pieces = []
    rest = value
    for part in range(parts):
        piece = rest.astype(BF16)
        pieces.append(piece)
        if part < parts - 1:
            rest = rest - piece.astype(F32)
    return pieces


def segment_values(pos, conn, burg, links):
    blocks = links.shape[1]
    for end in range(2):
        for b in range(blocks):
            links[end, b : b + 1, :] = conn[end : end + 1, b * SEG : (b + 1) * SEG]
    low = [links[end] & (SEG - 1) for end in range(2)]
    high = [links[end] >> 7 for end in range(2)]

    def step(h, carry):
        lanes = pl.ds(pl.multiple_of(h * SEG, SEG), SEG)
        out = []
        for end in range(2):
            hit = high[end] == h
            for c in range(3):
                row = jnp.broadcast_to(pos[c : c + 1, lanes], (blocks, SEG))
                got = jnp.take_along_axis(row, low[end], axis=1)
                out.append(jnp.where(hit, got, carry[end * 3 + c]))
        return tuple(out)

    zero = jnp.zeros((blocks, SEG), F32)
    ends = lax.fori_loop(0, pos.shape[1] // SEG, step, (zero,) * 6, unroll=2)
    values = [0.5 * (ends[c] + ends[3 + c]) for c in range(3)]
    values += [ends[3 + c] - ends[c] for c in range(3)]
    diagonal = iota((blocks, blocks), 0) == iota((blocks, blocks), 1)
    kinds = jnp.broadcast_to(burg[...], (blocks, blocks)).astype(F32)
    kind = jnp.sum(jnp.where(diagonal, kinds, 0.0), axis=1, keepdims=True)
    values.append(jnp.broadcast_to(kind, (blocks, SEG)))
    return values


def burgers_of(kind):
    return [HALF_ROOT * value for value in whole_burgers(kind)]


def fill_requests(req, burg, wide, rows):
    cap, owners = req.shape
    blocks = burg.shape[1]
    wide[...] = jnp.zeros(wide.shape, I32)
    wide[:, 0:blocks] = burg[...]
    message = jnp.broadcast_to(wide[...], (owners, SEG))
    lane = iota((owners, SEG), 1)
    diagonal = iota((owners, owners), 0) == iota((owners, owners), 1)
    for t in range(cap):
        row = jnp.broadcast_to(req[t : t + 1, :], (owners, owners)).astype(F32)
        column = jnp.sum(jnp.where(diagonal, row, 0.0), axis=1, keepdims=True)
        column = jnp.broadcast_to(column, (owners, SEG)).astype(I32)
        message = jnp.where(lane == FIRST_ASK + t, column, message)
    for o in range(owners):
        rows[o] = message[o : o + 1, :]


def kind_table(own, heard, said, cap):
    groups = heard.shape[0]
    lane = iota((groups, SEG), 1)
    blocks = FIRST_ASK // 2
    wanted = jnp.zeros((groups, SEG), I32)
    for t in range(cap):
        column = jnp.broadcast_to(said[:, FIRST_ASK + t : FIRST_ASK + t + 1], (groups, SEG))
        wanted = jnp.where((lane & 3) == t, column, wanted)
    found = jnp.take_along_axis(heard, jnp.maximum(wanted, 0), axis=1)
    here = (lane >= blocks) & (((lane - blocks) >> 2) == iota((groups, SEG), 0))
    ghosts = jnp.sum(jnp.where(here, found, 0).astype(F32), axis=0, keepdims=True)
    return jnp.where(iota((1, SEG), 1) < blocks, own.astype(F32), ghosts)


def whole_burgers(kind):
    odd = jnp.where((kind == 1.0) | (kind == 3.0) | (kind == 5.0), -1.0, 1.0)
    return [
        jnp.where(kind < 4.0, 1.0, 0.0),
        jnp.where(kind < 2.0, odd, jnp.where(kind < 4.0, 0.0, 1.0)),
        jnp.where(kind < 2.0, 0.0, odd),
    ]


def spread_columns(flat, columns):
    blocks = columns.shape[0]

    def step(block, carry):
        tall = jnp.transpose(flat[pl.ds(pl.multiple_of(block * 8, 8), 8), :])
        for c in range(6):
            columns[block, c] = jnp.broadcast_to(tall[:, c : c + 1], (SEG, SEG))
        return carry

    lax.fori_loop(0, blocks, step, 0, unroll=2)


def for_partners(me, rho, groups, cuts, run):
    def step(i, carry):
        hop = jnp.where(lax.rem(i, 2) == 0, groups // 2 + lax.div(i, 2), groups // 2 - lax.div(i + 1, 2))
        m = lax.rem(lax.div(me, cuts) + hop, groups)
        other = m * cuts + rho

        @pl.when(other != me)
        def _():
            run(m, other)

        return carry

    lax.fori_loop(0, groups, step, 0)


def greet(me, cut, rho, groups, cuts):
    barrier = pltpu.get_barrier_semaphore()

    def signal(m, other):
        pl.semaphore_signal(barrier, inc=1, device_id=(other, cut), device_id_type=MESH)

    for_partners(me, rho, groups, cuts, signal)
    for d in range(1, cuts):
        peer = lax.rem(cut + d, cuts)
        pl.semaphore_signal(barrier, inc=1, device_id=(me, peer), device_id_type=MESH)


def await_greetings(me, rho, groups, cuts):
    own = jnp.where(rho == lax.rem(me, cuts), 1, 0)
    pl.semaphore_wait(pltpu.get_barrier_semaphore(), groups + cuts - 1 - own)


def prefix(flags):
    rows, lanes = flags.shape
    value = jnp.where(flags, 1.0, 0.0).astype(F32)
    coded = value.astype(BF16)
    upper = jnp.where(iota((lanes, lanes), 0) <= iota((lanes, lanes), 1), 1.0, 0.0).astype(BF16)
    along = dot(coded, upper, NN)
    ones = jnp.ones((lanes, lanes), BF16)
    totals = dot(coded, ones, NN)
    row = iota((rows, lanes), 0)
    offset = jnp.zeros((rows, lanes), F32)
    for r in range(rows - 1):
        offset = offset + jnp.where(row > r, jnp.broadcast_to(totals[r : r + 1, :], (rows, lanes)), 0.0)
    return (along - value + offset).astype(I32)


def count(flags):
    value = jnp.where(flags, 1.0, 0.0).astype(F32)
    return jnp.sum(jnp.sum(value, axis=1, keepdims=True), axis=0, keepdims=True).astype(I32)


def share_pairs(first, second, own_row, kinds, me, cut, cuts, cap, blocks):
    used = first >= 0
    ghost = second >= blocks
    slot = jnp.maximum(second - blocks, 0)
    owner = slot >> 2
    part = slot & 3
    own = ghost & (owner == me)
    far = ghost & (owner != me)
    wanted = jnp.zeros_like(second)
    for t in range(cap):
        row = jnp.broadcast_to(own_row[:, FIRST_ASK + t : FIRST_ASK + t + 1], second.shape)
        wanted = jnp.where(part == t, row, wanted)
    near_block = jnp.where(own, wanted, second)
    block = jnp.where(far, blocks + (owner >> 2) * cap + part, near_block)
    half = jnp.logical_and(jnp.logical_not(far), block == first)
    table = jnp.broadcast_to(kinds, first.shape)
    one = whole_burgers(jnp.take_along_axis(table, jnp.maximum(first, 0), axis=1))
    two = whole_burgers(jnp.take_along_axis(table, jnp.maximum(block, 0), axis=1))
    match = one[0] * two[0] + one[1] * two[1] + one[2] * two[2]
    match = jnp.where(half, 0.5 * match, match).astype(I32)
    alive = used & (match != 0)
    place = (owner + me) & 3
    mine_far = alive & far & (place == cut)
    near = alive & jnp.logical_not(far)
    part_size = (count(near) + cuts - 1) >> 2
    rank = prefix(near) - cut * part_size
    mine_near = near & (rank >= 0) & (rank < part_size)
    far_spot = prefix(mine_far)
    fits = (mine_far & (far_spot < FAR_SLOTS)) | (mine_near & (rank < NEAR_SLOTS))
    mine = mine_far | mine_near
    rest = mine & jnp.logical_not(fits)
    lanes = first.shape[1]
    spot = jnp.where(far, FAR_ROW * lanes + far_spot, NEAR_ROW * lanes + rank)
    spot = jnp.where(fits, spot, prefix(rest))
    first_code = jnp.where(mine, first + 32 * (match + 2), 0).astype(F32)
    second_code = jnp.where(mine, block, 0).astype(F32)
    rows = first.shape[0]
    codes = jnp.zeros((2 * LIST_ROWS, lanes), F32)
    for r in range(rows):
        at = spot[r : r + 1, :]
        hit = iota((LIST_ROWS, lanes), 0) == jnp.broadcast_to(at >> 7, (LIST_ROWS, lanes))
        left = jnp.concatenate(
            [
                jnp.where(hit, jnp.broadcast_to(first_code[r : r + 1, :], (LIST_ROWS, lanes)), 0.0),
                jnp.where(hit, jnp.broadcast_to(second_code[r : r + 1, :], (LIST_ROWS, lanes)), 0.0),
            ],
            axis=0,
        ).astype(BF16)
        chosen = iota((lanes, lanes), 0) == jnp.broadcast_to(at & (lanes - 1), (lanes, lanes))
        codes = codes + dot(left, jnp.where(chosen, 1.0, 0.0).astype(BF16), NT)
    return codes.astype(I32), count(rest)


def exchange_kernel(
    cuts, groups, cap, blocks,
    pos_in, conn_in, burg_in, req_in, pairs_in,
    data, ghost, asked, codes, extra, columns,
    pos, conn, burg, req, pairs, links, flat, wide, rows, heard, table, plist, stage, ordered,
    isem, rsend, rrecv, psend, precv, bsend, brecv,
):
    me = lax.axis_index("cell")
    cut = lax.axis_index("cuts")
    rho = lax.rem(cut - lax.rem(me, cuts) + cuts, cuts)
    slot = lax.div(me, cuts)
    inputs = [(req_in, req), (burg_in, burg), (pairs_in, pairs), (conn_in, conn), (pos_in, pos)]
    loads = [pltpu.make_async_copy(src, dst, isem.at[i]) for i, (src, dst) in enumerate(inputs)]
    for load in loads:
        load.start()
    heard[...] = jnp.full(heard.shape, -1, I32)
    ghost[...] = jnp.zeros(ghost.shape, F32)
    greet(me, cut, rho, groups, cuts)
    for load in loads[:3]:
        load.wait()
    fill_requests(req, burg, wide, rows)
    plist[cut] = jnp.zeros(plist.shape[1:], I32)
    for e in range(2):
        for r in range(2):
            plist[cut, 2 * e + r : 2 * e + r + 1, :] = pairs[e : e + 1, r * SEG : (r + 1) * SEG]
    await_greetings(me, rho, groups, cuts)

    def request_copy(m, other, at):
        return pltpu.make_async_remote_copy(
            src_ref=rows.at[other],
            dst_ref=heard.at[at],
            send_sem=rsend.at[m],
            recv_sem=rrecv.at[at],
            device_id=(other, cut),
            device_id_type=MESH,
        )

    def pair_copy(d, at):
        return pltpu.make_async_remote_copy(
            src_ref=plist.at[cut],
            dst_ref=plist.at[at],
            send_sem=psend.at[d - 1],
            recv_sem=precv.at[at],
            device_id=(me, lax.rem(cut + d, cuts)),
            device_id_type=MESH,
        )

    for_partners(me, rho, groups, cuts, lambda m, other: request_copy(m, other, slot).start())
    for d in range(1, cuts):
        pair_copy(d, cut).start()
    for load in loads[3:]:
        load.wait()
    values = segment_values(pos, conn, burg, links)
    table[...] = jnp.zeros(table.shape, table.dtype)
    for c in range(COMPS):
        lanes = slice(c * SEG, (c + 1) * SEG)
        data[:, lanes] = values[c]
        if c == SENT:
            continue
        flat[pl.ds(c, blocks, stride=8), :] = values[c]
        for part, piece in enumerate(split(values[c], 3)):
            table[part * blocks : (part + 1) * blocks, lanes] = piece
    for_partners(me, rho, groups, cuts, lambda m, other: request_copy(m, other, m).wait_recv())
    hear = jnp.concatenate([heard[m] for m in range(groups)], axis=0)
    asked[...] = jnp.full(asked.shape, -1, I32)
    for t in range(cap):
        column = hear[:, FIRST_ASK + t : FIRST_ASK + t + 1]
        asked[pl.ds(t, groups, stride=8), :] = jnp.broadcast_to(column, (groups, SEG))

    lane = iota(asked.shape, 1)
    hit = ((lane & (blocks - 1)) == asked[...]) & (lane < 3 * blocks)
    onehot = jnp.where(hit, 1.0, 0.0).astype(BF16)
    for c in range(SENT):
        lanes = slice(c * SEG, (c + 1) * SEG)
        got = dot(onehot, table[:, lanes], NN)
        for m in range(groups):
            stage[m, :, lanes] = got[m * 8 : m * 8 + cap, :]

    def block_copy(m, other, at):
        return pltpu.make_async_remote_copy(
            src_ref=stage.at[m],
            dst_ref=ghost.at[at],
            send_sem=bsend.at[m],
            recv_sem=brecv.at[at],
            device_id=(other, cut),
            device_id_type=MESH,
        )

    for_partners(me, rho, groups, cuts, lambda m, other: block_copy(m, other, slot).start())
    spread_columns(flat, columns)
    for d in range(1, cuts):
        pair_copy(d, lax.rem(cut - d + cuts, cuts)).wait_recv()
    for j in range(cuts):
        ordered[0, 2 * j : 2 * j + 2, :] = plist[j, 0:2, :]
        ordered[1, 2 * j : 2 * j + 2, :] = plist[j, 2:4, :]
    said = jnp.concatenate([rows[m * cuts + rho] for m in range(groups)], axis=0)
    own_row = rows[me]
    kinds = kind_table(own_row, hear, said, cap)
    listed, total = share_pairs(ordered[0], ordered[1], own_row, kinds, me, cut, cuts, cap, blocks)
    codes[...] = listed
    extra[...] = jnp.broadcast_to(total, extra.shape)
    for_partners(me, rho, groups, cuts, lambda m, other: block_copy(m, other, m).wait_recv())
    for_partners(me, rho, groups, cuts, lambda m, other: block_copy(m, other, m).wait_send())
    for_partners(me, rho, groups, cuts, lambda m, other: request_copy(m, other, m).wait_send())
    for d in range(1, cuts):
        pair_copy(d, cut).wait_send()


def fill_tables(data, ghost, everything, moments):
    blocks = data.shape[0]
    groups, cap, _ = ghost.shape

    def fill(target, row, value, start):
        target[start : start + value.shape[0], row, :] = value

    def fill_block(values, start):
        for c, value in enumerate(values):
            fill(everything, c, value, start)
        for c in range(3):
            for part, piece in enumerate(split(values[c], 3)):
                fill(moments, part * 3 + c, piece.astype(F32), start)

    moments[...] = jnp.where(iota(moments.shape, 1) == 9, 1.0, 0.0)
    fill_block([data[:, c * SEG : (c + 1) * SEG] for c in range(SENT)], 0)
    for m in range(groups):
        fill_block([ghost[m, :, c * SEG : (c + 1) * SEG] for c in range(SENT)], blocks + m * cap)


def one_pair(code, second, everything, moments, columns):
    first = code & 31
    kind = code >> 5
    factor = jnp.where(kind == 0, 0.0, (0.5 * MU_FACTOR) * (kind - 2).astype(F32))
    far = everything[second]
    middle = [far[c : c + 1] for c in range(3)]
    line = [far[3 + c : 4 + c] * factor for c in range(3)]
    high, low = [], []
    step = 32
    for start in range(0, SEG, step):
        rows = slice(start, start + step)
        r = [columns[first, c, rows, :] - middle[c] for c in range(3)]
        dist = r[0] * r[0] + CORE_SQUARED + r[1] * r[1] + r[2] * r[2]
        g = (
            columns[first, 3, rows, :] * line[0]
            + columns[first, 4, rows, :] * line[1]
            + columns[first, 5, rows, :] * line[2]
        )
        inverse = lax.rsqrt(dist)
        big, small = split(g * inverse * (inverse * inverse), 2)
        high.append(big)
        low.append(small)
    high = jnp.concatenate(high, axis=0)
    low = jnp.concatenate(low, axis=0)
    near_moments = moments[first].astype(BF16)
    far_moments = moments[second].astype(BF16)
    on_first = dot(
        jnp.concatenate([far_moments, far_moments], axis=1),
        jnp.concatenate([high, low], axis=1),
        NT,
    )
    on_second = dot(
        jnp.concatenate([near_moments, near_moments], axis=1),
        jnp.concatenate([high, low], axis=0),
        NN,
    )
    return first, on_first, on_second


def extra_kernel(extra, codes_in, data, ghost, columns, near_force, far_force, codes, sem, everything, moments, total):
    blocks = data.shape[0]
    groups, cap, _ = ghost.shape
    near_force[...] = jnp.zeros(near_force.shape, F32)
    far_force[...] = jnp.zeros(far_force.shape, F32)

    @pl.when(extra[0, 0] > 0)
    def _():
        load = pltpu.make_async_copy(codes_in, codes, sem)
        load.start()
        total[...] = jnp.zeros(total.shape, F32)
        fill_tables(data, ghost, everything, moments)
        load.wait()

        def body(index, carry):
            code = codes[index >> 7, index & (SEG - 1)]
            second = codes[LIST_ROWS + (index >> 7), index & (SEG - 1)]
            first, on_first, on_second = one_pair(code, second, everything, moments, columns)
            total[first] = total[first] + on_first
            total[second] = total[second] + on_second
            return carry

        lax.fori_loop(0, extra[0, 0], body, 0)

        def take(ref, row, start, rows):
            return ref[start : start + rows, row, :]

        def force(start, rows, c):
            weight = take(total, 9, start, rows)
            others = sum(take(total, 3 * part + c, start, rows) for part in range(3))
            return take(everything, c, start, rows) * weight - others

        for c in range(3):
            lanes = slice(c * SEG, (c + 1) * SEG)
            near_force[:, lanes] = force(0, blocks, c)
            for m in range(groups):
                far_force[m, :, lanes] = force(blocks + m * cap, cap, c)


def finish_kernel(
    cuts, groups, cap, blocks,
    near_extra, far_extra, codes_in, asked, data, ghost, columns, conn_in, stress,
    velocity,
    conn, isem, codes, csem, everything, moments, results, sums_of, near_force, far_force, back, table, shares, chosen, length, base, bsend, brecv, ssend, srecv,
):
    me = lax.axis_index("cell")
    cut = lax.axis_index("cuts")
    rho = lax.rem(cut - lax.rem(me, cuts) + cuts, cuts)
    slot = lax.div(me, cuts)
    load = pltpu.make_async_copy(conn_in, conn, isem)
    load.start()
    load_codes = pltpu.make_async_copy(codes_in, codes, csem)
    load_codes.start()
    back[...] = jnp.zeros(back.shape, F32)
    greet(me, cut, rho, groups, cuts)
    table[...] = jnp.zeros(table.shape, F32)
    fill_tables(data, ghost, everything, moments)
    load_codes.wait()

    def run_list(row, slots, unroll):
        def step(i, carry):
            for u in range(unroll):
                at = i * unroll + u
                code = codes[row, at]
                second = codes[LIST_ROWS + row, at]
                _, on_first, on_second = one_pair(code, second, everything, moments, columns)
                results[0, at] = on_first
                results[1, at] = on_second
            return carry

        lax.fori_loop(0, slots // unroll, step, 0)

    def collect(side, slots):
        def row(r):
            return results[side, 0:slots, r, :]

        for c in range(3):
            sums_of[0:slots, c * SEG : (c + 1) * SEG] = row(c) + row(3 + c) + row(6 + c)
        sums_of[0:slots, 3 * SEG : 4 * SEG] = row(9)
        return split(sums_of[...], 3)

    def near_collect(side):
        sums_of[...] = jnp.zeros(sums_of.shape, F32)
        return collect(side, NEAR_SLOTS)

    def scatter(at, start, size, pieces):
        hit = iota((size, SEG), 0) + start == jnp.broadcast_to(at, (size, SEG))
        onehot = jnp.where(hit, 1.0, 0.0).astype(BF16)
        return sum(dot(onehot, piece, NN) for piece in pieces)

    def middle_of(c, start, size):
        return everything[start : start + size, c, :]

    sums_of[...] = jnp.zeros(sums_of.shape, F32)
    run_list(FAR_ROW, FAR_SLOTS, FAR_STEP)
    ghosts = groups * cap
    second_at = codes_in[LIST_ROWS + FAR_ROW : LIST_ROWS + FAR_ROW + 1, :]
    far_sums = scatter(second_at, blocks, ghosts, collect(1, FAR_SLOTS))
    for c in range(3):
        lanes = slice(c * SEG, (c + 1) * SEG)
        force = middle_of(c, blocks, ghosts) * far_sums[:, 3 * SEG :] - far_sums[:, lanes]
        for m in range(groups):
            far_force[m, :, lanes] = force[m * cap : (m + 1) * cap, :] + far_extra[m, :, lanes]

    def node_of(b, end):
        return conn[end : end + 1, pl.ds(pl.multiple_of(b * SEG, SEG), SEG)]

    def choose(b, carry):
        for end in range(2):
            low = jnp.broadcast_to(node_of(b, end) & (SEG - 1), (SEG, SEG))
            hit = iota((SEG, SEG), 0) == low
            chosen[b, :, end * SEG : (end + 1) * SEG] = jnp.where(hit, 1.0, 0.0).astype(BF16)
        return carry

    await_greetings(me, rho, groups, cuts)

    def reaction_copy(m, other, at):
        return pltpu.make_async_remote_copy(
            src_ref=far_force.at[m],
            dst_ref=back.at[at],
            send_sem=bsend.at[m],
            recv_sem=brecv.at[at],
            device_id=(other, cut),
            device_id_type=MESH,
        )

    for_partners(me, rho, groups, cuts, lambda m, other: reaction_copy(m, other, slot).start())
    first_at = codes_in[FAR_ROW : FAR_ROW + 1, :] & 31
    near_sums = scatter(first_at, 0, blocks, collect(0, FAR_SLOTS))
    run_list(NEAR_ROW, NEAR_SLOTS, NEAR_STEP)
    first_at = codes_in[NEAR_ROW : NEAR_ROW + 1, :] & 31
    near_sums = near_sums + scatter(first_at, 0, blocks, near_collect(0))
    second_at = codes_in[LIST_ROWS + NEAR_ROW : LIST_ROWS + NEAR_ROW + 1, :]
    near_sums = near_sums + scatter(second_at, 0, blocks, near_collect(1))
    for c in range(3):
        lanes = slice(c * SEG, (c + 1) * SEG)
        force = middle_of(c, 0, blocks) * near_sums[:, 3 * SEG :] - near_sums[:, lanes]
        near_force[:, lanes] = force + near_extra[:, lanes]
    load.wait()
    lax.fori_loop(0, blocks, choose, 0, unroll=2)

    def node_step(g, eight, carry):
        for i in range(8):
            b = g * 8 + i
            left = []
            for end in range(2):
                high = jnp.broadcast_to(node_of(b, end) >> 7, (blocks, SEG))
                hit = iota((blocks, SEG), 0) == high
                column = [
                    jnp.where(hit, jnp.broadcast_to(piece[i : i + 1, :], (blocks, SEG)), 0.0)
                    for piece in eight
                ]
                left.append(jnp.concatenate(column, axis=0).astype(BF16))
            carry = carry + dot(jnp.concatenate(left, axis=1), chosen[b], NT)
        return carry

    def node_sums(fetch, parts):
        def step(g, carry):
            pieces = [piece.astype(F32) for value in fetch(g) for piece in split(value, 2)]
            return node_step(g, pieces, carry)

        sums = lax.fori_loop(0, blocks // 8, step, jnp.zeros((2 * parts * blocks, SEG), F32))
        rows = [sums[p * blocks : (p + 1) * blocks] for p in range(2 * parts)]
        return [rows[p] + rows[p + 1] for p in range(0, 2 * parts, 2)]

    def eight_rows(g):
        return pl.ds(pl.multiple_of(g * 8, 8), 8)

    value = [data[:, c * SEG : (c + 1) * SEG] for c in range(COMPS)]
    line = value[3:6]
    burgers = burgers_of(value[6])
    sigma = [[0.5 * (stress[a, b] + stress[b, a]) for b in range(3)] for a in range(3)]
    pull = [sigma[a][0] * burgers[0] + sigma[a][1] * burgers[1] + sigma[a][2] * burgers[2] for a in range(3)]
    for c in range(3):
        u, v = (c + 1) % 3, (c + 2) % 3
        base[:, c * SEG : (c + 1) * SEG] = pull[u] * line[v] - pull[v] * line[u]
    length[...] = jnp.sqrt(line[0] * line[0] + line[1] * line[1] + line[2] * line[2] + CORE_SQUARED)
    drag = node_sums(lambda g: [length[eight_rows(g), :]], 1)[0]
    hit = iota(asked.shape, 1) == asked[...]
    onehot = jnp.transpose(jnp.where(hit, 1.0, 0.0))[:blocks, :].astype(BF16)
    for_partners(me, rho, groups, cuts, lambda m, other: reaction_copy(m, other, m).wait_recv())
    for m in range(groups):
        table[m * 8 : m * 8 + cap, :] = back[m]
    mine = near_force[...]
    for piece in split(table[...], 3):
        mine = mine + dot(onehot, piece, NN)
    shares[cut] = mine

    def share_copy(d, at, g):
        return pltpu.make_async_remote_copy(
            src_ref=shares.at[cut, eight_rows(g)],
            dst_ref=shares.at[at, eight_rows(g)],
            send_sem=ssend.at[d - 1, g],
            recv_sem=srecv.at[at, g],
            device_id=(me, lax.rem(cut + d, cuts)),
            device_id_type=MESH,
        )

    for g in range(blocks // 8):
        for d in range(1, cuts):
            share_copy(d, cut, g).start()

    def added(g):
        for d in range(1, cuts):
            share_copy(d, lax.rem(cut - d + cuts, cuts), g).wait_recv()
        value = base[eight_rows(g), :]
        for j in range(cuts):
            value = value + shares[j, eight_rows(g), :]
        return [value[:, c * SEG : (c + 1) * SEG] for c in range(3)]

    sums = node_sums(added, 3)
    for c in range(3):
        speed = sums[c] / drag
        for b in range(blocks):
            velocity[c : c + 1, b * SEG : (b + 1) * SEG] = speed[b : b + 1, :]
    for g in range(blocks // 8):
        for d in range(1, cuts):
            share_copy(d, cut, g).wait_send()
    for_partners(me, rho, groups, cuts, lambda m, other: reaction_copy(m, other, m).wait_send())


def body(cuts, node_positions, connectivity, burgers_index, applied_stress, ghost_request, pair_list):
    blocks = burgers_index.shape[0]
    owners, cap = ghost_request.shape[1:]
    groups = owners // cuts
    nodes = node_positions.shape[1]
    width = COMPS * SEG
    shape = jax.ShapeDtypeStruct
    dma = pltpu.SemaphoreType.DMA
    data, ghost, asked, codes, extra, columns = pl.pallas_call(
        functools.partial(exchange_kernel, cuts, groups, cap, blocks),
        name="exchange",
        out_shape=(
            shape((blocks, width), F32),
            shape((groups, cap, SENT * SEG), F32),
            shape((groups * 8, SEG), I32),
            shape((2 * LIST_ROWS, SEG), I32),
            shape((1, SEG), I32),
            shape((blocks, 6, SEG, SEG), F32),
        ),
        in_specs=[ANY] * 5,
        out_specs=(VMEM,) * 6,
        scratch_shapes=[
            pltpu.VMEM((3, nodes), F32),
            pltpu.VMEM((2, nodes), I32),
            pltpu.VMEM((1, blocks), I32),
            pltpu.VMEM((cap, owners), I32),
            pltpu.VMEM(pair_list.shape, I32),
            pltpu.VMEM((2, blocks, SEG), I32),
            pltpu.VMEM((blocks * 8, SEG), F32),
            pltpu.VMEM((1, SEG), I32),
            pltpu.VMEM((owners, 1, SEG), I32),
            pltpu.VMEM((groups, 1, SEG), I32),
            pltpu.VMEM((SEG, SENT * SEG), BF16),
            pltpu.VMEM((cuts, 8, SEG), I32),
            pltpu.VMEM((groups, cap, SENT * SEG), F32),
            pltpu.VMEM((2, 8, SEG), I32),
            dma((5,)),
            dma((groups,)), dma((groups,)), dma((cuts,)), dma((cuts,)), dma((groups,)), dma((groups,)),
        ],
        compiler_params=pltpu.CompilerParams(
            collective_id=0, has_side_effects=True, vmem_limit_bytes=EXCHANGE_VMEM
        ),
    )(
        stay(node_positions),
        stay(connectivity),
        stay(burgers_index.reshape(1, blocks)),
        stay(jnp.transpose(ghost_request[0])),
        stay(pair_list),
    )
    total_blocks = blocks + groups * cap
    tables = [pltpu.VMEM((total_blocks, ROWS, SEG), F32)] * 2
    list_scratch = [pltpu.SMEM((2 * LIST_ROWS, SEG), I32), dma]
    near_extra, far_extra = pl.pallas_call(
        extra_kernel,
        name="extra",
        out_shape=(shape((blocks, 3 * SEG), F32), shape((groups, cap, 3 * SEG), F32)),
        in_specs=[SMEM, VMEM, VMEM, VMEM, VMEM],
        out_specs=(VMEM,) * 2,
        scratch_shapes=list_scratch + tables + [pltpu.VMEM((total_blocks, ROWS, SEG), F32)],
        compiler_params=pltpu.CompilerParams(vmem_limit_bytes=PAIRS_VMEM),
    )(extra, codes, data, ghost, columns)
    return pl.pallas_call(
        functools.partial(finish_kernel, cuts, groups, cap, blocks),
        name="finish",
        out_shape=shape((3, nodes), F32),
        in_specs=[VMEM] * 7 + [ANY, SMEM],
        out_specs=VMEM,
        scratch_shapes=[
            pltpu.VMEM((2, nodes), I32),
            dma,
            *list_scratch,
            *tables,
            pltpu.VMEM((2, SEG, ROWS, SEG), F32),
            pltpu.VMEM((SEG, 4 * SEG), F32),
            pltpu.VMEM((blocks, 3 * SEG), F32),
            pltpu.VMEM((groups, cap, 3 * SEG), F32),
            pltpu.VMEM((groups, cap, 3 * SEG), F32),
            pltpu.VMEM((groups * 8, 3 * SEG), F32),
            pltpu.VMEM((cuts, blocks, 3 * SEG), F32),
            pltpu.VMEM((blocks, SEG, 2 * SEG), BF16),
            pltpu.VMEM((blocks, SEG), F32),
            pltpu.VMEM((blocks, 3 * SEG), F32),
            dma((groups,)), dma((groups,)), dma((cuts, blocks // 8)), dma((cuts, blocks // 8)),
        ],
        compiler_params=pltpu.CompilerParams(
            collective_id=1, has_side_effects=True, vmem_limit_bytes=FINISH_VMEM
        ),
    )(near_extra, far_extra, codes, asked, data, ghost, columns, stay(connectivity), applied_stress)


def solution(mesh):
    in_specs = (
        P(None, "cell"),
        P(None, "cell"),
        P("cell"),
        P(),
        P("cell", None, None),
        P(None, ("cell", "cuts")),
    )
    return jax.shard_map(
        functools.partial(body, mesh.shape["cuts"]),
        mesh=mesh,
        in_specs=in_specs,
        out_specs=P(None, "cell"),
        check_vma=False,
    )
```

```python
import functools

import jax
import jax.numpy as jnp
from jax import lax
from jax.experimental import pallas as pl
from jax.experimental.pallas import tpu as pltpu
from jax.sharding import PartitionSpec as P

SEG = 128
COMPS = 7
SENT = 6
FIRST_ASK = 64
ROWS = 16
FIRST_SLOTS = 72
FIRST_STEP = 36
LAST_STEP = 48
NEAR_STEP = 40
FAR_SLOTS = 120
NEAR_SLOTS = 40
FAR_ROW = 8
NEAR_ROW = 9
LIST_ROWS = 16
MIB = 1024 * 1024
EXCHANGE_VMEM = 24 * MIB
PAIRS_VMEM = 24 * MIB
FINISH_VMEM = 24 * MIB
MU_FACTOR = 10.0
CORE_SQUARED = 0.25
HALF_ROOT = 0.5**0.5
MESH = pl.DeviceIdType.MESH
F32 = jnp.float32
BF16 = jnp.bfloat16
I32 = jnp.int32
VMEM = pl.BlockSpec(memory_space=pltpu.VMEM)
SMEM = pl.BlockSpec(memory_space=pltpu.SMEM)
ANY = pl.BlockSpec(memory_space=pltpu.HBM)
NN = (((1,), (0,)), ((), ()))
NT = (((1,), (1,)), ((), ()))


def stay(value):
    return pltpu.with_memory_space_constraint(value, pltpu.HBM)


def iota(shape, axis):
    return lax.broadcasted_iota(I32, shape, axis)


def dot(a, b, dims):
    return lax.dot_general(a, b, dims, preferred_element_type=F32)


def split(value, parts):
    pieces = []
    rest = value
    for part in range(parts):
        piece = rest.astype(BF16)
        pieces.append(piece)
        if part < parts - 1:
            rest = rest - piece.astype(F32)
    return pieces


def segment_values(pos, conn, burg, links):
    blocks = links.shape[1]
    for end in range(2):
        for b in range(blocks):
            links[end, b : b + 1, :] = conn[end : end + 1, b * SEG : (b + 1) * SEG]
    low = [links[end] & (SEG - 1) for end in range(2)]
    high = [links[end] >> 7 for end in range(2)]

    def step(h, carry):
        lanes = pl.ds(pl.multiple_of(h * SEG, SEG), SEG)
        out = []
        for end in range(2):
            hit = high[end] == h
            for c in range(3):
                row = jnp.broadcast_to(pos[c : c + 1, lanes], (blocks, SEG))
                got = jnp.take_along_axis(row, low[end], axis=1)
                out.append(jnp.where(hit, got, carry[end * 3 + c]))
        return tuple(out)

    zero = jnp.zeros((blocks, SEG), F32)
    ends = lax.fori_loop(0, pos.shape[1] // SEG, step, (zero,) * 6, unroll=2)
    values = [0.5 * (ends[c] + ends[3 + c]) for c in range(3)]
    values += [ends[3 + c] - ends[c] for c in range(3)]
    diagonal = iota((blocks, blocks), 0) == iota((blocks, blocks), 1)
    kinds = jnp.broadcast_to(burg[...], (blocks, blocks)).astype(F32)
    kind = jnp.sum(jnp.where(diagonal, kinds, 0.0), axis=1, keepdims=True)
    values.append(jnp.broadcast_to(kind, (blocks, SEG)))
    return values


def burgers_of(kind):
    return [HALF_ROOT * value for value in whole_burgers(kind)]


def fill_requests(req, burg, wide, rows):
    cap, owners = req.shape
    blocks = burg.shape[1]
    wide[...] = jnp.zeros(wide.shape, I32)
    wide[:, 0:blocks] = burg[...]
    message = jnp.broadcast_to(wide[...], (owners, SEG))
    lane = iota((owners, SEG), 1)
    diagonal = iota((owners, owners), 0) == iota((owners, owners), 1)
    for t in range(cap):
        row = jnp.broadcast_to(req[t : t + 1, :], (owners, owners)).astype(F32)
        column = jnp.sum(jnp.where(diagonal, row, 0.0), axis=1, keepdims=True)
        column = jnp.broadcast_to(column, (owners, SEG)).astype(I32)
        message = jnp.where(lane == FIRST_ASK + t, column, message)
    for o in range(owners):
        rows[o] = message[o : o + 1, :]


def kind_table(own, heard, said, cap):
    groups = heard.shape[0]
    lane = iota((groups, SEG), 1)
    blocks = FIRST_ASK // 2
    wanted = jnp.zeros((groups, SEG), I32)
    for t in range(cap):
        column = jnp.broadcast_to(said[:, FIRST_ASK + t : FIRST_ASK + t + 1], (groups, SEG))
        wanted = jnp.where((lane & 3) == t, column, wanted)
    found = jnp.take_along_axis(heard, jnp.maximum(wanted, 0), axis=1)
    here = (lane >= blocks) & (((lane - blocks) >> 2) == iota((groups, SEG), 0))
    ghosts = jnp.sum(jnp.where(here, found, 0).astype(F32), axis=0, keepdims=True)
    return jnp.where(iota((1, SEG), 1) < blocks, own.astype(F32), ghosts)


def whole_burgers(kind):
    odd = jnp.where((kind == 1.0) | (kind == 3.0) | (kind == 5.0), -1.0, 1.0)
    return [
        jnp.where(kind < 4.0, 1.0, 0.0),
        jnp.where(kind < 2.0, odd, jnp.where(kind < 4.0, 0.0, 1.0)),
        jnp.where(kind < 2.0, 0.0, odd),
    ]


def spread_columns(flat, columns):
    def step(block, carry):
        rows = flat[pl.ds(pl.multiple_of(block * 8, 8), 8), :]
        for c in range(6):
            columns[block, c] = jnp.transpose(jnp.broadcast_to(rows[c : c + 1, :], (SEG, SEG)))
        return carry

    lax.fori_loop(0, columns.shape[0], step, 0, unroll=8)


def node_of(conn, b, end):
    return conn[end : end + 1, pl.ds(pl.multiple_of(b * SEG, SEG), SEG)]


def eight_rows(g):
    return pl.ds(pl.multiple_of(g * 8, 8), 8)


def choose_nodes(conn, chosen):
    def choose(b, carry):
        for end in range(2):
            low = jnp.broadcast_to(node_of(conn, b, end) & (SEG - 1), (SEG, SEG))
            hit = iota((SEG, SEG), 0) == low
            chosen[b, :, end * SEG : (end + 1) * SEG] = jnp.where(hit, 1.0, 0.0).astype(BF16)
        return carry

    lax.fori_loop(0, chosen.shape[0], choose, 0, unroll=2)


def node_sums(conn, chosen, fetch, parts):
    blocks = chosen.shape[0]

    def step(g, carry):
        pieces = [piece.astype(F32) for value in fetch(g) for piece in split(value, 2)]
        for i in range(8):
            b = g * 8 + i
            left = []
            for end in range(2):
                high = jnp.broadcast_to(node_of(conn, b, end) >> 7, (blocks, SEG))
                hit = iota((blocks, SEG), 0) == high
                column = [
                    jnp.where(hit, jnp.broadcast_to(piece[i : i + 1, :], (blocks, SEG)), 0.0)
                    for piece in pieces
                ]
                left.append(jnp.concatenate(column, axis=0).astype(BF16))
            carry = carry + dot(jnp.concatenate(left, axis=1), chosen[b], NT)
        return carry

    sums = lax.fori_loop(0, blocks // 8, step, jnp.zeros((2 * parts * blocks, SEG), F32))
    rows = [sums[p * blocks : (p + 1) * blocks] for p in range(2 * parts)]
    return [rows[p] + rows[p + 1] for p in range(0, 2 * parts, 2)]


def outer_force(values, stress):
    line = values[3:6]
    burgers = burgers_of(values[6])
    sigma = [[0.5 * (stress[a, b] + stress[b, a]) for b in range(3)] for a in range(3)]
    pull = [sigma[a][0] * burgers[0] + sigma[a][1] * burgers[1] + sigma[a][2] * burgers[2] for a in range(3)]
    forces = []
    for c in range(3):
        u, v = (c + 1) % 3, (c + 2) % 3
        forces.append(pull[u] * line[v] - pull[v] * line[u])
    return forces


def partner(i, me, rho, groups, cuts):
    half = groups // 2
    hop = jnp.where(lax.rem(i, 2) == 0, half + lax.div(i, 2), half - lax.div(i + 1, 2))
    m = lax.rem(lax.div(me, cuts) + hop, groups)
    return m, m * cuts + rho


def for_partners(me, rho, groups, cuts, run, first=0, last=None):
    def step(i, carry):
        m, other = partner(i, me, rho, groups, cuts)

        @pl.when(other != me)
        def _():
            run(i, m, other)

        return carry

    lax.fori_loop(first, groups if last is None else last, step, 0)


def greet(me, cut, rho, groups, cuts):
    barrier = pltpu.get_barrier_semaphore()

    def signal(i, m, other):
        pl.semaphore_signal(barrier, inc=1, device_id=(other, cut), device_id_type=MESH)

    for_partners(me, rho, groups, cuts, signal)
    for d in range(1, cuts):
        peer = lax.rem(cut + d, cuts)
        pl.semaphore_signal(barrier, inc=1, device_id=(me, peer), device_id_type=MESH)


def await_greetings(me, rho, groups, cuts):
    own = jnp.where(rho == lax.rem(me, cuts), 1, 0)
    pl.semaphore_wait(pltpu.get_barrier_semaphore(), groups + cuts - 1 - own)


def prefix(flags):
    rows, lanes = flags.shape
    value = jnp.where(flags, 1.0, 0.0).astype(F32)
    coded = value.astype(BF16)
    upper = jnp.where(iota((lanes, lanes), 0) <= iota((lanes, lanes), 1), 1.0, 0.0).astype(BF16)
    along = dot(coded, upper, NN)
    ones = jnp.ones((lanes, lanes), BF16)
    totals = dot(coded, ones, NN)
    row = iota((rows, lanes), 0)
    offset = jnp.zeros((rows, lanes), F32)
    for r in range(rows - 1):
        offset = offset + jnp.where(row > r, jnp.broadcast_to(totals[r : r + 1, :], (rows, lanes)), 0.0)
    return (along - value + offset).astype(I32)


def count(flags):
    value = jnp.where(flags, 1.0, 0.0).astype(F32)
    return jnp.sum(jnp.sum(value, axis=1, keepdims=True), axis=0, keepdims=True).astype(I32)


def share_pairs(first, second, own_row, kinds, me, cut, cuts, cap, blocks):
    slot_of_me = me // cuts
    used = first >= 0
    ghost = second >= blocks
    slot = jnp.maximum(second - blocks, 0)
    owner = slot >> 2
    part = slot & 3
    own = ghost & (owner == me)
    far = ghost & (owner != me)
    wanted = jnp.zeros_like(second)
    for t in range(cap):
        row = jnp.broadcast_to(own_row[:, FIRST_ASK + t : FIRST_ASK + t + 1], second.shape)
        wanted = jnp.where(part == t, row, wanted)
    near_block = jnp.where(own, wanted, second)
    block = jnp.where(far, blocks + (owner >> 2) * cap + part, near_block)
    half = jnp.logical_and(jnp.logical_not(far), block == first)
    table = jnp.broadcast_to(kinds, first.shape)
    one = whole_burgers(jnp.take_along_axis(table, jnp.maximum(first, 0), axis=1))
    two = whole_burgers(jnp.take_along_axis(table, jnp.maximum(block, 0), axis=1))
    match = one[0] * two[0] + one[1] * two[1] + one[2] * two[2]
    match = jnp.where(half, 0.5 * match, match).astype(I32)
    alive = used & (match != 0)
    place = (owner + me) & 3
    mine_far = alive & far & (place == cut)
    near = alive & jnp.logical_not(far)
    part_size = (count(near) + cuts - 1) >> 2
    rank = prefix(near) - cut * part_size
    mine_near = near & (rank >= 0) & (rank < part_size)
    hop = ((owner >> 2) - slot_of_me) & 15
    distant = (hop >= 4) & (hop < 12)
    mine_first = mine_far & distant
    mine_last = mine_far & jnp.logical_not(distant)
    far_spot = jnp.where(distant, prefix(mine_first), count(mine_first) + prefix(mine_last))
    room = jnp.where(distant, FIRST_SLOTS, FAR_SLOTS)
    fits = (mine_far & (far_spot < room)) | (mine_near & (rank < NEAR_SLOTS))
    mine = mine_far | mine_near
    rest = mine & jnp.logical_not(fits)
    lanes = first.shape[1]
    spot = jnp.where(far, FAR_ROW * lanes + far_spot, NEAR_ROW * lanes + rank)
    spot = jnp.where(fits, spot, prefix(rest))
    first_code = jnp.where(mine, first + 32 * (match + 2), 0).astype(F32)
    second_code = jnp.where(mine, block, 0).astype(F32)
    rows = first.shape[0]
    codes = jnp.zeros((2 * LIST_ROWS, lanes), F32)
    for r in range(rows):
        at = spot[r : r + 1, :]
        hit = iota((LIST_ROWS, lanes), 0) == jnp.broadcast_to(at >> 7, (LIST_ROWS, lanes))
        left = jnp.concatenate(
            [
                jnp.where(hit, jnp.broadcast_to(first_code[r : r + 1, :], (LIST_ROWS, lanes)), 0.0),
                jnp.where(hit, jnp.broadcast_to(second_code[r : r + 1, :], (LIST_ROWS, lanes)), 0.0),
            ],
            axis=0,
        ).astype(BF16)
        chosen = iota((lanes, lanes), 0) == jnp.broadcast_to(at & (lanes - 1), (lanes, lanes))
        codes = codes + dot(left, jnp.where(chosen, 1.0, 0.0).astype(BF16), NT)
    return codes.astype(I32), count(rest)


def exchange_kernel(
    cuts, groups, cap, blocks,
    pos_in, conn_in, burg_in, req_in, pairs_in,
    data, ghost, asked, codes, extra, columns, chosen, drag, conn,
    pos, burg, req, pairs, links, flat, length, wide, rows, heard, table, plist, stage, ordered,
    isem, rsend, rrecv, psend, precv, bsend, brecv,
):
    me = lax.axis_index("cell")
    cut = lax.axis_index("cuts")
    rho = lax.rem(cut - lax.rem(me, cuts) + cuts, cuts)
    slot = lax.div(me, cuts)
    heard[slot] = jnp.full(heard.shape[1:], -1, I32)
    ghost[slot] = jnp.zeros(ghost.shape[1:], F32)
    greet(me, cut, rho, groups, cuts)
    inputs = [(req_in, req), (burg_in, burg), (pairs_in, pairs), (conn_in, conn), (pos_in, pos)]
    loads = [pltpu.make_async_copy(src, dst, isem.at[i]) for i, (src, dst) in enumerate(inputs)]
    for load in loads:
        load.start()
    for load in loads[:3]:
        load.wait()
    fill_requests(req, burg, wide, rows)
    plist[cut] = jnp.zeros(plist.shape[1:], I32)
    for e in range(2):
        for r in range(2):
            plist[cut, 2 * e + r : 2 * e + r + 1, :] = pairs[e : e + 1, r * SEG : (r + 1) * SEG]
    await_greetings(me, rho, groups, cuts)

    def request_copy(m, other, at):
        return pltpu.make_async_remote_copy(
            src_ref=rows.at[other],
            dst_ref=heard.at[at],
            send_sem=rsend.at[m],
            recv_sem=rrecv.at[at],
            device_id=(other, cut),
            device_id_type=MESH,
        )

    def pair_copy(d, at):
        return pltpu.make_async_remote_copy(
            src_ref=plist.at[cut],
            dst_ref=plist.at[at],
            send_sem=psend.at[d - 1],
            recv_sem=precv.at[at],
            device_id=(me, lax.rem(cut + d, cuts)),
            device_id_type=MESH,
        )

    for_partners(me, rho, groups, cuts, lambda i, m, other: request_copy(m, other, slot).start())
    for d in range(1, cuts):
        pair_copy(d, cut).start()
    for load in loads[3:]:
        load.wait()
    values = segment_values(pos, conn, burg, links)
    table[...] = jnp.zeros(table.shape, table.dtype)
    for c in range(COMPS):
        lanes = slice(c * SEG, (c + 1) * SEG)
        data[:, lanes] = values[c]
        if c == SENT:
            continue
        flat[pl.ds(c, blocks, stride=8), :] = values[c]
        for part, piece in enumerate(split(values[c], 3)):
            table[part * blocks : (part + 1) * blocks, lanes] = piece
    def block_copy(i, m, other, at):
        return pltpu.make_async_remote_copy(
            src_ref=stage.at[i],
            dst_ref=ghost.at[at],
            send_sem=bsend.at[i],
            recv_sem=brecv.at[at],
            device_id=(other, cut),
            device_id_type=MESH,
        )

    def serve(first, last):
        def arrived(i, m, other):
            request_copy(m, other, m).wait_recv()

        for_partners(me, rho, groups, cuts, arrived, first, last)
        count = last - first
        order = [partner(i, me, rho, groups, cuts)[0] for i in range(first, last)]
        asks = jnp.concatenate([heard[m] for m in order], axis=0)
        columns_of = [asks[:, FIRST_ASK + t : FIRST_ASK + t + 1] for t in range(cap)]
        wanted = jnp.concatenate([jnp.broadcast_to(column, (count, SEG)) for column in columns_of], axis=0)
        lane = iota(wanted.shape, 1)
        hit = ((lane & (blocks - 1)) == wanted) & (lane < 3 * blocks)
        onehot = jnp.where(hit, 1.0, 0.0).astype(BF16)
        for c in range(SENT):
            lanes = slice(c * SEG, (c + 1) * SEG)
            got = dot(onehot, table[:, lanes], NN)
            for t in range(cap):
                stage[first:last, t, lanes] = got[t * count : (t + 1) * count, :]
        for_partners(me, rho, groups, cuts, lambda i, m, other: block_copy(i, m, other, slot).start(), first, last)

    serve(groups // 2, groups)
    serve(0, groups // 2)
    hear = jnp.concatenate([heard[m] for m in range(groups)], axis=0)
    asked[...] = jnp.full(asked.shape, -1, I32)
    for t in range(cap):
        column = hear[:, FIRST_ASK + t : FIRST_ASK + t + 1]
        asked[pl.ds(t, groups, stride=8), :] = jnp.broadcast_to(column, (groups, SEG))

    spread_columns(flat, columns)
    for d in range(1, cuts):
        pair_copy(d, lax.rem(cut - d + cuts, cuts)).wait_recv()
    for j in range(cuts):
        ordered[0, 2 * j : 2 * j + 2, :] = plist[j, 0:2, :]
        ordered[1, 2 * j : 2 * j + 2, :] = plist[j, 2:4, :]
    said = jnp.concatenate([rows[m * cuts + rho] for m in range(groups)], axis=0)
    own_row = rows[me]
    kinds = kind_table(own_row, hear, said, cap)
    listed, total = share_pairs(ordered[0], ordered[1], own_row, kinds, me, cut, cuts, cap, blocks)
    codes[...] = listed
    extra[...] = jnp.broadcast_to(total, extra.shape)
    choose_nodes(conn, chosen)
    line = [data[:, c * SEG : (c + 1) * SEG] for c in range(3, 6)]
    length[...] = jnp.sqrt(line[0] * line[0] + line[1] * line[1] + line[2] * line[2] + CORE_SQUARED)
    drag[...] = node_sums(conn, chosen, lambda g: [length[eight_rows(g), :]], 1)[0]
    for_partners(me, rho, groups, cuts, lambda i, m, other: block_copy(i, m, other, m).wait_recv())
    for_partners(me, rho, groups, cuts, lambda i, m, other: block_copy(i, m, other, m).wait_send())
    for_partners(me, rho, groups, cuts, lambda i, m, other: request_copy(m, other, m).wait_send())
    for d in range(1, cuts):
        pair_copy(d, cut).wait_send()


def fill_tables(data, ghost, everything, moments):
    blocks = data.shape[0]
    groups, cap, _ = ghost.shape

    def fill(target, row, value, start):
        target[start : start + value.shape[0], row, :] = value

    def fill_block(values, start):
        for c, value in enumerate(values):
            fill(everything, c, value, start)
        for c in range(3):
            for part, piece in enumerate(split(values[c], 3)):
                fill(moments, part * 3 + c, piece.astype(F32), start)

    moments[...] = jnp.where(iota(moments.shape, 1) == 9, 1.0, 0.0)
    fill_block([data[:, c * SEG : (c + 1) * SEG] for c in range(SENT)], 0)
    for m in range(groups):
        fill_block([ghost[m, :, c * SEG : (c + 1) * SEG] for c in range(SENT)], blocks + m * cap)


def one_pair(code, second, everything, moments, columns):
    first = code & 31
    kind = code >> 5
    factor = jnp.where(kind == 0, 0.0, (0.5 * MU_FACTOR) * (kind - 2).astype(F32))
    far = everything[second]
    middle = [far[c : c + 1] for c in range(3)]
    line = [far[3 + c : 4 + c] * factor for c in range(3)]
    high, low = [], []
    step = 32
    for start in range(0, SEG, step):
        rows = slice(start, start + step)
        r = [columns[first, c, rows, :] - middle[c] for c in range(3)]
        dist = r[0] * r[0] + CORE_SQUARED + r[1] * r[1] + r[2] * r[2]
        g = (
            columns[first, 3, rows, :] * line[0]
            + columns[first, 4, rows, :] * line[1]
            + columns[first, 5, rows, :] * line[2]
        )
        inverse = lax.rsqrt(dist)
        big, small = split(g * inverse * (inverse * inverse), 2)
        high.append(big)
        low.append(small)
    high = jnp.concatenate(high, axis=0)
    low = jnp.concatenate(low, axis=0)
    near_moments = moments[first].astype(BF16)
    far_moments = moments[second].astype(BF16)
    on_first = dot(
        jnp.concatenate([far_moments, far_moments], axis=1),
        jnp.concatenate([high, low], axis=1),
        NT,
    )
    on_second = dot(
        jnp.concatenate([near_moments, near_moments], axis=1),
        jnp.concatenate([high, low], axis=0),
        NN,
    )
    return first, on_first, on_second


def extra_kernel(extra, codes_in, data, ghost, columns, near_force, far_force, codes, sem, everything, moments, total):
    blocks = data.shape[0]
    groups, cap, _ = ghost.shape
    near_force[...] = jnp.zeros(near_force.shape, F32)
    far_force[...] = jnp.zeros(far_force.shape, F32)

    left = jnp.max(extra[...].astype(F32)).astype(I32)

    @pl.when(left > 0)
    def _():
        load = pltpu.make_async_copy(codes_in, codes, sem)
        load.start()
        total[...] = jnp.zeros(total.shape, F32)
        fill_tables(data, ghost, everything, moments)
        load.wait()

        def body(index, carry):
            code = codes[index >> 7, index & (SEG - 1)]
            second = codes[LIST_ROWS + (index >> 7), index & (SEG - 1)]
            first, on_first, on_second = one_pair(code, second, everything, moments, columns)
            total[first] = total[first] + on_first
            total[second] = total[second] + on_second
            return carry

        lax.fori_loop(0, left, body, 0)

        def take(ref, row, start, rows):
            return ref[start : start + rows, row, :]

        def force(start, rows, c):
            weight = take(total, 9, start, rows)
            others = sum(take(total, 3 * part + c, start, rows) for part in range(3))
            return take(everything, c, start, rows) * weight - others

        for c in range(3):
            lanes = slice(c * SEG, (c + 1) * SEG)
            near_force[:, lanes] = force(0, blocks, c)
            for m in range(groups):
                far_force[m, :, lanes] = force(blocks + m * cap, cap, c)


def finish_kernel(
    cuts, groups, cap, blocks,
    near_extra, far_extra, codes_in, asked, data, ghost, columns, conn, chosen, drag, stress,
    velocity,
    base, codes, csem, everything, moments, results, sums_of, near_force, first_force, last_force, back, table, shares, bsend, brecv, ssend, srecv,
):
    me = lax.axis_index("cell")
    cut = lax.axis_index("cuts")
    rho = lax.rem(cut - lax.rem(me, cuts) + cuts, cuts)
    slot = lax.div(me, cuts)
    load_codes = pltpu.make_async_copy(codes_in, codes, csem)
    load_codes.start()
    back[slot] = jnp.zeros(back.shape[1:], F32)
    greet(me, cut, rho, groups, cuts)
    table[...] = jnp.zeros(table.shape, F32)
    fill_tables(data, ghost, everything, moments)
    load_codes.wait()

    def run_list(row, begin, slots, unroll):
        def step(i, carry):
            for u in range(unroll):
                at = begin + i * unroll + u
                code = codes[row, at]
                second = codes[LIST_ROWS + row, at]
                _, on_first, on_second = one_pair(code, second, everything, moments, columns)
                results[0, at] = on_first
                results[1, at] = on_second
            return carry

        lax.fori_loop(0, slots // unroll, step, 0)

    def collect(side, begin, slots):
        def row(r):
            return results[side, begin : begin + slots, r, :]

        at = slice(begin, begin + slots)
        sums_of[...] = jnp.zeros(sums_of.shape, F32)
        for c in range(3):
            sums_of[at, c * SEG : (c + 1) * SEG] = row(c) + row(3 + c) + row(6 + c)
        sums_of[at, 3 * SEG : 4 * SEG] = row(9)
        return split(sums_of[...], 3)

    def scatter(at, start, size, pieces):
        hit = iota((size, SEG), 0) + start == jnp.broadcast_to(at, (size, SEG))
        onehot = jnp.where(hit, 1.0, 0.0).astype(BF16)
        return sum(dot(onehot, piece, NN) for piece in pieces)

    def middle_of(c, start, size):
        return everything[start : start + size, c, :]

    ghosts = groups * cap
    second_at = codes_in[LIST_ROWS + FAR_ROW : LIST_ROWS + FAR_ROW + 1, :]

    def far_result(sums, out):
        for c in range(3):
            lanes = slice(c * SEG, (c + 1) * SEG)
            force = middle_of(c, blocks, ghosts) * sums[:, 3 * SEG :] - sums[:, lanes]
            for m in range(groups):
                out[m, :, lanes] = force[m * cap : (m + 1) * cap, :] + far_extra[m, :, lanes]

    def reaction_copy(source, m, other, at):
        return pltpu.make_async_remote_copy(
            src_ref=source.at[m],
            dst_ref=back.at[at],
            send_sem=bsend.at[m],
            recv_sem=brecv.at[at],
            device_id=(other, cut),
            device_id_type=MESH,
        )

    def send_first(i, m, other):
        reaction_copy(first_force, m, other, slot).start()

    def send_last(i, m, other):
        reaction_copy(last_force, m, other, slot).start()

    half = groups // 2
    run_list(FAR_ROW, 0, FIRST_SLOTS, FIRST_STEP)
    far_sums = scatter(second_at, blocks, ghosts, collect(1, 0, FIRST_SLOTS))
    far_result(far_sums, first_force)
    await_greetings(me, rho, groups, cuts)
    for_partners(me, rho, groups, cuts, send_first, 0, half)
    run_list(FAR_ROW, FIRST_SLOTS, FAR_SLOTS - FIRST_SLOTS, LAST_STEP)
    late = collect(1, FIRST_SLOTS, FAR_SLOTS - FIRST_SLOTS)
    far_result(far_sums + scatter(second_at, blocks, ghosts, late), last_force)
    for_partners(me, rho, groups, cuts, send_last, half, groups)
    first_at = codes_in[FAR_ROW : FAR_ROW + 1, :] & 31
    near_sums = scatter(first_at, 0, blocks, collect(0, 0, FAR_SLOTS))
    run_list(NEAR_ROW, 0, NEAR_SLOTS, NEAR_STEP)
    first_at = codes_in[NEAR_ROW : NEAR_ROW + 1, :] & 31
    near_sums = near_sums + scatter(first_at, 0, blocks, collect(0, 0, NEAR_SLOTS))
    second_at = codes_in[LIST_ROWS + NEAR_ROW : LIST_ROWS + NEAR_ROW + 1, :]
    near_sums = near_sums + scatter(second_at, 0, blocks, collect(1, 0, NEAR_SLOTS))
    for c in range(3):
        lanes = slice(c * SEG, (c + 1) * SEG)
        force = middle_of(c, 0, blocks) * near_sums[:, 3 * SEG :] - near_sums[:, lanes]
        near_force[:, lanes] = force + near_extra[:, lanes]

    values = [data[:, c * SEG : (c + 1) * SEG] for c in range(COMPS)]
    for c, force in enumerate(outer_force(values, stress)):
        base[:, c * SEG : (c + 1) * SEG] = force
    hit = iota(asked.shape, 1) == asked[...]
    onehot = jnp.transpose(jnp.where(hit, 1.0, 0.0))[:blocks, :].astype(BF16)
    for_partners(me, rho, groups, cuts, lambda i, m, other: reaction_copy(last_force, m, other, m).wait_recv())
    for m in range(groups):
        table[m * 8 : m * 8 + cap, :] = back[m]
    mine = near_force[...]
    for piece in split(table[...], 3):
        mine = mine + dot(onehot, piece, NN)
    shares[cut] = mine

    def share_copy(d, at, g):
        return pltpu.make_async_remote_copy(
            src_ref=shares.at[cut, eight_rows(g)],
            dst_ref=shares.at[at, eight_rows(g)],
            send_sem=ssend.at[d - 1, g],
            recv_sem=srecv.at[at, g],
            device_id=(me, lax.rem(cut + d, cuts)),
            device_id_type=MESH,
        )

    for g in range(blocks // 8):
        for d in range(1, cuts):
            share_copy(d, cut, g).start()

    def added(g):
        for d in range(1, cuts):
            share_copy(d, lax.rem(cut - d + cuts, cuts), g).wait_recv()
        value = base[eight_rows(g), :]
        for j in range(cuts):
            value = value + shares[j, eight_rows(g), :]
        return [value[:, c * SEG : (c + 1) * SEG] for c in range(3)]

    sums = node_sums(conn, chosen, added, 3)
    slow = drag[...]
    for c in range(3):
        speed = sums[c] / slow
        for b in range(blocks):
            velocity[c : c + 1, b * SEG : (b + 1) * SEG] = speed[b : b + 1, :]
    for g in range(blocks // 8):
        for d in range(1, cuts):
            share_copy(d, cut, g).wait_send()
    for_partners(me, rho, groups, cuts, lambda i, m, other: reaction_copy(last_force, m, other, m).wait_send())


def body(cuts, node_positions, connectivity, burgers_index, applied_stress, ghost_request, pair_list):
    blocks = burgers_index.shape[0]
    owners, cap = ghost_request.shape[1:]
    groups = owners // cuts
    nodes = node_positions.shape[1]
    width = COMPS * SEG
    shape = jax.ShapeDtypeStruct
    dma = pltpu.SemaphoreType.DMA
    data, ghost, asked, codes, extra, columns, chosen, drag, conn = pl.pallas_call(
        functools.partial(exchange_kernel, cuts, groups, cap, blocks),
        name="exchange",
        out_shape=(
            shape((blocks, width), F32),
            shape((groups, cap, SENT * SEG), F32),
            shape((groups * 8, SEG), I32),
            shape((2 * LIST_ROWS, SEG), I32),
            shape((1, SEG), I32),
            shape((blocks, 6, SEG, SEG), F32),
            shape((blocks, SEG, 2 * SEG), BF16),
            shape((blocks, SEG), F32),
            shape(connectivity.shape, I32),
        ),
        in_specs=[ANY] * 5,
        out_specs=(VMEM,) * 9,
        scratch_shapes=[
            pltpu.VMEM((3, nodes), F32),
            pltpu.VMEM((1, blocks), I32),
            pltpu.VMEM((cap, owners), I32),
            pltpu.VMEM(pair_list.shape, I32),
            pltpu.VMEM((2, blocks, SEG), I32),
            pltpu.VMEM((blocks * 8, SEG), F32),
            pltpu.VMEM((blocks, SEG), F32),
            pltpu.VMEM((1, SEG), I32),
            pltpu.VMEM((owners, 1, SEG), I32),
            pltpu.VMEM((groups, 1, SEG), I32),
            pltpu.VMEM((SEG, SENT * SEG), BF16),
            pltpu.VMEM((cuts, 8, SEG), I32),
            pltpu.VMEM((groups, cap, SENT * SEG), F32),
            pltpu.VMEM((2, 8, SEG), I32),
            dma((5,)),
            dma((groups,)), dma((groups,)), dma((cuts,)), dma((cuts,)), dma((groups,)), dma((groups,)),
        ],
        compiler_params=pltpu.CompilerParams(
            collective_id=0, has_side_effects=True, vmem_limit_bytes=EXCHANGE_VMEM
        ),
    )(
        stay(node_positions),
        stay(connectivity),
        stay(burgers_index.reshape(1, blocks)),
        stay(jnp.transpose(ghost_request[0])),
        stay(pair_list),
    )
    total_blocks = blocks + groups * cap
    tables = [pltpu.VMEM((total_blocks, ROWS, SEG), F32)] * 2
    list_scratch = [pltpu.SMEM((2 * LIST_ROWS, SEG), I32), dma]
    near_extra, far_extra = pl.pallas_call(
        extra_kernel,
        name="extra",
        out_shape=(shape((blocks, 3 * SEG), F32), shape((groups, cap, 3 * SEG), F32)),
        in_specs=[VMEM, VMEM, VMEM, VMEM, VMEM],
        out_specs=(VMEM,) * 2,
        scratch_shapes=list_scratch + tables + [pltpu.VMEM((total_blocks, ROWS, SEG), F32)],
        compiler_params=pltpu.CompilerParams(vmem_limit_bytes=PAIRS_VMEM),
    )(extra, codes, data, ghost, columns)
    return pl.pallas_call(
        functools.partial(finish_kernel, cuts, groups, cap, blocks),
        name="finish",
        out_shape=shape((3, nodes), F32),
        in_specs=[VMEM] * 10 + [SMEM],
        out_specs=VMEM,
        scratch_shapes=[
            pltpu.VMEM((blocks, 3 * SEG), F32),
            *list_scratch,
            *tables,
            pltpu.VMEM((2, SEG, ROWS, SEG), F32),
            pltpu.VMEM((SEG, 4 * SEG), F32),
            pltpu.VMEM((blocks, 3 * SEG), F32),
            pltpu.VMEM((groups, cap, 3 * SEG), F32),
            pltpu.VMEM((groups, cap, 3 * SEG), F32),
            pltpu.VMEM((groups, cap, 3 * SEG), F32),
            pltpu.VMEM((groups * 8, 3 * SEG), F32),
            pltpu.VMEM((cuts, blocks, 3 * SEG), F32),
            dma((groups,)), dma((groups,)), dma((cuts, blocks // 8)), dma((cuts, blocks // 8)),
        ],
        compiler_params=pltpu.CompilerParams(
            collective_id=1, has_side_effects=True, vmem_limit_bytes=FINISH_VMEM
        ),
    )(near_extra, far_extra, codes, asked, data, ghost, columns, conn, chosen, drag, applied_stress)


def solution(mesh):
    in_specs = (
        P(None, "cell"),
        P(None, "cell"),
        P("cell"),
        P(),
        P("cell", None, None),
        P(None, ("cell", "cuts")),
    )
    return jax.shard_map(
        functools.partial(body, mesh.shape["cuts"]),
        mesh=mesh,
        in_specs=in_specs,
        out_specs=P(None, "cell"),
        check_vma=False,
    )
```

```python
import functools

import jax
import jax.numpy as jnp
from jax import lax
from jax.experimental import pallas as pl
from jax.experimental.pallas import tpu as pltpu
from jax.sharding import PartitionSpec as P

SEG = 128
COMPS = 7
SENT = 6
FIRST_ASK = 64
ROWS = 16
FIRST_SLOTS = 72
FIRST_STEP = 36
LAST_STEP = 44
NEAR_STEP = 40
FAR_SLOTS = 116
NEAR_SLOTS = 40
FAR_ROW = 8
NEAR_ROW = 9
LIST_ROWS = 16
MIB = 1024 * 1024
EXCHANGE_VMEM = 24 * MIB
PAIRS_VMEM = 24 * MIB
FINISH_VMEM = 24 * MIB
MU_FACTOR = 10.0
CORE_SQUARED = 0.25
HALF_ROOT = 0.5**0.5
MESH = pl.DeviceIdType.MESH
F32 = jnp.float32
BF16 = jnp.bfloat16
I32 = jnp.int32
VMEM = pl.BlockSpec(memory_space=pltpu.VMEM)
SMEM = pl.BlockSpec(memory_space=pltpu.SMEM)
ANY = pl.BlockSpec(memory_space=pltpu.HBM)
NN = (((1,), (0,)), ((), ()))
NT = (((1,), (1,)), ((), ()))


def stay(value):
    return pltpu.with_memory_space_constraint(value, pltpu.HBM)


def iota(shape, axis):
    return lax.broadcasted_iota(I32, shape, axis)


def dot(a, b, dims):
    return lax.dot_general(a, b, dims, preferred_element_type=F32)


def split(value, parts):
    pieces = []
    rest = value
    for part in range(parts):
        piece = rest.astype(BF16)
        pieces.append(piece)
        if part < parts - 1:
            rest = rest - piece.astype(F32)
    return pieces


def segment_values(pos, conn, burg, links):
    blocks = links.shape[1]
    for end in range(2):
        for b in range(blocks):
            links[end, b : b + 1, :] = conn[end : end + 1, b * SEG : (b + 1) * SEG]
    low = [links[end] & (SEG - 1) for end in range(2)]
    high = [links[end] >> 7 for end in range(2)]

    def step(h, carry):
        lanes = pl.ds(pl.multiple_of(h * SEG, SEG), SEG)
        out = []
        for end in range(2):
            hit = high[end] == h
            for c in range(3):
                row = jnp.broadcast_to(pos[c : c + 1, lanes], (blocks, SEG))
                got = jnp.take_along_axis(row, low[end], axis=1)
                out.append(jnp.where(hit, got, carry[end * 3 + c]))
        return tuple(out)

    zero = jnp.zeros((blocks, SEG), F32)
    ends = lax.fori_loop(0, pos.shape[1] // SEG, step, (zero,) * 6, unroll=2)
    values = [0.5 * (ends[c] + ends[3 + c]) for c in range(3)]
    values += [ends[3 + c] - ends[c] for c in range(3)]
    diagonal = iota((blocks, blocks), 0) == iota((blocks, blocks), 1)
    kinds = jnp.broadcast_to(burg[...], (blocks, blocks)).astype(F32)
    kind = jnp.sum(jnp.where(diagonal, kinds, 0.0), axis=1, keepdims=True)
    values.append(jnp.broadcast_to(kind, (blocks, SEG)))
    return values


def burgers_of(kind):
    return [HALF_ROOT * value for value in whole_burgers(kind)]


def fill_requests(req, burg, wide, rows):
    cap, owners = req.shape
    blocks = burg.shape[1]
    wide[...] = jnp.zeros(wide.shape, I32)
    wide[:, 0:blocks] = burg[...]
    message = jnp.broadcast_to(wide[...], (owners, SEG))
    lane = iota((owners, SEG), 1)
    diagonal = iota((owners, owners), 0) == iota((owners, owners), 1)
    for t in range(cap):
        row = jnp.broadcast_to(req[t : t + 1, :], (owners, owners)).astype(F32)
        column = jnp.sum(jnp.where(diagonal, row, 0.0), axis=1, keepdims=True)
        column = jnp.broadcast_to(column, (owners, SEG)).astype(I32)
        message = jnp.where(lane == FIRST_ASK + t, column, message)
    for o in range(owners):
        rows[o] = message[o : o + 1, :]


def kind_table(own, heard, said, cap):
    groups = heard.shape[0]
    lane = iota((groups, SEG), 1)
    blocks = FIRST_ASK // 2
    wanted = jnp.zeros((groups, SEG), I32)
    for t in range(cap):
        column = jnp.broadcast_to(said[:, FIRST_ASK + t : FIRST_ASK + t + 1], (groups, SEG))
        wanted = jnp.where((lane & 3) == t, column, wanted)
    found = jnp.take_along_axis(heard, jnp.maximum(wanted, 0), axis=1)
    here = (lane >= blocks) & (((lane - blocks) >> 2) == iota((groups, SEG), 0))
    ghosts = jnp.sum(jnp.where(here, found, 0).astype(F32), axis=0, keepdims=True)
    return jnp.where(iota((1, SEG), 1) < blocks, own.astype(F32), ghosts)


def whole_burgers(kind):
    odd = jnp.where((kind == 1.0) | (kind == 3.0) | (kind == 5.0), -1.0, 1.0)
    return [
        jnp.where(kind < 4.0, 1.0, 0.0),
        jnp.where(kind < 2.0, odd, jnp.where(kind < 4.0, 0.0, 1.0)),
        jnp.where(kind < 2.0, 0.0, odd),
    ]


def spread_columns(flat, columns):
    def step(block, carry):
        rows = flat[pl.ds(pl.multiple_of(block * 8, 8), 8), :]
        for c in range(6):
            columns[block, c] = jnp.transpose(jnp.broadcast_to(rows[c : c + 1, :], (SEG, SEG)))
        return carry

    lax.fori_loop(0, columns.shape[0], step, 0, unroll=8)


def node_of(conn, b, end):
    return conn[end : end + 1, pl.ds(pl.multiple_of(b * SEG, SEG), SEG)]


def eight_rows(g):
    return pl.ds(pl.multiple_of(g * 8, 8), 8)


def choose_nodes(conn, chosen):
    def choose(b, carry):
        for end in range(2):
            low = jnp.broadcast_to(node_of(conn, b, end) & (SEG - 1), (SEG, SEG))
            hit = iota((SEG, SEG), 0) == low
            chosen[b, :, end * SEG : (end + 1) * SEG] = jnp.where(hit, 1.0, 0.0).astype(BF16)
        return carry

    lax.fori_loop(0, chosen.shape[0], choose, 0, unroll=2)


def node_sums(conn, chosen, fetch, parts):
    blocks = chosen.shape[0]

    def step(g, carry):
        pieces = [piece.astype(F32) for value in fetch(g) for piece in split(value, 2)]
        for i in range(8):
            b = g * 8 + i
            left = []
            for end in range(2):
                high = jnp.broadcast_to(node_of(conn, b, end) >> 7, (blocks, SEG))
                hit = iota((blocks, SEG), 0) == high
                column = [
                    jnp.where(hit, jnp.broadcast_to(piece[i : i + 1, :], (blocks, SEG)), 0.0)
                    for piece in pieces
                ]
                left.append(jnp.concatenate(column, axis=0).astype(BF16))
            carry = carry + dot(jnp.concatenate(left, axis=1), chosen[b], NT)
        return carry

    sums = lax.fori_loop(0, blocks // 8, step, jnp.zeros((2 * parts * blocks, SEG), F32))
    rows = [sums[p * blocks : (p + 1) * blocks] for p in range(2 * parts)]
    return [rows[p] + rows[p + 1] for p in range(0, 2 * parts, 2)]


def outer_force(values, stress):
    line = values[3:6]
    burgers = burgers_of(values[6])
    sigma = [[0.5 * (stress[a, b] + stress[b, a]) for b in range(3)] for a in range(3)]
    pull = [sigma[a][0] * burgers[0] + sigma[a][1] * burgers[1] + sigma[a][2] * burgers[2] for a in range(3)]
    forces = []
    for c in range(3):
        u, v = (c + 1) % 3, (c + 2) % 3
        forces.append(pull[u] * line[v] - pull[v] * line[u])
    return forces


def partner(i, me, rho, groups, cuts):
    half = groups // 2
    hop = jnp.where(lax.rem(i, 2) == 0, half + lax.div(i, 2), half - lax.div(i + 1, 2))
    m = lax.rem(lax.div(me, cuts) + hop, groups)
    return m, m * cuts + rho


def for_partners(me, rho, groups, cuts, run, first=0, last=None):
    def step(i, carry):
        m, other = partner(i, me, rho, groups, cuts)

        @pl.when(other != me)
        def _():
            run(i, m, other)

        return carry

    lax.fori_loop(first, groups if last is None else last, step, 0)


def greet(me, cut, rho, groups, cuts):
    barrier = pltpu.get_barrier_semaphore()

    def signal(i, m, other):
        pl.semaphore_signal(barrier, inc=1, device_id=(other, cut), device_id_type=MESH)

    for_partners(me, rho, groups, cuts, signal)
    for d in range(1, cuts):
        peer = lax.rem(cut + d, cuts)
        pl.semaphore_signal(barrier, inc=1, device_id=(me, peer), device_id_type=MESH)


def await_greetings(me, rho, groups, cuts):
    own = jnp.where(rho == lax.rem(me, cuts), 1, 0)
    pl.semaphore_wait(pltpu.get_barrier_semaphore(), groups + cuts - 1 - own)


def prefix(flags):
    rows, lanes = flags.shape
    value = jnp.where(flags, 1.0, 0.0).astype(F32)
    coded = value.astype(BF16)
    upper = jnp.where(iota((lanes, lanes), 0) <= iota((lanes, lanes), 1), 1.0, 0.0).astype(BF16)
    along = dot(coded, upper, NN)
    ones = jnp.ones((lanes, lanes), BF16)
    totals = dot(coded, ones, NN)
    row = iota((rows, lanes), 0)
    offset = jnp.zeros((rows, lanes), F32)
    for r in range(rows - 1):
        offset = offset + jnp.where(row > r, jnp.broadcast_to(totals[r : r + 1, :], (rows, lanes)), 0.0)
    return (along - value + offset).astype(I32)


def count(flags):
    value = jnp.where(flags, 1.0, 0.0).astype(F32)
    return jnp.sum(jnp.sum(value, axis=1, keepdims=True), axis=0, keepdims=True).astype(I32)


def share_pairs(first, second, own_row, kinds, me, cut, cuts, cap, blocks):
    slot_of_me = me // cuts
    used = first >= 0
    ghost = second >= blocks
    slot = jnp.maximum(second - blocks, 0)
    owner = slot >> 2
    part = slot & 3
    own = ghost & (owner == me)
    far = ghost & (owner != me)
    wanted = jnp.zeros_like(second)
    for t in range(cap):
        row = jnp.broadcast_to(own_row[:, FIRST_ASK + t : FIRST_ASK + t + 1], second.shape)
        wanted = jnp.where(part == t, row, wanted)
    near_block = jnp.where(own, wanted, second)
    block = jnp.where(far, blocks + (owner >> 2) * cap + part, near_block)
    half = jnp.logical_and(jnp.logical_not(far), block == first)
    table = jnp.broadcast_to(kinds, first.shape)
    one = whole_burgers(jnp.take_along_axis(table, jnp.maximum(first, 0), axis=1))
    two = whole_burgers(jnp.take_along_axis(table, jnp.maximum(block, 0), axis=1))
    match = one[0] * two[0] + one[1] * two[1] + one[2] * two[2]
    match = jnp.where(half, 0.5 * match, match).astype(I32)
    alive = used & (match != 0)
    place = (owner + me) & 3
    mine_far = alive & far & (place == cut)
    near = alive & jnp.logical_not(far)
    part_size = (count(near) + cuts - 1) >> 2
    rank = prefix(near) - cut * part_size
    mine_near = near & (rank >= 0) & (rank < part_size)
    hop = ((owner >> 2) - slot_of_me) & 15
    distant = (hop >= 4) & (hop < 12)
    mine_first = mine_far & distant
    mine_last = mine_far & jnp.logical_not(distant)
    far_spot = jnp.where(distant, prefix(mine_first), count(mine_first) + prefix(mine_last))
    room = jnp.where(distant, FIRST_SLOTS, FAR_SLOTS)
    fits = (mine_far & (far_spot < room)) | (mine_near & (rank < NEAR_SLOTS))
    mine = mine_far | mine_near
    rest = mine & jnp.logical_not(fits)
    lanes = first.shape[1]
    spot = jnp.where(far, FAR_ROW * lanes + far_spot, NEAR_ROW * lanes + rank)
    spot = jnp.where(fits, spot, prefix(rest))
    first_code = jnp.where(mine, first + 32 * (match + 2), 0).astype(F32)
    second_code = jnp.where(mine, block, 0).astype(F32)
    rows = first.shape[0]
    codes = jnp.zeros((2 * LIST_ROWS, lanes), F32)
    for r in range(rows):
        at = spot[r : r + 1, :]
        hit = iota((LIST_ROWS, lanes), 0) == jnp.broadcast_to(at >> 7, (LIST_ROWS, lanes))
        left = jnp.concatenate(
            [
                jnp.where(hit, jnp.broadcast_to(first_code[r : r + 1, :], (LIST_ROWS, lanes)), 0.0),
                jnp.where(hit, jnp.broadcast_to(second_code[r : r + 1, :], (LIST_ROWS, lanes)), 0.0),
            ],
            axis=0,
        ).astype(BF16)
        chosen = iota((lanes, lanes), 0) == jnp.broadcast_to(at & (lanes - 1), (lanes, lanes))
        codes = codes + dot(left, jnp.where(chosen, 1.0, 0.0).astype(BF16), NT)
    return codes.astype(I32), count(rest)


def exchange_kernel(
    cuts, groups, cap, blocks,
    pos_in, conn_in, burg_in, req_in, pairs_in,
    data, ghost, asked, codes, extra, columns, chosen, drag, conn,
    pos, burg, req, pairs, links, flat, length, wide, rows, heard, table, plist, stage, ordered,
    isem, rsend, rrecv, psend, precv, bsend, brecv,
):
    me = lax.axis_index("cell")
    cut = lax.axis_index("cuts")
    rho = lax.rem(cut - lax.rem(me, cuts) + cuts, cuts)
    slot = lax.div(me, cuts)
    heard[slot] = jnp.full(heard.shape[1:], -1, I32)
    ghost[slot] = jnp.zeros(ghost.shape[1:], F32)
    greet(me, cut, rho, groups, cuts)
    inputs = [(req_in, req), (burg_in, burg), (pairs_in, pairs), (conn_in, conn), (pos_in, pos)]
    loads = [pltpu.make_async_copy(src, dst, isem.at[i]) for i, (src, dst) in enumerate(inputs)]
    for load in loads:
        load.start()
    for load in loads[:3]:
        load.wait()
    fill_requests(req, burg, wide, rows)
    plist[cut] = jnp.zeros(plist.shape[1:], I32)
    for e in range(2):
        for r in range(2):
            plist[cut, 2 * e + r : 2 * e + r + 1, :] = pairs[e : e + 1, r * SEG : (r + 1) * SEG]
    await_greetings(me, rho, groups, cuts)

    def request_copy(m, other, at):
        return pltpu.make_async_remote_copy(
            src_ref=rows.at[other],
            dst_ref=heard.at[at],
            send_sem=rsend.at[m],
            recv_sem=rrecv.at[at],
            device_id=(other, cut),
            device_id_type=MESH,
        )

    def pair_copy(d, at):
        return pltpu.make_async_remote_copy(
            src_ref=plist.at[cut],
            dst_ref=plist.at[at],
            send_sem=psend.at[d - 1],
            recv_sem=precv.at[at],
            device_id=(me, lax.rem(cut + d, cuts)),
            device_id_type=MESH,
        )

    for_partners(me, rho, groups, cuts, lambda i, m, other: request_copy(m, other, slot).start())
    for d in range(1, cuts):
        pair_copy(d, cut).start()
    for load in loads[3:]:
        load.wait()
    values = segment_values(pos, conn, burg, links)
    table[...] = jnp.zeros(table.shape, table.dtype)
    for c in range(COMPS):
        lanes = slice(c * SEG, (c + 1) * SEG)
        data[:, lanes] = values[c]
        if c == SENT:
            continue
        flat[pl.ds(c, blocks, stride=8), :] = values[c]
        for part, piece in enumerate(split(values[c], 3)):
            table[part * blocks : (part + 1) * blocks, lanes] = piece
    def block_copy(i, m, other, at):
        return pltpu.make_async_remote_copy(
            src_ref=stage.at[i],
            dst_ref=ghost.at[at],
            send_sem=bsend.at[i],
            recv_sem=brecv.at[at],
            device_id=(other, cut),
            device_id_type=MESH,
        )

    def serve(first, last):
        def arrived(i, m, other):
            request_copy(m, other, m).wait_recv()

        for_partners(me, rho, groups, cuts, arrived, first, last)
        count = last - first
        order = [partner(i, me, rho, groups, cuts)[0] for i in range(first, last)]
        asks = jnp.concatenate([heard[m] for m in order], axis=0)
        columns_of = [asks[:, FIRST_ASK + t : FIRST_ASK + t + 1] for t in range(cap)]
        wanted = jnp.concatenate([jnp.broadcast_to(column, (count, SEG)) for column in columns_of], axis=0)
        lane = iota(wanted.shape, 1)
        hit = ((lane & (blocks - 1)) == wanted) & (lane < 3 * blocks)
        onehot = jnp.where(hit, 1.0, 0.0).astype(BF16)
        for c in range(SENT):
            lanes = slice(c * SEG, (c + 1) * SEG)
            got = dot(onehot, table[:, lanes], NN)
            for t in range(cap):
                stage[first:last, t, lanes] = got[t * count : (t + 1) * count, :]
        for_partners(me, rho, groups, cuts, lambda i, m, other: block_copy(i, m, other, slot).start(), first, last)

    serve(groups // 2, groups)
    serve(0, groups // 2)
    hear = jnp.concatenate([heard[m] for m in range(groups)], axis=0)
    asked[...] = jnp.full(asked.shape, -1, I32)
    for t in range(cap):
        column = hear[:, FIRST_ASK + t : FIRST_ASK + t + 1]
        asked[pl.ds(t, groups, stride=8), :] = jnp.broadcast_to(column, (groups, SEG))

    spread_columns(flat, columns)
    for d in range(1, cuts):
        pair_copy(d, lax.rem(cut - d + cuts, cuts)).wait_recv()
    for j in range(cuts):
        ordered[0, 2 * j : 2 * j + 2, :] = plist[j, 0:2, :]
        ordered[1, 2 * j : 2 * j + 2, :] = plist[j, 2:4, :]
    said = jnp.concatenate([rows[m * cuts + rho] for m in range(groups)], axis=0)
    own_row = rows[me]
    kinds = kind_table(own_row, hear, said, cap)
    listed, total = share_pairs(ordered[0], ordered[1], own_row, kinds, me, cut, cuts, cap, blocks)
    codes[...] = listed
    extra[...] = jnp.broadcast_to(total, extra.shape)
    choose_nodes(conn, chosen)
    line = [data[:, c * SEG : (c + 1) * SEG] for c in range(3, 6)]
    length[...] = jnp.sqrt(line[0] * line[0] + line[1] * line[1] + line[2] * line[2] + CORE_SQUARED)
    drag[...] = node_sums(conn, chosen, lambda g: [length[eight_rows(g), :]], 1)[0]
    for_partners(me, rho, groups, cuts, lambda i, m, other: block_copy(i, m, other, m).wait_recv())
    for_partners(me, rho, groups, cuts, lambda i, m, other: block_copy(i, m, other, m).wait_send())
    for_partners(me, rho, groups, cuts, lambda i, m, other: request_copy(m, other, m).wait_send())
    for d in range(1, cuts):
        pair_copy(d, cut).wait_send()


def fill_tables(data, ghost, everything, moments):
    blocks = data.shape[0]
    groups, cap, _ = ghost.shape

    def fill(target, row, value, start):
        target[start : start + value.shape[0], row, :] = value

    def fill_block(values, start):
        for c, value in enumerate(values):
            fill(everything, c, value, start)
        for c in range(3):
            for part, piece in enumerate(split(values[c], 3)):
                fill(moments, part * 3 + c, piece.astype(F32), start)

    moments[...] = jnp.where(iota(moments.shape, 1) == 9, 1.0, 0.0)
    fill_block([data[:, c * SEG : (c + 1) * SEG] for c in range(SENT)], 0)
    for m in range(groups):
        fill_block([ghost[m, :, c * SEG : (c + 1) * SEG] for c in range(SENT)], blocks + m * cap)


def one_pair(code, second, everything, moments, columns):
    first = code & 31
    kind = code >> 5
    factor = jnp.where(kind == 0, 0.0, (0.5 * MU_FACTOR) * (kind - 2).astype(F32))
    far = everything[second]
    middle = [far[c : c + 1] for c in range(3)]
    line = [far[3 + c : 4 + c] * factor for c in range(3)]
    high, low = [], []
    step = 32
    for start in range(0, SEG, step):
        rows = slice(start, start + step)
        r = [columns[first, c, rows, :] - middle[c] for c in range(3)]
        dist = r[0] * r[0] + CORE_SQUARED + r[1] * r[1] + r[2] * r[2]
        g = (
            columns[first, 3, rows, :] * line[0]
            + columns[first, 4, rows, :] * line[1]
            + columns[first, 5, rows, :] * line[2]
        )
        inverse = lax.rsqrt(dist)
        big, small = split(g * inverse * (inverse * inverse), 2)
        high.append(big)
        low.append(small)
    high = jnp.concatenate(high, axis=0)
    low = jnp.concatenate(low, axis=0)
    near_moments = moments[first].astype(BF16)
    far_moments = moments[second].astype(BF16)
    on_first = dot(
        jnp.concatenate([far_moments, far_moments], axis=1),
        jnp.concatenate([high, low], axis=1),
        NT,
    )
    on_second = dot(
        jnp.concatenate([near_moments, near_moments], axis=1),
        jnp.concatenate([high, low], axis=0),
        NN,
    )
    return first, on_first, on_second


def extra_kernel(extra, codes_in, data, ghost, columns, near_force, far_force, codes, sem, everything, moments, total):
    blocks = data.shape[0]
    groups, cap, _ = ghost.shape
    near_force[...] = jnp.zeros(near_force.shape, F32)
    far_force[...] = jnp.zeros(far_force.shape, F32)

    left = jnp.max(extra[...].astype(F32)).astype(I32)

    @pl.when(left > 0)
    def _():
        load = pltpu.make_async_copy(codes_in, codes, sem)
        load.start()
        total[...] = jnp.zeros(total.shape, F32)
        fill_tables(data, ghost, everything, moments)
        load.wait()

        def body(index, carry):
            code = codes[index >> 7, index & (SEG - 1)]
            second = codes[LIST_ROWS + (index >> 7), index & (SEG - 1)]
            first, on_first, on_second = one_pair(code, second, everything, moments, columns)
            total[first] = total[first] + on_first
            total[second] = total[second] + on_second
            return carry

        lax.fori_loop(0, left, body, 0)

        def take(ref, row, start, rows):
            return ref[start : start + rows, row, :]

        def force(start, rows, c):
            weight = take(total, 9, start, rows)
            others = sum(take(total, 3 * part + c, start, rows) for part in range(3))
            return take(everything, c, start, rows) * weight - others

        for c in range(3):
            lanes = slice(c * SEG, (c + 1) * SEG)
            near_force[:, lanes] = force(0, blocks, c)
            for m in range(groups):
                far_force[m, :, lanes] = force(blocks + m * cap, cap, c)


def finish_kernel(
    cuts, groups, cap, blocks,
    near_extra, far_extra, codes_in, asked, data, ghost, columns, conn, chosen, drag, stress,
    velocity,
    base, codes, csem, everything, moments, results, sums_of, near_force, first_force, last_force, back, table, shares, bsend, brecv, ssend, srecv,
):
    me = lax.axis_index("cell")
    cut = lax.axis_index("cuts")
    rho = lax.rem(cut - lax.rem(me, cuts) + cuts, cuts)
    slot = lax.div(me, cuts)
    load_codes = pltpu.make_async_copy(codes_in, codes, csem)
    load_codes.start()
    back[slot] = jnp.zeros(back.shape[1:], F32)
    greet(me, cut, rho, groups, cuts)
    table[...] = jnp.zeros(table.shape, F32)
    fill_tables(data, ghost, everything, moments)
    load_codes.wait()

    def run_list(row, begin, slots, unroll):
        def step(i, carry):
            for u in range(unroll):
                at = begin + i * unroll + u
                code = codes[row, at]
                second = codes[LIST_ROWS + row, at]
                _, on_first, on_second = one_pair(code, second, everything, moments, columns)
                results[0, at] = on_first
                results[1, at] = on_second
            return carry

        lax.fori_loop(0, slots // unroll, step, 0)

    def collect(side, begin, slots):
        def row(r):
            return results[side, begin : begin + slots, r, :]

        at = slice(begin, begin + slots)
        sums_of[...] = jnp.zeros(sums_of.shape, F32)
        for c in range(3):
            sums_of[at, c * SEG : (c + 1) * SEG] = row(c) + row(3 + c) + row(6 + c)
        sums_of[at, 3 * SEG : 4 * SEG] = row(9)
        return split(sums_of[...], 3)

    def scatter(at, start, size, pieces):
        hit = iota((size, SEG), 0) + start == jnp.broadcast_to(at, (size, SEG))
        onehot = jnp.where(hit, 1.0, 0.0).astype(BF16)
        return sum(dot(onehot, piece, NN) for piece in pieces)

    def middle_of(c, start, size):
        return everything[start : start + size, c, :]

    ghosts = groups * cap
    second_at = codes_in[LIST_ROWS + FAR_ROW : LIST_ROWS + FAR_ROW + 1, :]

    def far_result(sums, out):
        for c in range(3):
            lanes = slice(c * SEG, (c + 1) * SEG)
            force = middle_of(c, blocks, ghosts) * sums[:, 3 * SEG :] - sums[:, lanes]
            for m in range(groups):
                out[m, :, lanes] = force[m * cap : (m + 1) * cap, :] + far_extra[m, :, lanes]

    def reaction_copy(source, m, other, at):
        return pltpu.make_async_remote_copy(
            src_ref=source.at[m],
            dst_ref=back.at[at],
            send_sem=bsend.at[m],
            recv_sem=brecv.at[at],
            device_id=(other, cut),
            device_id_type=MESH,
        )

    def send_first(i, m, other):
        reaction_copy(first_force, m, other, slot).start()

    def send_last(i, m, other):
        reaction_copy(last_force, m, other, slot).start()

    half = groups // 2
    run_list(FAR_ROW, 0, FIRST_SLOTS, FIRST_STEP)
    far_sums = scatter(second_at, blocks, ghosts, collect(1, 0, FIRST_SLOTS))
    far_result(far_sums, first_force)
    await_greetings(me, rho, groups, cuts)
    for_partners(me, rho, groups, cuts, send_first, 0, half)
    run_list(FAR_ROW, FIRST_SLOTS, FAR_SLOTS - FIRST_SLOTS, LAST_STEP)
    late = collect(1, FIRST_SLOTS, FAR_SLOTS - FIRST_SLOTS)
    far_result(far_sums + scatter(second_at, blocks, ghosts, late), last_force)
    for_partners(me, rho, groups, cuts, send_last, half, groups)
    first_at = codes_in[FAR_ROW : FAR_ROW + 1, :] & 31
    near_sums = scatter(first_at, 0, blocks, collect(0, 0, FAR_SLOTS))
    run_list(NEAR_ROW, 0, NEAR_SLOTS, NEAR_STEP)
    first_at = codes_in[NEAR_ROW : NEAR_ROW + 1, :] & 31
    near_sums = near_sums + scatter(first_at, 0, blocks, collect(0, 0, NEAR_SLOTS))
    second_at = codes_in[LIST_ROWS + NEAR_ROW : LIST_ROWS + NEAR_ROW + 1, :]
    near_sums = near_sums + scatter(second_at, 0, blocks, collect(1, 0, NEAR_SLOTS))
    for c in range(3):
        lanes = slice(c * SEG, (c + 1) * SEG)
        force = middle_of(c, 0, blocks) * near_sums[:, 3 * SEG :] - near_sums[:, lanes]
        near_force[:, lanes] = force + near_extra[:, lanes]

    values = [data[:, c * SEG : (c + 1) * SEG] for c in range(COMPS)]
    for c, force in enumerate(outer_force(values, stress)):
        base[:, c * SEG : (c + 1) * SEG] = force
    hit = iota(asked.shape, 1) == asked[...]
    onehot = jnp.transpose(jnp.where(hit, 1.0, 0.0))[:blocks, :].astype(BF16)
    for_partners(me, rho, groups, cuts, lambda i, m, other: reaction_copy(last_force, m, other, m).wait_recv())
    for m in range(groups):
        table[m * 8 : m * 8 + cap, :] = back[m]
    mine = near_force[...]
    for piece in split(table[...], 3):
        mine = mine + dot(onehot, piece, NN)
    shares[cut] = mine

    def share_copy(d, at, g):
        return pltpu.make_async_remote_copy(
            src_ref=shares.at[cut, eight_rows(g)],
            dst_ref=shares.at[at, eight_rows(g)],
            send_sem=ssend.at[d - 1, g],
            recv_sem=srecv.at[at, g],
            device_id=(me, lax.rem(cut + d, cuts)),
            device_id_type=MESH,
        )

    for g in range(blocks // 8):
        for d in range(1, cuts):
            share_copy(d, cut, g).start()

    def added(g):
        for d in range(1, cuts):
            share_copy(d, lax.rem(cut - d + cuts, cuts), g).wait_recv()
        value = base[eight_rows(g), :]
        for j in range(cuts):
            value = value + shares[j, eight_rows(g), :]
        return [value[:, c * SEG : (c + 1) * SEG] for c in range(3)]

    sums = node_sums(conn, chosen, added, 3)
    slow = drag[...]
    for c in range(3):
        speed = sums[c] / slow
        for b in range(blocks):
            velocity[c : c + 1, b * SEG : (b + 1) * SEG] = speed[b : b + 1, :]
    for g in range(blocks // 8):
        for d in range(1, cuts):
            share_copy(d, cut, g).wait_send()
    for_partners(me, rho, groups, cuts, lambda i, m, other: reaction_copy(last_force, m, other, m).wait_send())


def body(cuts, node_positions, connectivity, burgers_index, applied_stress, ghost_request, pair_list):
    blocks = burgers_index.shape[0]
    owners, cap = ghost_request.shape[1:]
    groups = owners // cuts
    nodes = node_positions.shape[1]
    width = COMPS * SEG
    shape = jax.ShapeDtypeStruct
    dma = pltpu.SemaphoreType.DMA
    data, ghost, asked, codes, extra, columns, chosen, drag, conn = pl.pallas_call(
        functools.partial(exchange_kernel, cuts, groups, cap, blocks),
        name="exchange",
        out_shape=(
            shape((blocks, width), F32),
            shape((groups, cap, SENT * SEG), F32),
            shape((groups * 8, SEG), I32),
            shape((2 * LIST_ROWS, SEG), I32),
            shape((1, SEG), I32),
            shape((blocks, 6, SEG, SEG), F32),
            shape((blocks, SEG, 2 * SEG), BF16),
            shape((blocks, SEG), F32),
            shape(connectivity.shape, I32),
        ),
        in_specs=[ANY] * 5,
        out_specs=(VMEM,) * 9,
        scratch_shapes=[
            pltpu.VMEM((3, nodes), F32),
            pltpu.VMEM((1, blocks), I32),
            pltpu.VMEM((cap, owners), I32),
            pltpu.VMEM(pair_list.shape, I32),
            pltpu.VMEM((2, blocks, SEG), I32),
            pltpu.VMEM((blocks * 8, SEG), F32),
            pltpu.VMEM((blocks, SEG), F32),
            pltpu.VMEM((1, SEG), I32),
            pltpu.VMEM((owners, 1, SEG), I32),
            pltpu.VMEM((groups, 1, SEG), I32),
            pltpu.VMEM((SEG, SENT * SEG), BF16),
            pltpu.VMEM((cuts, 8, SEG), I32),
            pltpu.VMEM((groups, cap, SENT * SEG), F32),
            pltpu.VMEM((2, 8, SEG), I32),
            dma((5,)),
            dma((groups,)), dma((groups,)), dma((cuts,)), dma((cuts,)), dma((groups,)), dma((groups,)),
        ],
        compiler_params=pltpu.CompilerParams(
            collective_id=0, has_side_effects=True, vmem_limit_bytes=EXCHANGE_VMEM
        ),
    )(
        stay(node_positions),
        stay(connectivity),
        stay(burgers_index.reshape(1, blocks)),
        stay(jnp.transpose(ghost_request[0])),
        stay(pair_list),
    )
    total_blocks = blocks + groups * cap
    tables = [pltpu.VMEM((total_blocks, ROWS, SEG), F32)] * 2
    list_scratch = [pltpu.SMEM((2 * LIST_ROWS, SEG), I32), dma]
    near_extra, far_extra = pl.pallas_call(
        extra_kernel,
        name="extra",
        out_shape=(shape((blocks, 3 * SEG), F32), shape((groups, cap, 3 * SEG), F32)),
        in_specs=[VMEM, VMEM, VMEM, VMEM, VMEM],
        out_specs=(VMEM,) * 2,
        scratch_shapes=list_scratch + tables + [pltpu.VMEM((total_blocks, ROWS, SEG), F32)],
        compiler_params=pltpu.CompilerParams(vmem_limit_bytes=PAIRS_VMEM),
    )(extra, codes, data, ghost, columns)
    return pl.pallas_call(
        functools.partial(finish_kernel, cuts, groups, cap, blocks),
        name="finish",
        out_shape=shape((3, nodes), F32),
        in_specs=[VMEM] * 10 + [SMEM],
        out_specs=VMEM,
        scratch_shapes=[
            pltpu.VMEM((blocks, 3 * SEG), F32),
            *list_scratch,
            *tables,
            pltpu.VMEM((2, SEG, ROWS, SEG), F32),
            pltpu.VMEM((SEG, 4 * SEG), F32),
            pltpu.VMEM((blocks, 3 * SEG), F32),
            pltpu.VMEM((groups, cap, 3 * SEG), F32),
            pltpu.VMEM((groups, cap, 3 * SEG), F32),
            pltpu.VMEM((groups, cap, 3 * SEG), F32),
            pltpu.VMEM((groups * 8, 3 * SEG), F32),
            pltpu.VMEM((cuts, blocks, 3 * SEG), F32),
            dma((groups,)), dma((groups,)), dma((cuts, blocks // 8)), dma((cuts, blocks // 8)),
        ],
        compiler_params=pltpu.CompilerParams(
            collective_id=1, has_side_effects=True, vmem_limit_bytes=FINISH_VMEM
        ),
    )(near_extra, far_extra, codes, asked, data, ghost, columns, conn, chosen, drag, applied_stress)


def solution(mesh):
    in_specs = (
        P(None, "cell"),
        P(None, "cell"),
        P("cell"),
        P(),
        P("cell", None, None),
        P(None, ("cell", "cuts")),
    )
    return jax.shard_map(
        functools.partial(body, mesh.shape["cuts"]),
        mesh=mesh,
        in_specs=in_specs,
        out_specs=P(None, "cell"),
        check_vma=False,
    )
```

```python
import functools

import jax
import jax.numpy as jnp
from jax import lax
from jax.experimental import pallas as pl
from jax.experimental.pallas import tpu as pltpu
from jax.sharding import PartitionSpec as P

SEG = 128
COMPS = 7
SENT = 6
FIRST_ASK = 64
ROWS = 16
FIRST_SLOTS = 72
LATER_HOPS = (8, 6, 10, 1, 15, 4, 12, 2, 14, 0)
FIRST_STEP = 36
LAST_STEP = 44
NEAR_STEP = 40
FAR_SLOTS = 116
NEAR_SLOTS = 40
FAR_ROW = 8
NEAR_ROW = 9
LIST_ROWS = 16
MIB = 1024 * 1024
EXCHANGE_VMEM = 24 * MIB
PAIRS_VMEM = 24 * MIB
FINISH_VMEM = 24 * MIB
MU_FACTOR = 10.0
CORE_SQUARED = 0.25
HALF_ROOT = 0.5**0.5
MESH = pl.DeviceIdType.MESH
F32 = jnp.float32
BF16 = jnp.bfloat16
I32 = jnp.int32
VMEM = pl.BlockSpec(memory_space=pltpu.VMEM)
SMEM = pl.BlockSpec(memory_space=pltpu.SMEM)
ANY = pl.BlockSpec(memory_space=pltpu.HBM)
NN = (((1,), (0,)), ((), ()))
NT = (((1,), (1,)), ((), ()))


def stay(value):
    return pltpu.with_memory_space_constraint(value, pltpu.HBM)


def iota(shape, axis):
    return lax.broadcasted_iota(I32, shape, axis)


def dot(a, b, dims):
    return lax.dot_general(a, b, dims, preferred_element_type=F32)


def split(value, parts):
    pieces = []
    rest = value
    for part in range(parts):
        piece = rest.astype(BF16)
        pieces.append(piece)
        if part < parts - 1:
            rest = rest - piece.astype(F32)
    return pieces


def segment_values(pos, conn, burg, links):
    blocks = links.shape[1]
    for end in range(2):
        for b in range(blocks):
            links[end, b : b + 1, :] = conn[end : end + 1, b * SEG : (b + 1) * SEG]
    low = [links[end] & (SEG - 1) for end in range(2)]
    high = [links[end] >> 7 for end in range(2)]

    def step(h, carry):
        lanes = pl.ds(pl.multiple_of(h * SEG, SEG), SEG)
        out = []
        for end in range(2):
            hit = high[end] == h
            for c in range(3):
                row = jnp.broadcast_to(pos[c : c + 1, lanes], (blocks, SEG))
                got = jnp.take_along_axis(row, low[end], axis=1)
                out.append(jnp.where(hit, got, carry[end * 3 + c]))
        return tuple(out)

    zero = jnp.zeros((blocks, SEG), F32)
    ends = lax.fori_loop(0, pos.shape[1] // SEG, step, (zero,) * 6, unroll=2)
    values = [0.5 * (ends[c] + ends[3 + c]) for c in range(3)]
    values += [ends[3 + c] - ends[c] for c in range(3)]
    diagonal = iota((blocks, blocks), 0) == iota((blocks, blocks), 1)
    kinds = jnp.broadcast_to(burg[...], (blocks, blocks)).astype(F32)
    kind = jnp.sum(jnp.where(diagonal, kinds, 0.0), axis=1, keepdims=True)
    values.append(jnp.broadcast_to(kind, (blocks, SEG)))
    return values


def burgers_of(kind):
    return [HALF_ROOT * value for value in whole_burgers(kind)]


def fill_requests(req, burg, wide, rows):
    cap, owners = req.shape
    blocks = burg.shape[1]
    wide[...] = jnp.zeros(wide.shape, I32)
    wide[:, 0:blocks] = burg[...]
    message = jnp.broadcast_to(wide[...], (owners, SEG))
    lane = iota((owners, SEG), 1)
    diagonal = iota((owners, owners), 0) == iota((owners, owners), 1)
    for t in range(cap):
        row = jnp.broadcast_to(req[t : t + 1, :], (owners, owners)).astype(F32)
        column = jnp.sum(jnp.where(diagonal, row, 0.0), axis=1, keepdims=True)
        column = jnp.broadcast_to(column, (owners, SEG)).astype(I32)
        message = jnp.where(lane == FIRST_ASK + t, column, message)
    for o in range(owners):
        rows[o] = message[o : o + 1, :]


def kind_table(own, heard, said, cap):
    groups = heard.shape[0]
    lane = iota((groups, SEG), 1)
    blocks = FIRST_ASK // 2
    wanted = jnp.zeros((groups, SEG), I32)
    for t in range(cap):
        column = jnp.broadcast_to(said[:, FIRST_ASK + t : FIRST_ASK + t + 1], (groups, SEG))
        wanted = jnp.where((lane & 3) == t, column, wanted)
    found = jnp.take_along_axis(heard, jnp.maximum(wanted, 0), axis=1)
    here = (lane >= blocks) & (((lane - blocks) >> 2) == iota((groups, SEG), 0))
    ghosts = jnp.sum(jnp.where(here, found, 0).astype(F32), axis=0, keepdims=True)
    return jnp.where(iota((1, SEG), 1) < blocks, own.astype(F32), ghosts)


def whole_burgers(kind):
    odd = jnp.where((kind == 1.0) | (kind == 3.0) | (kind == 5.0), -1.0, 1.0)
    return [
        jnp.where(kind < 4.0, 1.0, 0.0),
        jnp.where(kind < 2.0, odd, jnp.where(kind < 4.0, 0.0, 1.0)),
        jnp.where(kind < 2.0, 0.0, odd),
    ]


def spread_columns(flat, columns):
    def step(block, carry):
        rows = flat[pl.ds(pl.multiple_of(block * 8, 8), 8), :]
        for c in range(6):
            columns[block, c] = jnp.transpose(jnp.broadcast_to(rows[c : c + 1, :], (SEG, SEG)))
        return carry

    lax.fori_loop(0, columns.shape[0], step, 0, unroll=8)


def node_of(conn, b, end):
    return conn[end : end + 1, pl.ds(pl.multiple_of(b * SEG, SEG), SEG)]


def eight_rows(g):
    return pl.ds(pl.multiple_of(g * 8, 8), 8)


def choose_nodes(conn, chosen):
    def choose(b, carry):
        for end in range(2):
            low = jnp.broadcast_to(node_of(conn, b, end) & (SEG - 1), (SEG, SEG))
            hit = iota((SEG, SEG), 0) == low
            chosen[b, :, end * SEG : (end + 1) * SEG] = jnp.where(hit, 1.0, 0.0).astype(BF16)
        return carry

    lax.fori_loop(0, chosen.shape[0], choose, 0, unroll=2)


def node_sums(conn, chosen, fetch, parts):
    blocks = chosen.shape[0]

    def step(g, carry):
        pieces = [piece.astype(F32) for value in fetch(g) for piece in split(value, 2)]
        for i in range(8):
            b = g * 8 + i
            left = []
            for end in range(2):
                high = jnp.broadcast_to(node_of(conn, b, end) >> 7, (blocks, SEG))
                hit = iota((blocks, SEG), 0) == high
                column = [
                    jnp.where(hit, jnp.broadcast_to(piece[i : i + 1, :], (blocks, SEG)), 0.0)
                    for piece in pieces
                ]
                left.append(jnp.concatenate(column, axis=0).astype(BF16))
            carry = carry + dot(jnp.concatenate(left, axis=1), chosen[b], NT)
        return carry

    sums = lax.fori_loop(0, blocks // 8, step, jnp.zeros((2 * parts * blocks, SEG), F32))
    rows = [sums[p * blocks : (p + 1) * blocks] for p in range(2 * parts)]
    return [rows[p] + rows[p + 1] for p in range(0, 2 * parts, 2)]


def outer_force(values, stress):
    line = values[3:6]
    burgers = burgers_of(values[6])
    sigma = [[0.5 * (stress[a, b] + stress[b, a]) for b in range(3)] for a in range(3)]
    pull = [sigma[a][0] * burgers[0] + sigma[a][1] * burgers[1] + sigma[a][2] * burgers[2] for a in range(3)]
    forces = []
    for c in range(3):
        u, v = (c + 1) % 3, (c + 2) % 3
        forces.append(pull[u] * line[v] - pull[v] * line[u])
    return forces


def partner(i, me, rho, groups, cuts):
    hop = jnp.where(lax.rem(i, 2) == 0, 7 - i, 8 + i)
    for at, other in enumerate(LATER_HOPS):
        hop = jnp.where(i == 6 + at, other, hop)
    m = lax.rem(lax.div(me, cuts) + hop, groups)
    return m, m * cuts + rho


def for_partners(me, rho, groups, cuts, run, first=0, last=None):
    def step(i, carry):
        m, other = partner(i, me, rho, groups, cuts)

        @pl.when(other != me)
        def _():
            run(i, m, other)

        return carry

    lax.fori_loop(first, groups if last is None else last, step, 0)


def greet(me, cut, rho, groups, cuts):
    barrier = pltpu.get_barrier_semaphore()

    def signal(i, m, other):
        pl.semaphore_signal(barrier, inc=1, device_id=(other, cut), device_id_type=MESH)

    for_partners(me, rho, groups, cuts, signal)
    for d in range(1, cuts):
        peer = lax.rem(cut + d, cuts)
        pl.semaphore_signal(barrier, inc=1, device_id=(me, peer), device_id_type=MESH)


def await_greetings(me, rho, groups, cuts):
    own = jnp.where(rho == lax.rem(me, cuts), 1, 0)
    pl.semaphore_wait(pltpu.get_barrier_semaphore(), groups + cuts - 1 - own)


def prefix(flags):
    rows, lanes = flags.shape
    value = jnp.where(flags, 1.0, 0.0).astype(F32)
    coded = value.astype(BF16)
    upper = jnp.where(iota((lanes, lanes), 0) <= iota((lanes, lanes), 1), 1.0, 0.0).astype(BF16)
    along = dot(coded, upper, NN)
    ones = jnp.ones((lanes, lanes), BF16)
    totals = dot(coded, ones, NN)
    row = iota((rows, lanes), 0)
    offset = jnp.zeros((rows, lanes), F32)
    for r in range(rows - 1):
        offset = offset + jnp.where(row > r, jnp.broadcast_to(totals[r : r + 1, :], (rows, lanes)), 0.0)
    return (along - value + offset).astype(I32)


def count(flags):
    value = jnp.where(flags, 1.0, 0.0).astype(F32)
    return jnp.sum(jnp.sum(value, axis=1, keepdims=True), axis=0, keepdims=True).astype(I32)


def share_pairs(first, second, own_row, kinds, me, cut, cuts, cap, blocks):
    slot_of_me = me // cuts
    used = first >= 0
    ghost = second >= blocks
    slot = jnp.maximum(second - blocks, 0)
    owner = slot >> 2
    part = slot & 3
    own = ghost & (owner == me)
    far = ghost & (owner != me)
    wanted = jnp.zeros_like(second)
    for t in range(cap):
        row = jnp.broadcast_to(own_row[:, FIRST_ASK + t : FIRST_ASK + t + 1], second.shape)
        wanted = jnp.where(part == t, row, wanted)
    near_block = jnp.where(own, wanted, second)
    block = jnp.where(far, blocks + (owner >> 2) * cap + part, near_block)
    half = jnp.logical_and(jnp.logical_not(far), block == first)
    table = jnp.broadcast_to(kinds, first.shape)
    one = whole_burgers(jnp.take_along_axis(table, jnp.maximum(first, 0), axis=1))
    two = whole_burgers(jnp.take_along_axis(table, jnp.maximum(block, 0), axis=1))
    match = one[0] * two[0] + one[1] * two[1] + one[2] * two[2]
    match = jnp.where(half, 0.5 * match, match).astype(I32)
    alive = used & (match != 0)
    place = (owner + me) & 3
    mine_far = alive & far & (place == cut)
    near = alive & jnp.logical_not(far)
    part_size = (count(near) + cuts - 1) >> 2
    rank = prefix(near) - cut * part_size
    mine_near = near & (rank >= 0) & (rank < part_size)
    hop = ((owner >> 2) - slot_of_me) & 15
    distant = ((hop & 1) == 1) & (hop >= 3) & (hop < 14) | (hop == 8) | (hop == 6)
    mine_first = mine_far & distant
    mine_last = mine_far & jnp.logical_not(distant)
    far_spot = jnp.where(distant, prefix(mine_first), count(mine_first) + prefix(mine_last))
    room = jnp.where(distant, FIRST_SLOTS, FAR_SLOTS)
    fits = (mine_far & (far_spot < room)) | (mine_near & (rank < NEAR_SLOTS))
    mine = mine_far | mine_near
    rest = mine & jnp.logical_not(fits)
    lanes = first.shape[1]
    spot = jnp.where(far, FAR_ROW * lanes + far_spot, NEAR_ROW * lanes + rank)
    spot = jnp.where(fits, spot, prefix(rest))
    first_code = jnp.where(mine, first + 32 * (match + 2), 0).astype(F32)
    second_code = jnp.where(mine, block, 0).astype(F32)
    rows = first.shape[0]
    codes = jnp.zeros((2 * LIST_ROWS, lanes), F32)
    for r in range(rows):
        at = spot[r : r + 1, :]
        hit = iota((LIST_ROWS, lanes), 0) == jnp.broadcast_to(at >> 7, (LIST_ROWS, lanes))
        left = jnp.concatenate(
            [
                jnp.where(hit, jnp.broadcast_to(first_code[r : r + 1, :], (LIST_ROWS, lanes)), 0.0),
                jnp.where(hit, jnp.broadcast_to(second_code[r : r + 1, :], (LIST_ROWS, lanes)), 0.0),
            ],
            axis=0,
        ).astype(BF16)
        chosen = iota((lanes, lanes), 0) == jnp.broadcast_to(at & (lanes - 1), (lanes, lanes))
        codes = codes + dot(left, jnp.where(chosen, 1.0, 0.0).astype(BF16), NT)
    return codes.astype(I32), count(rest)


def exchange_kernel(
    cuts, groups, cap, blocks,
    pos_in, conn_in, burg_in, req_in, pairs_in,
    data, ghost, asked, codes, extra, columns, chosen, drag, conn,
    pos, burg, req, pairs, links, flat, length, wide, rows, heard, table, plist, stage, ordered,
    isem, rsend, rrecv, psend, precv, bsend, brecv,
):
    me = lax.axis_index("cell")
    cut = lax.axis_index("cuts")
    rho = lax.rem(cut - lax.rem(me, cuts) + cuts, cuts)
    slot = lax.div(me, cuts)
    heard[slot] = jnp.full(heard.shape[1:], -1, I32)
    ghost[slot] = jnp.zeros(ghost.shape[1:], F32)
    greet(me, cut, rho, groups, cuts)
    inputs = [(req_in, req), (burg_in, burg), (pairs_in, pairs), (conn_in, conn), (pos_in, pos)]
    loads = [pltpu.make_async_copy(src, dst, isem.at[i]) for i, (src, dst) in enumerate(inputs)]
    for load in loads:
        load.start()
    for load in loads[:3]:
        load.wait()
    fill_requests(req, burg, wide, rows)
    plist[cut] = jnp.zeros(plist.shape[1:], I32)
    for e in range(2):
        for r in range(2):
            plist[cut, 2 * e + r : 2 * e + r + 1, :] = pairs[e : e + 1, r * SEG : (r + 1) * SEG]
    await_greetings(me, rho, groups, cuts)

    def request_copy(m, other, at):
        return pltpu.make_async_remote_copy(
            src_ref=rows.at[other],
            dst_ref=heard.at[at],
            send_sem=rsend.at[m],
            recv_sem=rrecv.at[at],
            device_id=(other, cut),
            device_id_type=MESH,
        )

    def pair_copy(d, at):
        return pltpu.make_async_remote_copy(
            src_ref=plist.at[cut],
            dst_ref=plist.at[at],
            send_sem=psend.at[d - 1],
            recv_sem=precv.at[at],
            device_id=(me, lax.rem(cut + d, cuts)),
            device_id_type=MESH,
        )

    for_partners(me, rho, groups, cuts, lambda i, m, other: request_copy(m, other, slot).start())
    for d in range(1, cuts):
        pair_copy(d, cut).start()
    for load in loads[3:]:
        load.wait()
    values = segment_values(pos, conn, burg, links)
    table[...] = jnp.zeros(table.shape, table.dtype)
    for c in range(COMPS):
        lanes = slice(c * SEG, (c + 1) * SEG)
        data[:, lanes] = values[c]
        if c == SENT:
            continue
        flat[pl.ds(c, blocks, stride=8), :] = values[c]
        for part, piece in enumerate(split(values[c], 3)):
            table[part * blocks : (part + 1) * blocks, lanes] = piece
    def block_copy(i, m, other, at):
        return pltpu.make_async_remote_copy(
            src_ref=stage.at[i],
            dst_ref=ghost.at[at],
            send_sem=bsend.at[i],
            recv_sem=brecv.at[at],
            device_id=(other, cut),
            device_id_type=MESH,
        )

    def serve(first, last):
        def arrived(i, m, other):
            request_copy(m, other, m).wait_recv()

        for_partners(me, rho, groups, cuts, arrived, first, last)
        count = last - first
        order = [partner(i, me, rho, groups, cuts)[0] for i in range(first, last)]
        asks = jnp.concatenate([heard[m] for m in order], axis=0)
        columns_of = [asks[:, FIRST_ASK + t : FIRST_ASK + t + 1] for t in range(cap)]
        wanted = jnp.concatenate([jnp.broadcast_to(column, (count, SEG)) for column in columns_of], axis=0)
        lane = iota(wanted.shape, 1)
        hit = ((lane & (blocks - 1)) == wanted) & (lane < 3 * blocks)
        onehot = jnp.where(hit, 1.0, 0.0).astype(BF16)
        for c in range(SENT):
            lanes = slice(c * SEG, (c + 1) * SEG)
            got = dot(onehot, table[:, lanes], NN)
            for t in range(cap):
                stage[first:last, t, lanes] = got[t * count : (t + 1) * count, :]
        for_partners(me, rho, groups, cuts, lambda i, m, other: block_copy(i, m, other, slot).start(), first, last)

    serve(groups // 2, groups)
    serve(0, groups // 2)
    hear = jnp.concatenate([heard[m] for m in range(groups)], axis=0)
    asked[...] = jnp.full(asked.shape, -1, I32)
    for t in range(cap):
        column = hear[:, FIRST_ASK + t : FIRST_ASK + t + 1]
        asked[pl.ds(t, groups, stride=8), :] = jnp.broadcast_to(column, (groups, SEG))

    spread_columns(flat, columns)
    for d in range(1, cuts):
        pair_copy(d, lax.rem(cut - d + cuts, cuts)).wait_recv()
    for j in range(cuts):
        ordered[0, 2 * j : 2 * j + 2, :] = plist[j, 0:2, :]
        ordered[1, 2 * j : 2 * j + 2, :] = plist[j, 2:4, :]
    said = jnp.concatenate([rows[m * cuts + rho] for m in range(groups)], axis=0)
    own_row = rows[me]
    kinds = kind_table(own_row, hear, said, cap)
    listed, total = share_pairs(ordered[0], ordered[1], own_row, kinds, me, cut, cuts, cap, blocks)
    codes[...] = listed
    extra[...] = jnp.broadcast_to(total, extra.shape)
    choose_nodes(conn, chosen)
    line = [data[:, c * SEG : (c + 1) * SEG] for c in range(3, 6)]
    length[...] = jnp.sqrt(line[0] * line[0] + line[1] * line[1] + line[2] * line[2] + CORE_SQUARED)
    drag[...] = node_sums(conn, chosen, lambda g: [length[eight_rows(g), :]], 1)[0]
    for_partners(me, rho, groups, cuts, lambda i, m, other: block_copy(i, m, other, m).wait_recv())
    for_partners(me, rho, groups, cuts, lambda i, m, other: block_copy(i, m, other, m).wait_send())
    for_partners(me, rho, groups, cuts, lambda i, m, other: request_copy(m, other, m).wait_send())
    for d in range(1, cuts):
        pair_copy(d, cut).wait_send()


def fill_tables(data, ghost, everything, moments):
    blocks = data.shape[0]
    groups, cap, _ = ghost.shape

    def fill(target, row, value, start):
        target[start : start + value.shape[0], row, :] = value

    def fill_block(values, start):
        for c, value in enumerate(values):
            fill(everything, c, value, start)
        for c in range(3):
            for part, piece in enumerate(split(values[c], 3)):
                fill(moments, part * 3 + c, piece.astype(F32), start)

    moments[...] = jnp.where(iota(moments.shape, 1) == 9, 1.0, 0.0)
    fill_block([data[:, c * SEG : (c + 1) * SEG] for c in range(SENT)], 0)
    for m in range(groups):
        fill_block([ghost[m, :, c * SEG : (c + 1) * SEG] for c in range(SENT)], blocks + m * cap)


def one_pair(code, second, everything, moments, columns):
    first = code & 31
    kind = code >> 5
    factor = jnp.where(kind == 0, 0.0, (0.5 * MU_FACTOR) * (kind - 2).astype(F32))
    far = everything[second]
    middle = [far[c : c + 1] for c in range(3)]
    line = [far[3 + c : 4 + c] * factor for c in range(3)]
    high, low = [], []
    step = 32
    for start in range(0, SEG, step):
        rows = slice(start, start + step)
        r = [columns[first, c, rows, :] - middle[c] for c in range(3)]
        dist = r[0] * r[0] + CORE_SQUARED + r[1] * r[1] + r[2] * r[2]
        g = (
            columns[first, 3, rows, :] * line[0]
            + columns[first, 4, rows, :] * line[1]
            + columns[first, 5, rows, :] * line[2]
        )
        inverse = lax.rsqrt(dist)
        big, small = split(g * inverse * (inverse * inverse), 2)
        high.append(big)
        low.append(small)
    high = jnp.concatenate(high, axis=0)
    low = jnp.concatenate(low, axis=0)
    near_moments = moments[first].astype(BF16)
    far_moments = moments[second].astype(BF16)
    on_first = dot(
        jnp.concatenate([far_moments, far_moments], axis=1),
        jnp.concatenate([high, low], axis=1),
        NT,
    )
    on_second = dot(
        jnp.concatenate([near_moments, near_moments], axis=1),
        jnp.concatenate([high, low], axis=0),
        NN,
    )
    return first, on_first, on_second


def extra_kernel(extra, codes_in, data, ghost, columns, near_force, far_force, codes, sem, everything, moments, total):
    blocks = data.shape[0]
    groups, cap, _ = ghost.shape
    near_force[...] = jnp.zeros(near_force.shape, F32)
    far_force[...] = jnp.zeros(far_force.shape, F32)

    left = jnp.max(extra[...].astype(F32)).astype(I32)

    @pl.when(left > 0)
    def _():
        load = pltpu.make_async_copy(codes_in, codes, sem)
        load.start()
        total[...] = jnp.zeros(total.shape, F32)
        fill_tables(data, ghost, everything, moments)
        load.wait()

        def body(index, carry):
            code = codes[index >> 7, index & (SEG - 1)]
            second = codes[LIST_ROWS + (index >> 7), index & (SEG - 1)]
            first, on_first, on_second = one_pair(code, second, everything, moments, columns)
            total[first] = total[first] + on_first
            total[second] = total[second] + on_second
            return carry

        lax.fori_loop(0, left, body, 0)

        def take(ref, row, start, rows):
            return ref[start : start + rows, row, :]

        def force(start, rows, c):
            weight = take(total, 9, start, rows)
            others = sum(take(total, 3 * part + c, start, rows) for part in range(3))
            return take(everything, c, start, rows) * weight - others

        for c in range(3):
            lanes = slice(c * SEG, (c + 1) * SEG)
            near_force[:, lanes] = force(0, blocks, c)
            for m in range(groups):
                far_force[m, :, lanes] = force(blocks + m * cap, cap, c)


def finish_kernel(
    cuts, groups, cap, blocks,
    near_extra, far_extra, codes_in, asked, data, ghost, columns, conn, chosen, drag, stress,
    velocity,
    base, codes, csem, everything, moments, results, sums_of, near_force, first_force, last_force, back, table, shares, bsend, brecv, ssend, srecv,
):
    me = lax.axis_index("cell")
    cut = lax.axis_index("cuts")
    rho = lax.rem(cut - lax.rem(me, cuts) + cuts, cuts)
    slot = lax.div(me, cuts)
    load_codes = pltpu.make_async_copy(codes_in, codes, csem)
    load_codes.start()
    back[slot] = jnp.zeros(back.shape[1:], F32)
    greet(me, cut, rho, groups, cuts)
    table[...] = jnp.zeros(table.shape, F32)
    fill_tables(data, ghost, everything, moments)
    load_codes.wait()

    def run_list(row, begin, slots, unroll):
        def step(i, carry):
            for u in range(unroll):
                at = begin + i * unroll + u
                code = codes[row, at]
                second = codes[LIST_ROWS + row, at]
                _, on_first, on_second = one_pair(code, second, everything, moments, columns)
                results[0, at] = on_first
                results[1, at] = on_second
            return carry

        lax.fori_loop(0, slots // unroll, step, 0)

    def collect(side, begin, slots):
        def row(r):
            return results[side, begin : begin + slots, r, :]

        at = slice(begin, begin + slots)
        sums_of[...] = jnp.zeros(sums_of.shape, F32)
        for c in range(3):
            sums_of[at, c * SEG : (c + 1) * SEG] = row(c) + row(3 + c) + row(6 + c)
        sums_of[at, 3 * SEG : 4 * SEG] = row(9)
        return split(sums_of[...], 3)

    def scatter(at, start, size, pieces):
        hit = iota((size, SEG), 0) + start == jnp.broadcast_to(at, (size, SEG))
        onehot = jnp.where(hit, 1.0, 0.0).astype(BF16)
        return sum(dot(onehot, piece, NN) for piece in pieces)

    def middle_of(c, start, size):
        return everything[start : start + size, c, :]

    ghosts = groups * cap
    second_at = codes_in[LIST_ROWS + FAR_ROW : LIST_ROWS + FAR_ROW + 1, :]

    def far_result(sums, out):
        for c in range(3):
            lanes = slice(c * SEG, (c + 1) * SEG)
            force = middle_of(c, blocks, ghosts) * sums[:, 3 * SEG :] - sums[:, lanes]
            for m in range(groups):
                out[m, :, lanes] = force[m * cap : (m + 1) * cap, :] + far_extra[m, :, lanes]

    def reaction_copy(source, m, other, at):
        return pltpu.make_async_remote_copy(
            src_ref=source.at[m],
            dst_ref=back.at[at],
            send_sem=bsend.at[m],
            recv_sem=brecv.at[at],
            device_id=(other, cut),
            device_id_type=MESH,
        )

    def send_first(i, m, other):
        reaction_copy(first_force, m, other, slot).start()

    def send_last(i, m, other):
        reaction_copy(last_force, m, other, slot).start()

    half = groups // 2
    run_list(FAR_ROW, 0, FIRST_SLOTS, FIRST_STEP)
    far_sums = scatter(second_at, blocks, ghosts, collect(1, 0, FIRST_SLOTS))
    far_result(far_sums, first_force)
    await_greetings(me, rho, groups, cuts)
    for_partners(me, rho, groups, cuts, send_first, 0, half)
    run_list(FAR_ROW, FIRST_SLOTS, FAR_SLOTS - FIRST_SLOTS, LAST_STEP)
    late = collect(1, FIRST_SLOTS, FAR_SLOTS - FIRST_SLOTS)
    far_result(far_sums + scatter(second_at, blocks, ghosts, late), last_force)
    for_partners(me, rho, groups, cuts, send_last, half, groups)
    first_at = codes_in[FAR_ROW : FAR_ROW + 1, :] & 31
    near_sums = scatter(first_at, 0, blocks, collect(0, 0, FAR_SLOTS))
    run_list(NEAR_ROW, 0, NEAR_SLOTS, NEAR_STEP)
    first_at = codes_in[NEAR_ROW : NEAR_ROW + 1, :] & 31
    near_sums = near_sums + scatter(first_at, 0, blocks, collect(0, 0, NEAR_SLOTS))
    second_at = codes_in[LIST_ROWS + NEAR_ROW : LIST_ROWS + NEAR_ROW + 1, :]
    near_sums = near_sums + scatter(second_at, 0, blocks, collect(1, 0, NEAR_SLOTS))
    for c in range(3):
        lanes = slice(c * SEG, (c + 1) * SEG)
        force = middle_of(c, 0, blocks) * near_sums[:, 3 * SEG :] - near_sums[:, lanes]
        near_force[:, lanes] = force + near_extra[:, lanes]

    values = [data[:, c * SEG : (c + 1) * SEG] for c in range(COMPS)]
    for c, force in enumerate(outer_force(values, stress)):
        base[:, c * SEG : (c + 1) * SEG] = force
    hit = iota(asked.shape, 1) == asked[...]
    onehot = jnp.transpose(jnp.where(hit, 1.0, 0.0))[:blocks, :].astype(BF16)
    for_partners(me, rho, groups, cuts, lambda i, m, other: reaction_copy(last_force, m, other, m).wait_recv())
    for m in range(groups):
        table[m * 8 : m * 8 + cap, :] = back[m]
    mine = near_force[...]
    for piece in split(table[...], 3):
        mine = mine + dot(onehot, piece, NN)
    shares[cut] = mine

    def share_copy(d, at, g):
        return pltpu.make_async_remote_copy(
            src_ref=shares.at[cut, eight_rows(g)],
            dst_ref=shares.at[at, eight_rows(g)],
            send_sem=ssend.at[d - 1, g],
            recv_sem=srecv.at[at, g],
            device_id=(me, lax.rem(cut + d, cuts)),
            device_id_type=MESH,
        )

    for g in range(blocks // 8):
        for d in range(1, cuts):
            share_copy(d, cut, g).start()

    def added(g):
        for d in range(1, cuts):
            share_copy(d, lax.rem(cut - d + cuts, cuts), g).wait_recv()
        value = base[eight_rows(g), :]
        for j in range(cuts):
            value = value + shares[j, eight_rows(g), :]
        return [value[:, c * SEG : (c + 1) * SEG] for c in range(3)]

    sums = node_sums(conn, chosen, added, 3)
    slow = drag[...]
    for c in range(3):
        speed = sums[c] / slow
        for b in range(blocks):
            velocity[c : c + 1, b * SEG : (b + 1) * SEG] = speed[b : b + 1, :]
    for g in range(blocks // 8):
        for d in range(1, cuts):
            share_copy(d, cut, g).wait_send()
    for_partners(me, rho, groups, cuts, lambda i, m, other: reaction_copy(last_force, m, other, m).wait_send())


def body(cuts, node_positions, connectivity, burgers_index, applied_stress, ghost_request, pair_list):
    blocks = burgers_index.shape[0]
    owners, cap = ghost_request.shape[1:]
    groups = owners // cuts
    nodes = node_positions.shape[1]
    width = COMPS * SEG
    shape = jax.ShapeDtypeStruct
    dma = pltpu.SemaphoreType.DMA
    data, ghost, asked, codes, extra, columns, chosen, drag, conn = pl.pallas_call(
        functools.partial(exchange_kernel, cuts, groups, cap, blocks),
        name="exchange",
        out_shape=(
            shape((blocks, width), F32),
            shape((groups, cap, SENT * SEG), F32),
            shape((groups * 8, SEG), I32),
            shape((2 * LIST_ROWS, SEG), I32),
            shape((1, SEG), I32),
            shape((blocks, 6, SEG, SEG), F32),
            shape((blocks, SEG, 2 * SEG), BF16),
            shape((blocks, SEG), F32),
            shape(connectivity.shape, I32),
        ),
        in_specs=[ANY] * 5,
        out_specs=(VMEM,) * 9,
        scratch_shapes=[
            pltpu.VMEM((3, nodes), F32),
            pltpu.VMEM((1, blocks), I32),
            pltpu.VMEM((cap, owners), I32),
            pltpu.VMEM(pair_list.shape, I32),
            pltpu.VMEM((2, blocks, SEG), I32),
            pltpu.VMEM((blocks * 8, SEG), F32),
            pltpu.VMEM((blocks, SEG), F32),
            pltpu.VMEM((1, SEG), I32),
            pltpu.VMEM((owners, 1, SEG), I32),
            pltpu.VMEM((groups, 1, SEG), I32),
            pltpu.VMEM((SEG, SENT * SEG), BF16),
            pltpu.VMEM((cuts, 8, SEG), I32),
            pltpu.VMEM((groups, cap, SENT * SEG), F32),
            pltpu.VMEM((2, 8, SEG), I32),
            dma((5,)),
            dma((groups,)), dma((groups,)), dma((cuts,)), dma((cuts,)), dma((groups,)), dma((groups,)),
        ],
        compiler_params=pltpu.CompilerParams(
            collective_id=0, has_side_effects=True, vmem_limit_bytes=EXCHANGE_VMEM
        ),
    )(
        stay(node_positions),
        stay(connectivity),
        stay(burgers_index.reshape(1, blocks)),
        stay(jnp.transpose(ghost_request[0])),
        stay(pair_list),
    )
    total_blocks = blocks + groups * cap
    tables = [pltpu.VMEM((total_blocks, ROWS, SEG), F32)] * 2
    list_scratch = [pltpu.SMEM((2 * LIST_ROWS, SEG), I32), dma]
    near_extra, far_extra = pl.pallas_call(
        extra_kernel,
        name="extra",
        out_shape=(shape((blocks, 3 * SEG), F32), shape((groups, cap, 3 * SEG), F32)),
        in_specs=[VMEM, VMEM, VMEM, VMEM, VMEM],
        out_specs=(VMEM,) * 2,
        scratch_shapes=list_scratch + tables + [pltpu.VMEM((total_blocks, ROWS, SEG), F32)],
        compiler_params=pltpu.CompilerParams(vmem_limit_bytes=PAIRS_VMEM),
    )(extra, codes, data, ghost, columns)
    return pl.pallas_call(
        functools.partial(finish_kernel, cuts, groups, cap, blocks),
        name="finish",
        out_shape=shape((3, nodes), F32),
        in_specs=[VMEM] * 10 + [SMEM],
        out_specs=VMEM,
        scratch_shapes=[
            pltpu.VMEM((blocks, 3 * SEG), F32),
            *list_scratch,
            *tables,
            pltpu.VMEM((2, SEG, ROWS, SEG), F32),
            pltpu.VMEM((SEG, 4 * SEG), F32),
            pltpu.VMEM((blocks, 3 * SEG), F32),
            pltpu.VMEM((groups, cap, 3 * SEG), F32),
            pltpu.VMEM((groups, cap, 3 * SEG), F32),
            pltpu.VMEM((groups, cap, 3 * SEG), F32),
            pltpu.VMEM((groups * 8, 3 * SEG), F32),
            pltpu.VMEM((cuts, blocks, 3 * SEG), F32),
            dma((groups,)), dma((groups,)), dma((cuts, blocks // 8)), dma((cuts, blocks // 8)),
        ],
        compiler_params=pltpu.CompilerParams(
            collective_id=1, has_side_effects=True, vmem_limit_bytes=FINISH_VMEM
        ),
    )(near_extra, far_extra, codes, asked, data, ghost, columns, conn, chosen, drag, applied_stress)


def solution(mesh):
    in_specs = (
        P(None, "cell"),
        P(None, "cell"),
        P("cell"),
        P(),
        P("cell", None, None),
        P(None, ("cell", "cuts")),
    )
    return jax.shard_map(
        functools.partial(body, mesh.shape["cuts"]),
        mesh=mesh,
        in_specs=in_specs,
        out_specs=P(None, "cell"),
        check_vma=False,
    )
```
